32 devices in a mesh: gx: 8 (over z, core), yz: 4 (over y, x).
Axes of the slice: x: 2, y: 2, z: 4, core: 2. Of those that a mesh axis runs over, the one named last changes fastest.
Arguments:
- gauge_links: float32 [16, 2, 3, 3, 512], P('gx', None, None, None, 'yz'), may hold values from -1 to 1, as said below
- in_field: float32 [8, 16, 2, 3, 3, 512], P(None, 'gx', None, None, None, 'yz'), may hold values from -6 to 6
- cotangent: float32 [8, 16, 2, 3, 3, 512], P(None, 'gx', None, None, None, 'yz'), may hold values from -6 to 6
- bilinear_weights: float32 [8, 8, 8, 8], replicated, may hold values from -0.25 to 0.25
Outputs:
- grad_field: float32 [8, 16, 2, 3, 3, 512], P(None, 'gx', None, None, None, 'yz')
- grad_weights: float32 [8, 8, 8, 8], replicated
The draws below stay inside these ranges and needn't reach their ends.
Inputs may be any that keep to these rules, and one draw needn't show every extreme that they name: `gauge_links`: every site's link is a special unitary 3 x 3 matrix (unitary with determinant 1), stored as real and imaginary parts.
All inputs are finite; a program needn't handle non-finite values.
Results may differ from the reference program's by a relative error of at most 0.0003.
Values sent between devices are 32-bit elements; how exact they have to be, the bound alone decides.
A program may use at most 64 MiB of HBM per device.

```python
import jax
import jax.numpy as jnp
from jax import lax

C = 8
SDEV = 128
X = 16
S = 512
LMAX = 8
N_YZ = 4


def rotation_pair(alpha, beta, gamma, first, second):
    zeros = jnp.zeros(alpha.shape, jnp.float32)
    ones = jnp.ones(alpha.shape, jnp.float32)
    cos_a = jnp.cos(alpha)
    sin_a = jnp.sin(alpha)
    real_rows = [[ones, zeros, zeros], [zeros, ones, zeros], [zeros, zeros, ones]]
    imag_rows = [[zeros, zeros, zeros], [zeros, zeros, zeros], [zeros, zeros, zeros]]
    real_rows[first][first] = cos_a * jnp.cos(beta)
    imag_rows[first][first] = cos_a * jnp.sin(beta)
    real_rows[first][second] = sin_a * jnp.cos(gamma)
    imag_rows[first][second] = sin_a * jnp.sin(gamma)
    real_rows[second][first] = -sin_a * jnp.cos(gamma)
    imag_rows[second][first] = sin_a * jnp.sin(gamma)
    real_rows[second][second] = cos_a * jnp.cos(beta)
    imag_rows[second][second] = -cos_a * jnp.sin(beta)
    real_part = jnp.stack([jnp.stack(row, axis=0) for row in real_rows], axis=0)
    imag_part = jnp.stack([jnp.stack(row, axis=0) for row in imag_rows], axis=0)
    return (real_part, imag_part)


def small_product(left_re, left_im, right_re, right_im):
    real_part = jnp.sum(left_re[:, :, None] * right_re[None, :, :], axis=1) - jnp.sum(left_im[:, :, None] * right_im[None, :, :], axis=1)
    imag_part = jnp.sum(left_re[:, :, None] * right_im[None, :, :], axis=1) + jnp.sum(left_im[:, :, None] * right_re[None, :, :], axis=1)
    return (real_part, imag_part)


def draw_gauge_links(key, part):
    base_key = jax.random.fold_in(key, 11)
    angles = jax.random.uniform(base_key, (11, X, S), jnp.float32, -3.14159, 3.14159)
    result_re, result_im = rotation_pair(angles[0], angles[1], angles[2], 0, 1)
    for index, (first, second) in enumerate(((1, 2), (0, 1))):
        step_re, step_im = rotation_pair(angles[3 + 3 * index], angles[4 + 3 * index], angles[5 + 3 * index], first, second)
        result_re, result_im = small_product(result_re, result_im, step_re, step_im)
    phase_one = angles[9]
    phase_two = angles[10]
    phase_three = -(phase_one + phase_two)
    phase_re = jnp.stack([jnp.cos(phase_one), jnp.cos(phase_two), jnp.cos(phase_three)], axis=0)
    phase_im = jnp.stack([jnp.sin(phase_one), jnp.sin(phase_two), jnp.sin(phase_three)], axis=0)
    final_re = result_re * phase_re[None] - result_im * phase_im[None]
    final_im = result_re * phase_im[None] + result_im * phase_re[None]
    matrices = jnp.stack([final_re, final_im], axis=0)
    return jnp.moveaxis(matrices, 3, 0).astype(jnp.float32)


def shard_levels(key, dims, split, least, top_value):
    factor_of = 1.0
    for position, parts in split:
        draws = jax.random.uniform(jax.random.fold_in(jax.random.fold_in(key, 6), position), (parts,), jnp.float32, least / len(split), top_value / len(split))
        factor_of = factor_of * jnp.repeat(jnp.exp(draws), dims[position] // parts).reshape((-1,) + (1,) * (len(dims) - 1 - position))
    return factor_of


def scatter_about(rng, shape, deviation, reach, split=(), kind=jnp.bfloat16):
    drawn = deviation * jax.random.normal(rng, shape, jnp.float32)
    if split:
        drawn = drawn * shard_levels(rng, shape, split, -0.22, 0.18)
    return jnp.clip(drawn, -reach, reach).astype(kind)


def setup_inputs(seed: int = 0) -> dict:
    key_list = jax.random.split(jax.random.key(seed), 5)
    gauge_links = draw_gauge_links(jax.random.fold_in(key_list[4], 71), 0)
    in_field = scatter_about(key_list[1], (C, X, 2, 3, 3, S), 1.0, 6.0, ((1, 8), (5, 4)), jnp.float32)
    cotangent = scatter_about(key_list[2], (C, X, 2, 3, 3, S), 1.0, 6.0, ((1, 8), (5, 4)), jnp.float32)
    bilinear_weights = scatter_about(key_list[3], (C, C, LMAX, C), (LMAX * C * C) ** -0.5, 0.25, (), jnp.float32)
    return dict(gauge_links=gauge_links, in_field=in_field, cotangent=cotangent, bilinear_weights=bilinear_weights)


def matmul_three(left, right):
    return lax.optimization_barrier(jnp.sum(left[..., :, :, None, :] * right[..., None, :, :, :], axis=-3))

def complex_mul(left, right):
    left_re = left[..., 0, :, :, :]
    left_im = left[..., 1, :, :, :]
    right_re = right[..., 0, :, :, :]
    right_im = right[..., 1, :, :, :]
    real_part = matmul_three(left_re, right_re) - matmul_three(left_im, right_im)
    imag_part = matmul_three(left_re, right_im) + matmul_three(left_im, right_re)
    return jnp.stack([real_part, imag_part], axis=-4)

def dagger(matrix):
    swapped = jnp.swapaxes(matrix, -3, -2)
    return jnp.stack([swapped[..., 0, :, :, :], -swapped[..., 1, :, :, :]], axis=-4)

def reference(gauge_links, in_field, cotangent, bilinear_weights):
    weight_rows = bilinear_weights.reshape(C * C, LMAX * C)
    highest = lax.Precision.HIGHEST

    def one_block(block):
        block_links, block_field, block_cot = block
        pair_grad = complex_mul(dagger(block_field)[None], block_cot[:, None]).reshape(C * C, -1)
        line = block_links
        mixed = jnp.zeros((C * C, pair_grad.shape[1]), jnp.float32)
        transport_grad = jnp.zeros(block_field.shape, jnp.float32)
        pieces = []
        for offset in range(1, LMAX + 1):
            moved = jnp.roll(block_field, -offset, axis=1)
            transported = complex_mul(complex_mul(line[None], moved), dagger(line)[None])
            flat = transported.reshape(C, -1)
            weight_part = weight_rows[:, (offset - 1) * C:offset * C]
            mixed = mixed + jnp.dot(weight_part, flat, precision=highest)
            pieces.append(jnp.dot(pair_grad, flat.T, precision=highest))
            line_grad = jnp.dot(weight_part.T, pair_grad, precision=highest).reshape(block_field.shape)
            back_term = complex_mul(complex_mul(dagger(line)[None], line_grad), line[None])
            transport_grad = transport_grad + jnp.roll(back_term, offset, axis=1)
            line = complex_mul(line, jnp.roll(block_links, -offset, axis=0))
        mixed_matrix = mixed.reshape((C, C) + block_field.shape[1:])
        direct = lax.optimization_barrier(jnp.sum(complex_mul(block_cot[:, None], dagger(mixed_matrix)), axis=0))
        return (direct + transport_grad, jnp.concatenate(pieces, axis=1))
    links_blocks = jnp.moveaxis(gauge_links.reshape(X, 2, 3, 3, N_YZ, SDEV), 4, 0)
    field_blocks = jnp.moveaxis(in_field.reshape(C, X, 2, 3, 3, N_YZ, SDEV), 5, 0)
    cot_blocks = jnp.moveaxis(cotangent.reshape(C, X, 2, 3, 3, N_YZ, SDEV), 5, 0)
    grads, partials = lax.map(one_block, (links_blocks, field_blocks, cot_blocks))
    grad_field = jnp.moveaxis(grads, 0, 5).reshape(C, X, 2, 3, 3, S)
    grad_weights = lax.optimization_barrier(jnp.sum(partials, axis=0)).reshape(C, C, LMAX, C) / jnp.sqrt(100.0 * X * S)
    return (grad_field, grad_weights)
```

```python
import functools
import math

import jax
import jax.numpy as jnp
from jax import lax
from jax.experimental import pallas as pl
from jax.experimental.pallas import tpu as pltpu
from jax.sharding import PartitionSpec as P

MESH = pl.DeviceIdType.MESH
LANES = 128
VMEM_BYTES = 56 * 1024 * 1024


def from_behind(block, axis, distance):
    devices = range(lax.axis_size(axis))
    route = [((i - distance) % len(devices), i) for i in devices]
    return lax.ppermute(block, axis, route)


def matmul_three(left, right):
    return jnp.sum(left[..., :, :, None, :] * right[..., None, :, :, :], axis=-3)


def complex_mul(left, right):
    left_re = left[..., 0, :, :, :]
    left_im = left[..., 1, :, :, :]
    right_re = right[..., 0, :, :, :]
    right_im = right[..., 1, :, :, :]
    real_part = matmul_three(left_re, right_re) - matmul_three(left_im, right_im)
    imag_part = matmul_three(left_re, right_im) + matmul_three(left_im, right_re)
    return jnp.stack([real_part, imag_part], axis=-4)


def dagger(matrix):
    swapped = jnp.swapaxes(matrix, -3, -2)
    return jnp.stack([swapped[..., 0, :, :, :], -swapped[..., 1, :, :, :]], axis=-4)


def general(gauge_links, in_field, cotangent, bilinear_weights):
    part_x = gauge_links.shape[0]
    channels = in_field.shape[0]
    line_count = bilinear_weights.shape[2]
    site_count = gauge_links.shape[-1]
    reach_devs = (part_x - 1 + line_count) // part_x
    highest = lax.Precision.HIGHEST
    weight_rows = bilinear_weights.reshape(channels * channels, line_count * channels)

    def advance(carry, unused):
        arrived = from_behind(carry, "gx", -1)
        return (arrived, arrived)

    unused_last, stacked = lax.scan(advance, (gauge_links, in_field), None, length=reach_devs)
    window_links = jnp.concatenate(
        [gauge_links, stacked[0].reshape((-1, 2, 3, 3, site_count))], axis=0
    )
    later_field = jnp.moveaxis(stacked[1], 0, 1).reshape((channels, -1, 2, 3, 3, site_count))
    window_field = jnp.concatenate([in_field, later_field], axis=1)
    pair_grad = complex_mul(dagger(in_field)[None], cotangent[:, None]).reshape(
        channels * channels, -1
    )

    def forward_step(line, offset):
        shifted = lax.dynamic_slice_in_dim(window_field, offset, part_x, axis=1)
        transported = complex_mul(complex_mul(line[None], shifted), dagger(line)[None])
        next_links = lax.dynamic_slice_in_dim(window_links, offset, part_x, axis=0)
        return (complex_mul(line, next_links), (transported, line))

    offsets = jnp.arange(1, line_count + 1, dtype=jnp.int32)
    unused_line, (all_transported, all_lines) = lax.scan(forward_step, gauge_links, offsets)
    transported_flat = all_transported.reshape(line_count * channels, -1)
    partial_grad = lax.dot_general(
        pair_grad, transported_flat, (((1,), (1,)), ((), ())), precision=highest
    )
    mixed = jnp.dot(weight_rows, transported_flat, precision=highest)
    mixed_matrix = mixed.reshape((channels, channels) + in_field.shape[1:])
    direct = jnp.sum(complex_mul(cotangent[:, None], dagger(mixed_matrix)), axis=0)
    line_grad = jnp.dot(weight_rows.T, pair_grad, precision=highest)
    line_grad = line_grad.reshape((line_count,) + in_field.shape)
    accumulator = jnp.zeros((channels, (reach_devs + 1) * part_x, 2, 3, 3, site_count), jnp.float32)

    def backward_step(carry, inputs):
        offset, grad_piece, line = inputs
        contribution = complex_mul(complex_mul(dagger(line)[None], grad_piece), line[None])
        current = lax.dynamic_slice_in_dim(carry, offset, part_x, axis=1)
        return (
            lax.dynamic_update_slice_in_dim(carry, current + contribution, offset, axis=1),
            None,
        )

    accumulator, unused_out = lax.scan(backward_step, accumulator, (offsets, line_grad, all_lines))
    block_count = reach_devs + 1
    half_span = 1 << reach_devs.bit_length() - 1
    pending = accumulator
    while half_span >= 1:
        moving = pending[:, half_span * part_x : block_count * part_x]
        arrived = from_behind(moving, "gx", half_span)
        kept_count = block_count - half_span
        updated = pending[:, : kept_count * part_x] + arrived
        pending = jnp.concatenate(
            [updated, pending[:, kept_count * part_x : half_span * part_x]], axis=1
        )
        block_count = half_span
        half_span = half_span // 2
    grad_field = direct + pending
    total_x = part_x * lax.axis_size("gx")
    total_sites = site_count * lax.axis_size("yz")
    summed = lax.psum(partial_grad, ("gx", "yz"))
    grad_weights = summed.reshape(channels, channels, line_count, channels) / math.sqrt(
        100.0 * total_x * total_sites
    )
    return (grad_field, grad_weights)


def block_transpose(arrays):
    arrays = list(arrays)
    lane = lax.broadcasted_iota(jnp.int32, arrays[0].shape, 1)
    for bit in (1, 2, 4):
        upper = (lane & (16 * bit)) != 0
        for r in range(8):
            if r & bit:
                continue
            low, high = arrays[r], arrays[r | bit]
            arrays[r] = jnp.where(upper, pltpu.roll(high, 16 * bit, 1), low)
            arrays[r | bit] = jnp.where(upper, high, pltpu.roll(low, LANES - 16 * bit, 1))
    return arrays


def greet(axes):
    barrier = pltpu.get_barrier_semaphore()
    total = 0
    for axis, count in axes:
        me = lax.axis_index(axis)
        for k in range(1, count):
            peer = lax.rem(me + k, count)
            pl.semaphore_signal(barrier, inc=1, device_id={axis: peer}, device_id_type=MESH)
        total += count - 1
    return lambda: pl.semaphore_wait(barrier, total)


def exchange(axis, count, source, target, send_sem, recv_sem):
    me = lax.axis_index(axis)

    def copy(k):
        peer = lax.rem(me + k, count)
        return pltpu.make_async_remote_copy(
            src_ref=source.at[peer],
            dst_ref=target.at[me],
            send_sem=send_sem.at[k],
            recv_sem=recv_sem.at[k],
            device_id={axis: peer},
            device_id_type=MESH,
        )

    def arrival(k):
        origin = lax.rem(me + count - k, count)
        return pltpu.make_async_remote_copy(
            src_ref=source.at[origin],
            dst_ref=target.at[origin],
            send_sem=send_sem.at[k],
            recv_sem=recv_sem.at[k],
            device_id={axis: origin},
            device_id_type=MESH,
        )

    return [copy(k) for k in range(1, count)], [arrival(k) for k in range(1, count)]


def gather_kernel(u_ref, w_ref, g_ref, out_ref, packed, sending, landed, send_sem, recv_sem):
    me = lax.axis_index("gx")
    ready = greet((("gx", 8),))
    packed[:, 72:80, :] = jnp.zeros((8, 8, LANES), jnp.float32)
    for x in range(2):
        for part in range(2):
            for a in range(3):
                row = ((x * 2 + part) * 3 + a) * 3
                packed[:, row : row + 3, :] = w_ref[:, x, part, a, :, :]
                packed[:, 36 + row : 39 + row, :] = g_ref[:, x, part, a, :, :]
                for b in range(3):
                    r, t = divmod(row + b, 5)
                    packed[r, 72 + t : 73 + t, :] = u_ref[x, part, a, b : b + 1, :]
    for start in (0, 40):
        rows = slice(start, start + 40)
        for d, value in enumerate(block_transpose([packed[r, rows, :] for r in range(8)])):
            sending[d, rows, :] = value
    ready()
    copies, arrivals = exchange("gx", 8, sending, landed, send_sem, recv_sem)
    for copy in copies:
        copy.start()
    landed[me] = sending[me]
    for arrival in arrivals:
        arrival.wait_recv()
    for start in (0, 40):
        rows = slice(start, start + 40)
        for d, value in enumerate(block_transpose([landed[r, rows, :] for r in range(8)])):
            out_ref[d, rows, :] = value
    for copy in copies:
        copy.wait_send()


def mm(left, right, left_h=False, right_h=False):
    def pick(m, h, a, b):
        return (m[0][b][a], m[1][b][a]) if h else (m[0][a][b], m[1][a][b])

    real = [[None] * 3 for _ in range(3)]
    imag = [[None] * 3 for _ in range(3)]
    for a in range(3):
        for b in range(3):
            re = im = None
            for k in range(3):
                lr, li = pick(left, left_h, a, k)
                rr, ri = pick(right, right_h, k, b)
                rr_lr, ii = lr * rr, li * ri
                re = rr_lr if re is None else re + rr_lr
                re = re + ii if left_h != right_h else re - ii
                first, second = lr * ri, li * rr
                if right_h and left_h:
                    term = -(first + second)
                elif right_h:
                    term = second - first
                elif left_h:
                    term = first - second
                else:
                    term = first + second
                im = term if im is None else im + term
            real[a][b], imag[a][b] = re, im
    return [real, imag]


def map_matrix(f, *ms):
    return [[[f(*(m[r][a][b] for m in ms)) for b in range(3)] for a in range(3)] for r in range(2)]


def comp(r, a, b):
    return (r * 3 + a) * 3 + b


def read_matrix(f):
    return [[[f(comp(r, a, b)) for b in range(3)] for a in range(3)] for r in range(2)]


def each(m):
    for r in range(2):
        for a in range(3):
            for b in range(3):
                yield comp(r, a, b), m[r][a][b]


def conjugate_by(v, m):
    return mm(mm(v, m), v, right_h=True)


def conjugate_by_h(v, m):
    return mm(mm(v, m, left_h=True), v)


def split(value):
    high = value.astype(jnp.bfloat16)
    return high, (value - high.astype(jnp.float32)).astype(jnp.bfloat16)


def compute_kernel(
    b_ref, w3_ref, wt3_ref, back_ref, gw_ref, field, cot, wrapped, v_all, v_wrap, z, pair, mixed, line, total, final
):
    lane1 = lax.broadcasted_iota(jnp.int32, (1, LANES), 1)
    lane = lax.broadcasted_iota(jnp.int32, (8, LANES), 1)
    with jax.named_scope("frames"):
        def link(p, c):
            r, t = divmod(p * 18 + c, 5)
            return b_ref[pl.ds(r * 80 + 72 + t, 1), :]

        u0 = read_matrix(lambda c: link(0, c))
        u1 = read_matrix(lambda c: link(1, c))
        one = [[[jnp.float32(1.0 if r == 0 and a == b else 0.0) for b in range(3)] for a in range(3)] for r in range(2)]
        prefix = mm(u0, u1)
        for step in (1, 2, 4):
            before = map_matrix(
                lambda m, i: jnp.where(lane1 >= 16 * step, pltpu.roll(m, 16 * step, 1), i), prefix, one
            )
            prefix = mm(before, prefix)
        start = map_matrix(lambda m, i: jnp.where(lane1 >= 16, pltpu.roll(m, 16, 1), i), prefix, one)

        def last_group(m):
            m = jnp.where(lane1 >= 112, m, 0.0)
            for step in (1, 2, 4):
                m = m + pltpu.roll(m, 16 * step, 1)
            return m

        loop = map_matrix(last_group, prefix)
        odd = mm(start, u0)
        for p, m in enumerate((start, odd)):
            for c, value in each(m):
                v_all[c, p] = jnp.broadcast_to(value, (8, LANES))
            for c, value in each(mm(loop, m)):
                v_wrap[c, p] = jnp.broadcast_to(value, (8, LANES))

    with jax.named_scope("to_frame"):
        for p in range(2):
            v = read_matrix(lambda c: v_all[c, p])
            vw = read_matrix(lambda c: v_wrap[c, p])
            w = read_matrix(lambda c: b_ref[pl.ds(p * 18 + c, 8, stride=80), :])
            g = read_matrix(lambda c: b_ref[pl.ds(36 + p * 18 + c, 8, stride=80), :])
            for c, value in each(conjugate_by(v, w)):
                field[c, p] = value
            for c, value in each(conjugate_by(vw, w)):
                wrapped[c, p] = value
            for c, value in each(conjugate_by(v, g)):
                cot[c, p] = value

    with jax.named_scope("window"):
        for c in range(18):
            pieces = []
            for t in range(9):
                q, k = (t + 1) % 2, (t + 1) // 2
                if k == 0:
                    pieces.append(field[c, q])
                else:
                    joined = jnp.where(lane < 16 * k, wrapped[c, q], field[c, q])
                    pieces.append(pltpu.roll(joined, LANES - 16 * k, 1))
            pieces.append(jnp.zeros((8, LANES), jnp.float32))
            high, low = split(jnp.concatenate(pieces, axis=0))
            columns = slice(c * LANES, (c + 1) * LANES)
            z[0:80, columns] = high
            z[80:160, columns] = low
            z[160:240, columns] = high

    with jax.named_scope("pairs"):
        @pl.loop(0, 8)
        def _(i):
            for p in range(2):
                w = read_matrix(lambda c: field[c, p])
                g = read_matrix(lambda c: jnp.broadcast_to(cot[c, p, pl.ds(i, 1), :], (8, LANES)))
                row = pl.multiple_of(p * 64 + i * 8, 8)
                for c, value in each(mm(w, g, left_h=True)):
                    pair[pl.ds(row, 8), c * LANES : (c + 1) * LANES] = value

    with jax.named_scope("products"):
        def rows_of(ref, width, edge):
            value = ref[...]
            at = lax.broadcasted_iota(jnp.int32, value.shape, 1)
            high = value.astype(jnp.bfloat16).astype(jnp.float32)
            return jnp.where(at < edge, high, value - high).astype(jnp.bfloat16)

        w3 = rows_of(w3_ref, 240, 160)
        wt3 = rows_of(wt3_ref, 384, 256)
        weights = jnp.zeros((256, 160), jnp.float32)
        for chunk in range(9):
            columns = slice(chunk * 256, (chunk + 1) * 256)
            high, low = split(pair[:, columns])
            zc = z[:, columns]
            weights = weights + lax.dot_general(
                jnp.concatenate([high, low], axis=0),
                zc[0:160],
                (((1,), (1,)), ((), ())),
                preferred_element_type=jnp.float32,
            )
            mixed[:, columns] = jnp.dot(w3, zc, preferred_element_type=jnp.float32)
            line[:, columns] = jnp.dot(
                wt3, jnp.concatenate([high, low, high], axis=0), preferred_element_type=jnp.float32
            )
        half = weights[0:128] + weights[128:256]
        both = half[:, 0:80] + half[:, 80:160]
        gw_ref[...] = jnp.zeros((64, LANES), jnp.float32)
        gw_ref[:, 0:64] = both[0:64, 0:64] + both[64:128, 8:72]

    with jax.named_scope("direct"):
        for p in range(2):
            @pl.loop(0, 3)
            def _(a):
                sums = [[None, None] for _ in range(3)]
                for i in range(8):
                    rows = slice(p * 64 + i * 8, p * 64 + i * 8 + 8)
                    for k in range(3):
                        gr = jnp.broadcast_to(cot[a * 3 + k, p, i : i + 1, :], (8, LANES))
                        gi = jnp.broadcast_to(cot[9 + a * 3 + k, p, i : i + 1, :], (8, LANES))
                        for b in range(3):
                            at = comp(0, b, k) * LANES
                            mr = mixed[rows, at : at + LANES]
                            at = comp(1, b, k) * LANES
                            mi = mixed[rows, at : at + LANES]
                            re = gr * mr + gi * mi
                            im = gi * mr - gr * mi
                            s = sums[b]
                            sums[b] = [re, im] if s[0] is None else [s[0] + re, s[1] + im]
                for b in range(3):
                    total[a * 3 + b, p] = sums[b][0]
                    total[9 + a * 3 + b, p] = sums[b][1]

    with jax.named_scope("from_frame"):
        final[...] = jnp.zeros((320, LANES), jnp.float32)
        for q in range(2):
            near, far = {}, {}
            for c in range(18):
                inside, outside = total[c, q], None
                for t in range(9):
                    if (t + 1) % 2 != q:
                        continue
                    k = (t + 1) // 2
                    piece = line[t * 8 : t * 8 + 8, c * LANES : (c + 1) * LANES]
                    if k == 0:
                        inside = inside + piece
                        continue
                    piece = pltpu.roll(piece, 16 * k, 1)
                    inside = inside + jnp.where(lane >= 16 * k, piece, 0.0)
                    beyond = jnp.where(lane < 16 * k, piece, 0.0)
                    outside = beyond if outside is None else outside + beyond
                near[c], far[c] = inside, outside
            first = conjugate_by_h(read_matrix(lambda c: v_all[c, q]), read_matrix(lambda c: near[c]))
            second = conjugate_by_h(read_matrix(lambda c: v_wrap[c, q]), read_matrix(lambda c: far[c]))
            for c, value in each(map_matrix(lambda m, n: m + n, first, second)):
                final[pl.ds(q * 18 + c, 8, stride=40), :] = value
        for d, value in enumerate(block_transpose([final[r * 40 : r * 40 + 40, :] for r in range(8)])):
            back_ref[d] = value


def return_kernel(
    scale,
    yz_count,
    back_ref,
    gw_ref,
    out_ref,
    gw_out,
    landed,
    shares,
    across,
    mine,
    whole,
    send_sem,
    recv_sem,
    share_send,
    share_recv,
    across_send,
    across_recv,
    whole_send,
    whole_recv,
):
    me = lax.axis_index("gx")
    here = lax.axis_index("yz")
    greet((("gx", 8), ("yz", yz_count)))()
    share_copies, share_arrivals = exchange("gx", 8, gw_ref, shares, share_send, share_recv)
    copies, arrivals = exchange("gx", 8, back_ref, landed, send_sem, recv_sem)
    for copy in share_copies:
        copy.start()
    for copy in copies:
        copy.start()
    landed[me] = back_ref[me]
    shares[me] = gw_ref[me]
    for arrival in share_arrivals:
        arrival.wait_recv()
    subtotal = shares[0]
    for s in range(1, 8):
        subtotal = subtotal + shares[s]
    mine[...] = subtotal

    def spread(axis, count, source, target, send, recv):
        at = lax.axis_index(axis)
        outgoing, incoming = [], []
        for k in range(1, count):
            for found, slot, there in (
                (outgoing, at, lax.rem(at + k, count)),
                (incoming, lax.rem(at + count - k, count), lax.rem(at + count - k, count)),
            ):
                found.append(
                    pltpu.make_async_remote_copy(
                        src_ref=source,
                        dst_ref=target.at[slot],
                        send_sem=send.at[k],
                        recv_sem=recv.at[k],
                        device_id={axis: there},
                        device_id_type=MESH,
                    )
                )
        return outgoing, incoming

    across_copies, across_arrivals = spread("yz", yz_count, mine, across, across_send, across_recv)
    for copy in across_copies:
        copy.start()
    across[here] = subtotal
    for arrival in across_arrivals:
        arrival.wait_recv()
    summed = across[0]
    for s in range(1, yz_count):
        summed = summed + across[s]
    summed = summed * scale
    whole[me] = summed
    whole_copies, whole_arrivals = spread("gx", 8, whole.at[me], whole, whole_send, whole_recv)
    for copy in whole_copies:
        copy.start()
    for arrival in arrivals:
        arrival.wait_recv()
    rows = block_transpose([landed[r] for r in range(8)])
    for c in range(8):
        for x in range(2):
            for part in range(2):
                for a in range(3):
                    row = ((x * 2 + part) * 3 + a) * 3
                    out_ref[c, x, part, a, :, :] = rows[c][row : row + 3]
    for arrival in whole_arrivals:
        arrival.wait_recv()
    gw_out[...] = whole[...]
    for copy in share_copies + copies + across_copies + whole_copies:
        copy.wait_send()


def resident(scale, yz_count, gauge_links, in_field, cotangent, bilinear_weights):
    f32 = jnp.float32
    vmem = pl.BlockSpec(memory_space=pltpu.VMEM)
    dma = pltpu.SemaphoreType.DMA
    gathered = pl.pallas_call(
        gather_kernel,
        out_shape=jax.ShapeDtypeStruct((8, 80, LANES), f32),
        in_specs=[vmem] * 3,
        out_specs=vmem,
        scratch_shapes=[pltpu.VMEM((8, 80, LANES), f32)] * 3 + [dma((8,)), dma((8,))],
        compiler_params=pltpu.CompilerParams(
            collective_id=0, has_side_effects=True, vmem_limit_bytes=VMEM_BYTES
        ),
        name="gather_sites",
    )(gauge_links, in_field, cotangent)
    rows = bilinear_weights.reshape(64, 64)
    shifted = jnp.concatenate(
        [jnp.pad(rows, ((0, 0), (0, 16))), jnp.pad(rows, ((0, 0), (8, 8)))], axis=0
    )
    w3 = jnp.concatenate([shifted] * 3, axis=1)
    wt3 = jnp.concatenate([shifted.T] * 3, axis=1)
    back, partial = pl.pallas_call(
        compute_kernel,
        out_shape=(
            jax.ShapeDtypeStruct((8, 40, LANES), f32),
            jax.ShapeDtypeStruct((64, LANES), f32),
        ),
        in_specs=[vmem] * 3,
        out_specs=(vmem, vmem),
        scratch_shapes=[
            pltpu.VMEM((18, 2, 8, LANES), f32),
            pltpu.VMEM((18, 2, 8, LANES), f32),
            pltpu.VMEM((18, 2, 8, LANES), f32),
            pltpu.VMEM((18, 2, 8, LANES), f32),
            pltpu.VMEM((18, 2, 8, LANES), f32),
            pltpu.VMEM((240, 18 * LANES), jnp.bfloat16),
            pltpu.VMEM((128, 18 * LANES), f32),
            pltpu.VMEM((128, 18 * LANES), f32),
            pltpu.VMEM((80, 18 * LANES), f32),
            pltpu.VMEM((18, 2, 8, LANES), f32),
            pltpu.VMEM((320, LANES), f32),
        ],
        compiler_params=pltpu.CompilerParams(vmem_limit_bytes=VMEM_BYTES),
        name="lattice_products",
    )(gathered.reshape(640, LANES), w3, wt3)
    grad_field, grad_weights = pl.pallas_call(
        functools.partial(return_kernel, scale, yz_count),
        out_shape=(
            jax.ShapeDtypeStruct((8, 2, 2, 3, 3, LANES), f32),
            jax.ShapeDtypeStruct((8, 8, LANES), f32),
        ),
        in_specs=[vmem] * 2,
        out_specs=(vmem, vmem),
        scratch_shapes=[
            pltpu.VMEM((8, 40, LANES), f32),
            pltpu.VMEM((8, 8, LANES), f32),
            pltpu.VMEM((yz_count, 8, LANES), f32),
            pltpu.VMEM((8, LANES), f32),
            pltpu.VMEM((8, 8, LANES), f32),
        ]
        + [dma((8,)), dma((8,)), dma((8,)), dma((8,))]
        + [dma((yz_count,)), dma((yz_count,)), dma((8,)), dma((8,))],
        compiler_params=pltpu.CompilerParams(
            collective_id=1, has_side_effects=True, vmem_limit_bytes=VMEM_BYTES
        ),
        name="return_sites",
    )(back, partial.reshape(8, 8, LANES))
    return grad_field, grad_weights[:, :, 0:64].reshape(8, 8, 8, 8)


def per_device(gauge_links, in_field, cotangent, bilinear_weights):
    gx = lax.axis_size("gx")
    yz = lax.axis_size("yz")
    fits = (
        gx == 8
        and in_field.shape == (8, 2, 2, 3, 3, LANES)
        and bilinear_weights.shape == (8, 8, 8, 8)
    )
    if not fits:
        return general(gauge_links, in_field, cotangent, bilinear_weights)
    total = gauge_links.shape[0] * gx * gauge_links.shape[-1] * yz
    scale = 1.0 / math.sqrt(100.0 * total)
    return resident(scale, yz, gauge_links, in_field, cotangent, bilinear_weights)


def solution(mesh):
    placed = (
        P("gx", None, None, None, "yz"),
        P(None, "gx", None, None, None, "yz"),
        P(None, "gx", None, None, None, "yz"),
        P(),
    )
    return jax.shard_map(
        per_device,
        mesh=mesh,
        in_specs=placed,
        out_specs=(P(None, "gx", None, None, None, "yz"), P()),
        check_vma=False,
    )
```

```python
import functools
import math

import jax
import jax.numpy as jnp
from jax import lax
from jax.experimental import pallas as pl
from jax.experimental.pallas import tpu as pltpu
from jax.sharding import PartitionSpec as P

MESH = pl.DeviceIdType.MESH
LANES = 128
VMEM_BYTES = 56 * 1024 * 1024


def from_behind(block, axis, distance):
    devices = range(lax.axis_size(axis))
    route = [((i - distance) % len(devices), i) for i in devices]
    return lax.ppermute(block, axis, route)


def matmul_three(left, right):
    return jnp.sum(left[..., :, :, None, :] * right[..., None, :, :, :], axis=-3)


def complex_mul(left, right):
    left_re = left[..., 0, :, :, :]
    left_im = left[..., 1, :, :, :]
    right_re = right[..., 0, :, :, :]
    right_im = right[..., 1, :, :, :]
    real_part = matmul_three(left_re, right_re) - matmul_three(left_im, right_im)
    imag_part = matmul_three(left_re, right_im) + matmul_three(left_im, right_re)
    return jnp.stack([real_part, imag_part], axis=-4)


def dagger(matrix):
    swapped = jnp.swapaxes(matrix, -3, -2)
    return jnp.stack([swapped[..., 0, :, :, :], -swapped[..., 1, :, :, :]], axis=-4)


def general(gauge_links, in_field, cotangent, bilinear_weights):
    part_x = gauge_links.shape[0]
    channels = in_field.shape[0]
    line_count = bilinear_weights.shape[2]
    site_count = gauge_links.shape[-1]
    reach_devs = (part_x - 1 + line_count) // part_x
    highest = lax.Precision.HIGHEST
    weight_rows = bilinear_weights.reshape(channels * channels, line_count * channels)

    def advance(carry, unused):
        arrived = from_behind(carry, "gx", -1)
        return (arrived, arrived)

    unused_last, stacked = lax.scan(advance, (gauge_links, in_field), None, length=reach_devs)
    window_links = jnp.concatenate(
        [gauge_links, stacked[0].reshape((-1, 2, 3, 3, site_count))], axis=0
    )
    later_field = jnp.moveaxis(stacked[1], 0, 1).reshape((channels, -1, 2, 3, 3, site_count))
    window_field = jnp.concatenate([in_field, later_field], axis=1)
    pair_grad = complex_mul(dagger(in_field)[None], cotangent[:, None]).reshape(
        channels * channels, -1
    )

    def forward_step(line, offset):
        shifted = lax.dynamic_slice_in_dim(window_field, offset, part_x, axis=1)
        transported = complex_mul(complex_mul(line[None], shifted), dagger(line)[None])
        next_links = lax.dynamic_slice_in_dim(window_links, offset, part_x, axis=0)
        return (complex_mul(line, next_links), (transported, line))

    offsets = jnp.arange(1, line_count + 1, dtype=jnp.int32)
    unused_line, (all_transported, all_lines) = lax.scan(forward_step, gauge_links, offsets)
    transported_flat = all_transported.reshape(line_count * channels, -1)
    partial_grad = lax.dot_general(
        pair_grad, transported_flat, (((1,), (1,)), ((), ())), precision=highest
    )
    mixed = jnp.dot(weight_rows, transported_flat, precision=highest)
    mixed_matrix = mixed.reshape((channels, channels) + in_field.shape[1:])
    direct = jnp.sum(complex_mul(cotangent[:, None], dagger(mixed_matrix)), axis=0)
    line_grad = jnp.dot(weight_rows.T, pair_grad, precision=highest)
    line_grad = line_grad.reshape((line_count,) + in_field.shape)
    accumulator = jnp.zeros((channels, (reach_devs + 1) * part_x, 2, 3, 3, site_count), jnp.float32)

    def backward_step(carry, inputs):
        offset, grad_piece, line = inputs
        contribution = complex_mul(complex_mul(dagger(line)[None], grad_piece), line[None])
        current = lax.dynamic_slice_in_dim(carry, offset, part_x, axis=1)
        return (
            lax.dynamic_update_slice_in_dim(carry, current + contribution, offset, axis=1),
            None,
        )

    accumulator, unused_out = lax.scan(backward_step, accumulator, (offsets, line_grad, all_lines))
    block_count = reach_devs + 1
    half_span = 1 << reach_devs.bit_length() - 1
    pending = accumulator
    while half_span >= 1:
        moving = pending[:, half_span * part_x : block_count * part_x]
        arrived = from_behind(moving, "gx", half_span)
        kept_count = block_count - half_span
        updated = pending[:, : kept_count * part_x] + arrived
        pending = jnp.concatenate(
            [updated, pending[:, kept_count * part_x : half_span * part_x]], axis=1
        )
        block_count = half_span
        half_span = half_span // 2
    grad_field = direct + pending
    total_x = part_x * lax.axis_size("gx")
    total_sites = site_count * lax.axis_size("yz")
    summed = lax.psum(partial_grad, ("gx", "yz"))
    grad_weights = summed.reshape(channels, channels, line_count, channels) / math.sqrt(
        100.0 * total_x * total_sites
    )
    return (grad_field, grad_weights)


def block_transpose(arrays):
    arrays = list(arrays)
    lane = lax.broadcasted_iota(jnp.int32, arrays[0].shape, 1)
    for bit in (1, 2, 4):
        upper = (lane & (16 * bit)) != 0
        for r in range(8):
            if r & bit:
                continue
            low, high = arrays[r], arrays[r | bit]
            arrays[r] = jnp.where(upper, pltpu.roll(high, 16 * bit, 1), low)
            arrays[r | bit] = jnp.where(upper, high, pltpu.roll(low, LANES - 16 * bit, 1))
    return arrays


def greet(axes):
    barrier = pltpu.get_barrier_semaphore()
    total = 0
    for axis, count in axes:
        me = lax.axis_index(axis)
        for k in range(1, count):
            peer = lax.rem(me + k, count)
            pl.semaphore_signal(barrier, inc=1, device_id={axis: peer}, device_id_type=MESH)
        total += count - 1
    return lambda: pl.semaphore_wait(barrier, total)


def spread(axis, count, source, target, send, recv):
    at = lax.axis_index(axis)
    outgoing, incoming = [], []
    for k in range(1, count):
        for found, slot, there in (
            (outgoing, at, lax.rem(at + k, count)),
            (incoming, lax.rem(at + count - k, count), lax.rem(at + count - k, count)),
        ):
            found.append(
                pltpu.make_async_remote_copy(
                    src_ref=source,
                    dst_ref=target.at[slot],
                    send_sem=send.at[k],
                    recv_sem=recv.at[k],
                    device_id={axis: there},
                    device_id_type=MESH,
                )
            )
    return outgoing, incoming


def exchange(source, target, rows, send_sem, recv_sem):
    me = lax.axis_index("gx")
    outgoing, incoming = [], []
    for k in range(1, 8):
        for found, here, slot, there in (
            (outgoing, lax.rem(me + k, 8), me, lax.rem(me + k, 8)),
            (incoming, lax.rem(me + k, 8), lax.rem(me + 8 - k, 8), lax.rem(me + 8 - k, 8)),
        ):
            found.append(
                pltpu.make_async_remote_copy(
                    src_ref=source.at[here, rows, :],
                    dst_ref=target.at[slot, rows, :],
                    send_sem=send_sem.at[k],
                    recv_sem=recv_sem.at[k],
                    device_id={"gx": there},
                    device_id_type=MESH,
                )
            )
    return outgoing, incoming


def whole_kernel(
    scale,
    yz_count,
    u_ref,
    w_ref,
    g_ref,
    weight_ref,
    out_ref,
    gw_out,
    packed,
    sending,
    landed,
    sites,
    field,
    cot,
    wrapped,
    v_all,
    v_wrap,
    rows_ref,
    z,
    pair,
    mixed,
    line,
    total,
    final,
    back,
    returned,
    partial,
    shares,
    mine,
    across,
    whole,
    first_send,
    first_recv,
    second_send,
    second_recv,
    back_send,
    back_recv,
    share_send,
    share_recv,
    across_send,
    across_recv,
    whole_send,
    whole_recv,
):
    me = lax.axis_index("gx")
    here = lax.axis_index("yz")
    ready = greet((("gx", 8), ("yz", yz_count)))
    lane1 = lax.broadcasted_iota(jnp.int32, (1, LANES), 1)
    lane = lax.broadcasted_iota(jnp.int32, (8, LANES), 1)
    early, late = slice(0, 48), slice(48, 80)

    with jax.named_scope("pack"):
        packed[:, 32:48, :] = jnp.zeros((8, 16, LANES), jnp.float32)
        packed[:, 72:80, :] = jnp.zeros((8, 8, LANES), jnp.float32)
        for x in range(2):
            for ab in range(9):
                row = x * 18 + ab * 2
                packed[:, row : row + 2, :] = w_ref[:, x, ab // 3, ab % 3, :, :]
                packed[:, 41 + row : 43 + row, :] = g_ref[:, x, ab // 3, ab % 3, :, :]
                for part in range(2):
                    r, t = divmod(row + part, 5)
                    packed[r, 36 + t : 37 + t, :] = u_ref[x, ab // 3, ab % 3, part : part + 1, :]
        started = []
        arrivals = []
        for rows, send, recv in ((early, first_send, first_recv), (late, second_send, second_recv)):
            for d, value in enumerate(block_transpose([packed[r, rows, :] for r in range(8)])):
                sending[d, rows, :] = value
            if not started:
                ready()
            copies, incoming = exchange(sending, landed, rows, send, recv)
            for copy in copies:
                copy.start()
            started += copies
            arrivals.append(incoming)
        landed[me] = sending[me]

    with jax.named_scope("weights"):
        rows_ref[...] = jnp.zeros((128, 256), jnp.float32)
        for i in range(8):
            pieces = [weight_ref[pl.ds(i * 64 + l, 8, stride=8), :] for l in range(8)]
            joined = jnp.concatenate(pieces, axis=1)
            rows_ref[i * 8 : i * 8 + 8, 0:64] = joined
            rows_ref[64 + i * 8 : 72 + i * 8, 8:72] = joined
        value = rows_ref[...]
        high = value.astype(jnp.bfloat16).astype(jnp.float32)
        low = value - high
        w3 = (high + pltpu.roll(high, 80, 1) + pltpu.roll(low, 160, 1)).astype(jnp.bfloat16)
        turned = value[:, 0:LANES].T[0:80]
        high, low = split(turned)
        wt3 = jnp.concatenate([high, high, low], axis=1)

    with jax.named_scope("links_and_field"):
        for arrival in arrivals[0]:
            arrival.wait_recv()
        for c, value in enumerate(block_transpose([landed[r, early, :] for r in range(8)])):
            sites[c * 80 : c * 80 + 48, :] = value

        def link(p, c):
            r, t = divmod(p * 18 + c, 5)
            return sites[r * 80 + 36 + t : r * 80 + 37 + t, :]

        u0 = read_matrix(lambda c: link(0, c))
        u1 = read_matrix(lambda c: link(1, c))
        one = [[[jnp.float32(1.0 if r == 0 and a == b else 0.0) for b in range(3)] for a in range(3)] for r in range(2)]
        prefix = mm(u0, u1)
        for step in (1, 2, 4):
            before = map_matrix(
                lambda m, i: jnp.where(lane1 >= 16 * step, pltpu.roll(m, 16 * step, 1), i), prefix, one
            )
            prefix = mm(before, prefix)
        start = map_matrix(lambda m, i: jnp.where(lane1 >= 16, pltpu.roll(m, 16, 1), i), prefix, one)

        def last_group(m):
            m = jnp.where(lane1 >= 112, m, 0.0)
            for step in (1, 2, 4):
                m = m + pltpu.roll(m, 16 * step, 1)
            return m

        loop = map_matrix(last_group, prefix)
        odd = mm(start, u0)
        for p, m in enumerate((start, odd)):
            for c, value in each(m):
                v_all[c, p] = jnp.broadcast_to(value, (8, LANES))
            for c, value in each(mm(loop, m)):
                v_wrap[c, p] = jnp.broadcast_to(value, (8, LANES))

        def read_sites(base):
            return read_matrix(
                lambda c: jnp.stack([sites[pl.ds(base + p * 18 + c, 8, stride=80), :] for p in range(2)])
            )

        v = read_matrix(lambda c: v_all[c])
        w = read_sites(0)
        for c, value in each(conjugate_by(v, w)):
            field[c] = value
        for c, value in each(conjugate_by(read_matrix(lambda c: v_wrap[c]), w)):
            wrapped[c] = value

    with jax.named_scope("window"):
        z[240:256, :] = jnp.zeros((16, 18 * LANES), jnp.bfloat16)
        for c in range(18):
            pieces = []
            for t in range(9):
                q, k = (t + 1) % 2, (t + 1) // 2
                if k == 0:
                    pieces.append(field[c, q])
                else:
                    joined = jnp.where(lane < 16 * k, wrapped[c, q], field[c, q])
                    pieces.append(pltpu.roll(joined, LANES - 16 * k, 1))
            pieces.append(jnp.zeros((8, LANES), jnp.float32))
            high, low = split(jnp.concatenate(pieces, axis=0))
            columns = slice(c * LANES, (c + 1) * LANES)
            z[0:80, columns] = high
            z[80:160, columns] = low
            z[160:240, columns] = high

    with jax.named_scope("pairs"):
        for arrival in arrivals[1]:
            arrival.wait_recv()
        for c, value in enumerate(block_transpose([landed[r, late, :] for r in range(8)])):
            sites[c * 80 + 48 : c * 80 + 80, :] = value
        v = read_matrix(lambda c: v_all[c])
        for c, value in each(conjugate_by(v, read_sites(41))):
            cot[c] = value

        @pl.loop(0, 8)
        def _(i):
            for p in range(2):
                w = read_matrix(lambda c: field[c, p])
                g = read_matrix(lambda c: jnp.broadcast_to(cot[c, p, pl.ds(i, 1), :], (8, LANES)))
                row = pl.multiple_of(p * 64 + i * 8, 8)
                for c, value in each(mm(w, g, left_h=True)):
                    pair[pl.ds(row, 8), c * LANES : (c + 1) * LANES] = value

    with jax.named_scope("products"):
        weights = jnp.zeros((256, 160), jnp.float32)
        for chunk in range(9):
            columns = slice(chunk * 256, (chunk + 1) * 256)
            high, low = split(pair[:, columns])
            zc = z[:, columns]
            weights = weights + lax.dot_general(
                jnp.concatenate([high, low], axis=0),
                zc[0:160],
                (((1,), (1,)), ((), ())),
                preferred_element_type=jnp.float32,
            )
            mixed[:, columns] = jnp.dot(w3, zc, preferred_element_type=jnp.float32)
            line[:, columns] = jnp.dot(
                wt3, jnp.concatenate([high, low, high], axis=0), preferred_element_type=jnp.float32
            )
        half = weights[0:128] + weights[128:256]
        both = half[:, 0:80] + half[:, 80:160]
        both = both[0:64, 0:64] + both[64:128, 8:72]
        both = jnp.concatenate([both, jnp.zeros((64, 64), jnp.float32)], axis=1)
        for d in range(8):
            partial[d] = both[d * 8 : d * 8 + 8]
        share_copies, share_arrivals = exchange(partial, shares, slice(0, 8), share_send, share_recv)
        for copy in share_copies:
            copy.start()
        shares[me] = partial[me]
        started += share_copies

    with jax.named_scope("direct"):
        @pl.loop(0, 3)
        def _(a):
            for p in range(2):
                sums = [[None, None] for _ in range(3)]
                for i in range(8):
                    rows = slice(p * 64 + i * 8, p * 64 + i * 8 + 8)
                    for k in range(3):
                        at = (a * 3 + k) * 2
                        gr = jnp.broadcast_to(cot[at, p, i : i + 1, :], (8, LANES))
                        gi = jnp.broadcast_to(cot[at + 1, p, i : i + 1, :], (8, LANES))
                        for b in range(3):
                            at = comp(0, b, k) * LANES
                            mr = mixed[rows, at : at + LANES]
                            at = comp(1, b, k) * LANES
                            mi = mixed[rows, at : at + LANES]
                            re = gr * mr + gi * mi
                            im = gi * mr - gr * mi
                            s = sums[b]
                            sums[b] = [re, im] if s[0] is None else [s[0] + re, s[1] + im]
                for b in range(3):
                    total[(a * 3 + b) * 2, p] = sums[b][0]
                    total[(a * 3 + b) * 2 + 1, p] = sums[b][1]

    with jax.named_scope("share_sum"):
        for arrival in share_arrivals:
            arrival.wait_recv()
        subtotal = shares[0]
        for s in range(1, 8):
            subtotal = subtotal + shares[s]
        mine[...] = subtotal
        across_copies, across_arrivals = spread("yz", yz_count, mine, across, across_send, across_recv)
        for copy in across_copies:
            copy.start()
        across[here] = subtotal
        started += across_copies

    with jax.named_scope("from_frame"):
        near, far = {}, {}
        for c in range(18):
            insides, outsides = [], []
            for q in range(2):
                inside, outside = total[c, q], None
                for t in range(9):
                    if (t + 1) % 2 != q:
                        continue
                    k = (t + 1) // 2
                    piece = line[t * 8 : t * 8 + 8, c * LANES : (c + 1) * LANES]
                    if k == 0:
                        inside = inside + piece
                        continue
                    piece = pltpu.roll(piece, 16 * k, 1)
                    inside = inside + jnp.where(lane >= 16 * k, piece, 0.0)
                    beyond = jnp.where(lane < 16 * k, piece, 0.0)
                    outside = beyond if outside is None else outside + beyond
                insides.append(inside)
                outsides.append(outside)
            near[c], far[c] = jnp.stack(insides), jnp.stack(outsides)
        first = conjugate_by_h(read_matrix(lambda c: v_all[c]), read_matrix(lambda c: near[c]))
        second = conjugate_by_h(read_matrix(lambda c: v_wrap[c]), read_matrix(lambda c: far[c]))
        for r in range(8):
            final[r * 40 + 32 : r * 40 + 40, :] = jnp.zeros((8, LANES), jnp.float32)
        for c, value in each(map_matrix(lambda m, n: m + n, first, second)):
            for q in range(2):
                final[pl.ds(q * 18 + c, 8, stride=40), :] = value[q]
        for d, value in enumerate(block_transpose([final[r * 40 : r * 40 + 40, :] for r in range(8)])):
            back[d] = value
        copies, back_arrivals = exchange(back, returned, slice(0, 40), back_send, back_recv)
        for copy in copies:
            copy.start()
        started += copies
        returned[me] = back[me]

    with jax.named_scope("weight_sum"):
        for arrival in across_arrivals:
            arrival.wait_recv()
        summed = across[0]
        for s in range(1, yz_count):
            summed = summed + across[s]
        whole[me] = summed * scale
        whole_copies, whole_arrivals = spread("gx", 8, whole.at[me], whole, whole_send, whole_recv)
        for copy in whole_copies:
            copy.start()
        started += whole_copies

    with jax.named_scope("unpack"):
        for arrival in back_arrivals:
            arrival.wait_recv()
        rows = block_transpose([returned[r] for r in range(8)])
        for c in range(8):
            for x in range(2):
                for ab in range(9):
                    row = x * 18 + ab * 2
                    out_ref[c, x, ab // 3, ab % 3, :, :] = rows[c][row : row + 2]
        for arrival in whole_arrivals:
            arrival.wait_recv()
        for i in range(8):
            value = whole[i]
            for l in range(8):
                gw_out[pl.ds(i * 64 + l, 8, stride=8), :] = value[:, l * 8 : l * 8 + 8]
        for copy in started:
            copy.wait_send()


def resident(scale, yz_count, gauge_links, in_field, cotangent, bilinear_weights):
    f32 = jnp.float32
    vmem = pl.BlockSpec(memory_space=pltpu.VMEM)
    dma = pltpu.SemaphoreType.DMA
    grad_field, grad_weights = pl.pallas_call(
        functools.partial(whole_kernel, scale, yz_count),
        out_shape=(
            jax.ShapeDtypeStruct((8, 2, 3, 3, 2, LANES), f32),
            jax.ShapeDtypeStruct((512, 8), f32),
        ),
        in_specs=[vmem] * 4,
        out_specs=(vmem, vmem),
        scratch_shapes=[
            pltpu.VMEM((8, 80, LANES), f32),
            pltpu.VMEM((8, 80, LANES), f32),
            pltpu.VMEM((8, 80, LANES), f32),
            pltpu.VMEM((640, LANES), f32),
            pltpu.VMEM((18, 2, 8, LANES), f32),
            pltpu.VMEM((18, 2, 8, LANES), f32),
            pltpu.VMEM((18, 2, 8, LANES), f32),
            pltpu.VMEM((18, 2, 8, LANES), f32),
            pltpu.VMEM((18, 2, 8, LANES), f32),
            pltpu.VMEM((128, 256), f32),
            pltpu.VMEM((256, 18 * LANES), jnp.bfloat16),
            pltpu.VMEM((128, 18 * LANES), f32),
            pltpu.VMEM((128, 18 * LANES), f32),
            pltpu.VMEM((80, 18 * LANES), f32),
            pltpu.VMEM((18, 2, 8, LANES), f32),
            pltpu.VMEM((320, LANES), f32),
            pltpu.VMEM((8, 40, LANES), f32),
            pltpu.VMEM((8, 40, LANES), f32),
            pltpu.VMEM((8, 8, LANES), f32),
            pltpu.VMEM((8, 8, LANES), f32),
            pltpu.VMEM((8, LANES), f32),
            pltpu.VMEM((yz_count, 8, LANES), f32),
            pltpu.VMEM((8, 8, LANES), f32),
        ]
        + [dma((8,))] * 8
        + [dma((yz_count,)), dma((yz_count,)), dma((8,)), dma((8,))],
        compiler_params=pltpu.CompilerParams(
            collective_id=0, has_side_effects=True, vmem_limit_bytes=VMEM_BYTES
        ),
        name="lattice_backward",
    )(
        gauge_links.transpose(0, 2, 3, 1, 4),
        in_field.transpose(0, 1, 3, 4, 2, 5),
        cotangent.transpose(0, 1, 3, 4, 2, 5),
        bilinear_weights.reshape(512, 8),
    )
    return grad_field.transpose(0, 1, 4, 2, 3, 5), grad_weights.reshape(8, 8, 8, 8)


def mm(left, right, left_h=False, right_h=False):
    def pick(m, h, a, b):
        return (m[0][b][a], m[1][b][a]) if h else (m[0][a][b], m[1][a][b])

    real = [[None] * 3 for _ in range(3)]
    imag = [[None] * 3 for _ in range(3)]
    for a in range(3):
        for b in range(3):
            re = im = None
            for k in range(3):
                lr, li = pick(left, left_h, a, k)
                rr, ri = pick(right, right_h, k, b)
                rr_lr, ii = lr * rr, li * ri
                re = rr_lr if re is None else re + rr_lr
                re = re + ii if left_h != right_h else re - ii
                first, second = lr * ri, li * rr
                if right_h and left_h:
                    term = -(first + second)
                elif right_h:
                    term = second - first
                elif left_h:
                    term = first - second
                else:
                    term = first + second
                im = term if im is None else im + term
            real[a][b], imag[a][b] = re, im
    return [real, imag]


def map_matrix(f, *ms):
    return [[[f(*(m[r][a][b] for m in ms)) for b in range(3)] for a in range(3)] for r in range(2)]


def comp(r, a, b):
    return (a * 3 + b) * 2 + r


def read_matrix(f):
    return [[[f(comp(r, a, b)) for b in range(3)] for a in range(3)] for r in range(2)]


def each(m):
    for r in range(2):
        for a in range(3):
            for b in range(3):
                yield comp(r, a, b), m[r][a][b]


def conjugate_by(v, m):
    return mm(mm(v, m), v, right_h=True)


def conjugate_by_h(v, m):
    return mm(mm(v, m, left_h=True), v)


def split(value):
    high = value.astype(jnp.bfloat16)
    return high, (value - high.astype(jnp.float32)).astype(jnp.bfloat16)


def per_device(gauge_links, in_field, cotangent, bilinear_weights):
    gx = lax.axis_size("gx")
    yz = lax.axis_size("yz")
    fits = (
        gx == 8
        and in_field.shape == (8, 2, 2, 3, 3, LANES)
        and bilinear_weights.shape == (8, 8, 8, 8)
    )
    if not fits:
        return general(gauge_links, in_field, cotangent, bilinear_weights)
    total = gauge_links.shape[0] * gx * gauge_links.shape[-1] * yz
    scale = 1.0 / math.sqrt(100.0 * total)
    return resident(scale, yz, gauge_links, in_field, cotangent, bilinear_weights)


def solution(mesh):
    placed = (
        P("gx", None, None, None, "yz"),
        P(None, "gx", None, None, None, "yz"),
        P(None, "gx", None, None, None, "yz"),
        P(),
    )
    return jax.shard_map(
        per_device,
        mesh=mesh,
        in_specs=placed,
        out_specs=(P(None, "gx", None, None, None, "yz"), P()),
        check_vma=False,
    )
```

```python
import functools
import math

import jax
import jax.numpy as jnp
from jax import lax
from jax.experimental import pallas as pl
from jax.experimental.pallas import tpu as pltpu
from jax.sharding import PartitionSpec as P

MESH = pl.DeviceIdType.MESH
LANES = 128
VMEM_BYTES = 20 * 1024 * 1024


def from_behind(block, axis, distance):
    devices = range(lax.axis_size(axis))
    route = [((i - distance) % len(devices), i) for i in devices]
    return lax.ppermute(block, axis, route)


def matmul_three(left, right):
    return jnp.sum(left[..., :, :, None, :] * right[..., None, :, :, :], axis=-3)


def complex_mul(left, right):
    left_re = left[..., 0, :, :, :]
    left_im = left[..., 1, :, :, :]
    right_re = right[..., 0, :, :, :]
    right_im = right[..., 1, :, :, :]
    real_part = matmul_three(left_re, right_re) - matmul_three(left_im, right_im)
    imag_part = matmul_three(left_re, right_im) + matmul_three(left_im, right_re)
    return jnp.stack([real_part, imag_part], axis=-4)


def dagger(matrix):
    swapped = jnp.swapaxes(matrix, -3, -2)
    return jnp.stack([swapped[..., 0, :, :, :], -swapped[..., 1, :, :, :]], axis=-4)


def general(gauge_links, in_field, cotangent, bilinear_weights):
    part_x = gauge_links.shape[0]
    channels = in_field.shape[0]
    line_count = bilinear_weights.shape[2]
    site_count = gauge_links.shape[-1]
    reach_devs = (part_x - 1 + line_count) // part_x
    highest = lax.Precision.HIGHEST
    weight_rows = bilinear_weights.reshape(channels * channels, line_count * channels)

    def advance(carry, unused):
        arrived = from_behind(carry, "gx", -1)
        return (arrived, arrived)

    unused_last, stacked = lax.scan(advance, (gauge_links, in_field), None, length=reach_devs)
    window_links = jnp.concatenate(
        [gauge_links, stacked[0].reshape((-1, 2, 3, 3, site_count))], axis=0
    )
    later_field = jnp.moveaxis(stacked[1], 0, 1).reshape((channels, -1, 2, 3, 3, site_count))
    window_field = jnp.concatenate([in_field, later_field], axis=1)
    pair_grad = complex_mul(dagger(in_field)[None], cotangent[:, None]).reshape(
        channels * channels, -1
    )

    def forward_step(line, offset):
        shifted = lax.dynamic_slice_in_dim(window_field, offset, part_x, axis=1)
        transported = complex_mul(complex_mul(line[None], shifted), dagger(line)[None])
        next_links = lax.dynamic_slice_in_dim(window_links, offset, part_x, axis=0)
        return (complex_mul(line, next_links), (transported, line))

    offsets = jnp.arange(1, line_count + 1, dtype=jnp.int32)
    unused_line, (all_transported, all_lines) = lax.scan(forward_step, gauge_links, offsets)
    transported_flat = all_transported.reshape(line_count * channels, -1)
    partial_grad = lax.dot_general(
        pair_grad, transported_flat, (((1,), (1,)), ((), ())), precision=highest
    )
    mixed = jnp.dot(weight_rows, transported_flat, precision=highest)
    mixed_matrix = mixed.reshape((channels, channels) + in_field.shape[1:])
    direct = jnp.sum(complex_mul(cotangent[:, None], dagger(mixed_matrix)), axis=0)
    line_grad = jnp.dot(weight_rows.T, pair_grad, precision=highest)
    line_grad = line_grad.reshape((line_count,) + in_field.shape)
    accumulator = jnp.zeros((channels, (reach_devs + 1) * part_x, 2, 3, 3, site_count), jnp.float32)

    def backward_step(carry, inputs):
        offset, grad_piece, line = inputs
        contribution = complex_mul(complex_mul(dagger(line)[None], grad_piece), line[None])
        current = lax.dynamic_slice_in_dim(carry, offset, part_x, axis=1)
        return (
            lax.dynamic_update_slice_in_dim(carry, current + contribution, offset, axis=1),
            None,
        )

    accumulator, unused_out = lax.scan(backward_step, accumulator, (offsets, line_grad, all_lines))
    block_count = reach_devs + 1
    half_span = 1 << reach_devs.bit_length() - 1
    pending = accumulator
    while half_span >= 1:
        moving = pending[:, half_span * part_x : block_count * part_x]
        arrived = from_behind(moving, "gx", half_span)
        kept_count = block_count - half_span
        updated = pending[:, : kept_count * part_x] + arrived
        pending = jnp.concatenate(
            [updated, pending[:, kept_count * part_x : half_span * part_x]], axis=1
        )
        block_count = half_span
        half_span = half_span // 2
    grad_field = direct + pending
    total_x = part_x * lax.axis_size("gx")
    total_sites = site_count * lax.axis_size("yz")
    summed = lax.psum(partial_grad, ("gx", "yz"))
    grad_weights = summed.reshape(channels, channels, line_count, channels) / math.sqrt(
        100.0 * total_x * total_sites
    )
    return (grad_field, grad_weights)


def block_transpose(arrays):
    arrays = list(arrays)
    lane = lax.broadcasted_iota(jnp.int32, arrays[0].shape, 1)
    for bit in (1, 2, 4):
        upper = (lane & (16 * bit)) != 0
        for r in range(8):
            if r & bit:
                continue
            low, high = arrays[r], arrays[r | bit]
            arrays[r] = jnp.where(upper, pltpu.roll(high, 16 * bit, 1), low)
            arrays[r | bit] = jnp.where(upper, high, pltpu.roll(low, LANES - 16 * bit, 1))
    return arrays


def greet(axes):
    barrier = pltpu.get_barrier_semaphore()
    total = 0
    for axis, count in axes:
        me = lax.axis_index(axis)
        for k in range(1, count):
            peer = lax.rem(me + k, count)
            pl.semaphore_signal(barrier, inc=1, device_id={axis: peer}, device_id_type=MESH)
        total += count - 1
    return lambda: pl.semaphore_wait(barrier, total)


def spread(axis, count, source, target, send, recv):
    at = lax.axis_index(axis)
    outgoing, incoming = [], []
    for k in range(1, count):
        for found, slot, there in (
            (outgoing, at, lax.rem(at + k, count)),
            (incoming, lax.rem(at + count - k, count), lax.rem(at + count - k, count)),
        ):
            found.append(
                pltpu.make_async_remote_copy(
                    src_ref=source,
                    dst_ref=target.at[slot],
                    send_sem=send.at[k],
                    recv_sem=recv.at[k],
                    device_id={axis: there},
                    device_id_type=MESH,
                )
            )
    return outgoing, incoming


def other(me, mask):
    for bit in (1, 2, 4):
        if mask & bit:
            me = me + bit - 2 * bit * (me // bit % 2)
    return me


FAR_FIRST = (4, 5, 6, 7, 2, 3, 1)


def exchange(source, target, rows, send_sem, recv_sem):
    me = lax.axis_index("gx")
    outgoing, incoming = [], []
    for k in FAR_FIRST:
        peer = other(me, k)
        for found, slot in ((outgoing, me), (incoming, peer)):
            found.append(
                pltpu.make_async_remote_copy(
                    src_ref=source.at[peer, rows, :],
                    dst_ref=target.at[slot, rows, :],
                    send_sem=send_sem.at[k],
                    recv_sem=recv_sem.at[k],
                    device_id={"gx": peer},
                    device_id_type=MESH,
                )
            )
    return outgoing, incoming


def whole_kernel(
    scale,
    yz_count,
    u_hbm,
    w_hbm,
    g_hbm,
    weight_hbm,
    out_ref,
    gw_out,
    u_ref,
    w_ref,
    g_ref,
    weight_ref,
    packed,
    sending,
    landed,
    sites,
    field,
    cot,
    wrapped,
    v_all,
    v_wrap,
    rows_ref,
    z,
    pair,
    halves,
    mixed,
    line,
    total,
    final,
    back,
    returned,
    partial,
    shares,
    mine,
    across,
    whole,
    first_send,
    first_recv,
    second_send,
    second_recv,
    back_send,
    back_recv,
    last_send,
    last_recv,
    share_send,
    share_recv,
    across_send,
    across_recv,
    whole_send,
    whole_recv,
    load_sem,
):
    me = lax.axis_index("gx")
    here = lax.axis_index("yz")
    loads = [
        pltpu.make_async_copy(source, target, load_sem.at[k])
        for k, (source, target) in enumerate(
            ((w_hbm, w_ref), (u_hbm, u_ref), (g_hbm, g_ref), (weight_hbm, weight_ref))
        )
    ]
    for load in loads:
        load.start()
    ready = greet((("gx", 8), ("yz", yz_count)))
    lane1 = lax.broadcasted_iota(jnp.int32, (1, LANES), 1)
    lane = lax.broadcasted_iota(jnp.int32, (8, LANES), 1)
    early, late = slice(0, 48), slice(48, 80)

    with jax.named_scope("pack"):
        packed[:, 32:48, :] = jnp.zeros((8, 16, LANES), jnp.float32)
        packed[:, 72:80, :] = jnp.zeros((8, 8, LANES), jnp.float32)
        loads[0].wait()
        loads[1].wait()
        for x in range(2):
            for ab in range(9):
                row = x * 18 + ab * 2
                packed[:, row : row + 2, :] = w_ref[:, x, ab // 3, ab % 3, :, :]
                for part in range(2):
                    r, t = divmod(row + part, 5)
                    packed[r, 36 + t : 37 + t, :] = u_ref[x, ab // 3, ab % 3, part : part + 1, :]
        loads[2].wait()
        for x in range(2):
            for ab in range(9):
                row = x * 18 + ab * 2
                packed[:, 41 + row : 43 + row, :] = g_ref[:, x, ab // 3, ab % 3, :, :]
        started = []
        arrivals = []
        for rows, send, recv in ((early, first_send, first_recv), (late, second_send, second_recv)):
            for d, value in enumerate(block_transpose([packed[r, rows, :] for r in range(8)])):
                sending[d, rows, :] = value
            if not started:
                ready()
            copies, incoming = exchange(sending, landed, rows, send, recv)
            for copy in copies:
                copy.start()
            started += copies
            arrivals.append(incoming)
        landed[me] = sending[me]

    with jax.named_scope("weights"):
        loads[3].wait()
        rows_ref[...] = jnp.zeros((128, 256), jnp.float32)
        for i in range(8):
            pieces = [weight_ref[pl.ds(i * 64 + l, 8, stride=8), :] for l in range(8)]
            joined = jnp.concatenate(pieces, axis=1)
            rows_ref[i * 8 : i * 8 + 8, 0:64] = joined
            rows_ref[64 + i * 8 : 72 + i * 8, 8:72] = joined
        value = rows_ref[...]
        high = value.astype(jnp.bfloat16).astype(jnp.float32)
        low = value - high
        w3 = (high + pltpu.roll(high, 80, 1) + pltpu.roll(low, 160, 1)).astype(jnp.bfloat16)
        turned = value[:, 0:LANES].T[0:80]
        high, low = split(turned)
        wt3 = jnp.concatenate([high, high, low], axis=1)

    with jax.named_scope("links_and_field"):
        for arrival in arrivals[0]:
            arrival.wait_recv()
        for c, value in enumerate(block_transpose([landed[r, early, :] for r in range(8)])):
            sites[c * 80 : c * 80 + 48, :] = value

        def link(p, c):
            r, t = divmod(p * 18 + c, 5)
            return sites[r * 80 + 36 + t : r * 80 + 37 + t, :]

        u0 = read_matrix(lambda c: link(0, c))
        u1 = read_matrix(lambda c: link(1, c))
        one = [[[jnp.float32(1.0 if r == 0 and a == b else 0.0) for b in range(3)] for a in range(3)] for r in range(2)]
        prefix = mm(u0, u1)
        for step in (1, 2, 4):
            before = map_matrix(
                lambda m, i: jnp.where(lane1 >= 16 * step, pltpu.roll(m, 16 * step, 1), i), prefix, one
            )
            prefix = mm(before, prefix)
        start = map_matrix(lambda m, i: jnp.where(lane1 >= 16, pltpu.roll(m, 16, 1), i), prefix, one)

        def last_group(m):
            m = jnp.where(lane1 >= 112, m, 0.0)
            for step in (1, 2, 4):
                m = m + pltpu.roll(m, 16 * step, 1)
            return m

        loop = map_matrix(last_group, prefix)
        odd = mm(start, u0)
        for p, m in enumerate((start, odd)):
            for c, value in each(m):
                v_all[c, p] = jnp.broadcast_to(value, (8, LANES))
            for c, value in each(mm(loop, m)):
                v_wrap[c, p] = jnp.broadcast_to(value, (8, LANES))

        def read_sites(base):
            return read_matrix(
                lambda c: jnp.stack([sites[pl.ds(base + p * 18 + c, 8, stride=80), :] for p in range(2)])
            )

        v = read_matrix(lambda c: v_all[c])
        w = read_sites(0)
        for c, value in each(conjugate_by(v, w)):
            field[c] = value
        for c, value in each(conjugate_by(read_matrix(lambda c: v_wrap[c]), w)):
            wrapped[c] = value

    with jax.named_scope("window"):
        z[240:256, :] = jnp.zeros((16, 18 * LANES), jnp.bfloat16)
        for c in range(18):
            pieces = []
            for t in range(9):
                q, k = (t + 1) % 2, (t + 1) // 2
                if k == 0:
                    pieces.append(field[c, q])
                else:
                    joined = jnp.where(lane < 16 * k, wrapped[c, q], field[c, q])
                    pieces.append(pltpu.roll(joined, LANES - 16 * k, 1))
            pieces.append(jnp.zeros((8, LANES), jnp.float32))
            high, low = split(jnp.concatenate(pieces, axis=0))
            columns = slice(c * LANES, (c + 1) * LANES)
            z[0:80, columns] = high
            z[80:160, columns] = low
            z[160:240, columns] = high

    with jax.named_scope("pairs"):
        for arrival in arrivals[1]:
            arrival.wait_recv()
        for c, value in enumerate(block_transpose([landed[r, late, :] for r in range(8)])):
            sites[c * 80 + 48 : c * 80 + 80, :] = value
        v = read_matrix(lambda c: v_all[c])
        for c, value in each(conjugate_by(v, read_sites(41))):
            cot[c] = value

        @pl.loop(0, 8)
        def _(i):
            for p in range(2):
                w = read_matrix(lambda c: field[c, p])
                g = read_matrix(lambda c: jnp.broadcast_to(cot[c, p, pl.ds(i, 1), :], (8, LANES)))
                row = pl.multiple_of(p * 64 + i * 8, 8)
                for c, value in each(mm(w, g, left_h=True)):
                    pair[pl.ds(row, 8), c * LANES : (c + 1) * LANES] = value

    with jax.named_scope("products"):
        for chunk in range(9):
            columns = slice(chunk * 256, (chunk + 1) * 256)
            high, low = split(pair[:, columns])
            halves[0:128, columns] = high
            halves[128:256, columns] = low
            halves[256:384, columns] = high
        weights = lax.dot_general(
            halves[0:256, :], z[0:160, :], (((1,), (1,)), ((), ())), preferred_element_type=jnp.float32
        )
        half = weights[0:128] + weights[128:256]
        both = half[:, 0:80] + half[:, 80:160]
        both = both[0:64, 0:64] + both[64:128, 8:72]
        both = jnp.concatenate([both, jnp.zeros((64, 64), jnp.float32)], axis=1)
        for d in range(8):
            partial[d] = both[d * 8 : d * 8 + 8]
        share_copies, share_arrivals = exchange(partial, shares, slice(0, 8), share_send, share_recv)
        for copy in share_copies:
            copy.start()
        shares[me] = partial[me]
        started += share_copies
        for chunk in range(9):
            columns = slice(chunk * 256, (chunk + 1) * 256)
            mixed[:, columns] = jnp.dot(w3, z[:, columns], preferred_element_type=jnp.float32)
            line[:, columns] = jnp.dot(wt3, halves[:, columns], preferred_element_type=jnp.float32)

    for r in range(8):
        final[r * 40 + 32 : r * 40 + 40, :] = jnp.zeros((8, LANES), jnp.float32)
    back_arrivals = []
    for p, rows, send, recv in (
        (0, slice(0, 16), back_send, back_recv),
        (1, slice(16, 40), last_send, last_recv),
    ):
        with jax.named_scope("direct"):
            @pl.loop(0, 3)
            def _(a):
                sums = [[None, None] for _ in range(3)]
                for i in range(8):
                    lines = slice(p * 64 + i * 8, p * 64 + i * 8 + 8)
                    for k in range(3):
                        at = (a * 3 + k) * 2
                        gr = jnp.broadcast_to(cot[at, p, i : i + 1, :], (8, LANES))
                        gi = jnp.broadcast_to(cot[at + 1, p, i : i + 1, :], (8, LANES))
                        for b in range(3):
                            at = comp(0, b, k) * LANES
                            mr = mixed[lines, at : at + LANES]
                            at = comp(1, b, k) * LANES
                            mi = mixed[lines, at : at + LANES]
                            re = gr * mr + gi * mi
                            im = gi * mr - gr * mi
                            s = sums[b]
                            sums[b] = [re, im] if s[0] is None else [s[0] + re, s[1] + im]
                for b in range(3):
                    total[(a * 3 + b) * 2, p] = sums[b][0]
                    total[(a * 3 + b) * 2 + 1, p] = sums[b][1]

        with jax.named_scope("from_frame"):
            near, far = {}, {}
            for c in range(18):
                inside, outside = total[c, p], None
                for t in range(9):
                    if (t + 1) % 2 != p:
                        continue
                    k = (t + 1) // 2
                    piece = line[t * 8 : t * 8 + 8, c * LANES : (c + 1) * LANES]
                    if k == 0:
                        inside = inside + piece
                        continue
                    piece = pltpu.roll(piece, 16 * k, 1)
                    inside = inside + jnp.where(lane >= 16 * k, piece, 0.0)
                    beyond = jnp.where(lane < 16 * k, piece, 0.0)
                    outside = beyond if outside is None else outside + beyond
                near[c], far[c] = inside, outside
            first = conjugate_by_h(read_matrix(lambda c: v_all[c, p]), read_matrix(lambda c: near[c]))
            second = conjugate_by_h(read_matrix(lambda c: v_wrap[c, p]), read_matrix(lambda c: far[c]))
            for c, value in each(map_matrix(lambda m, n: m + n, first, second)):
                final[pl.ds(p * 18 + c, 8, stride=40), :] = value
            ready_rows = [final[r * 40 + rows.start : r * 40 + rows.stop, :] for r in range(8)]
            for d, value in enumerate(block_transpose(ready_rows)):
                back[d, rows, :] = value
            copies, incoming = exchange(back, returned, rows, send, recv)
            for copy in copies:
                copy.start()
            started += copies
            back_arrivals.append((rows, incoming))
            returned[me, rows, :] = back[me, rows, :]

        if p == 0:
            with jax.named_scope("share_sum"):
                for arrival in share_arrivals:
                    arrival.wait_recv()
                subtotal = shares[0]
                for s in range(1, 8):
                    subtotal = subtotal + shares[s]
                mine[...] = subtotal
                across_copies, across_arrivals = spread(
                    "yz", yz_count, mine, across, across_send, across_recv
                )
                for copy in across_copies:
                    copy.start()
                across[here] = subtotal
                started += across_copies

    with jax.named_scope("weight_sum"):
        for arrival in across_arrivals:
            arrival.wait_recv()
        summed = across[0]
        for s in range(1, yz_count):
            summed = summed + across[s]
        whole[me] = summed * scale
        whole_copies, whole_arrivals = spread("gx", 8, whole.at[me], whole, whole_send, whole_recv)
        for copy in whole_copies:
            copy.start()
        started += whole_copies

    with jax.named_scope("unpack"):
        for rows, incoming in back_arrivals:
            for arrival in incoming:
                arrival.wait_recv()
            for c, value in enumerate(block_transpose([returned[r, rows, :] for r in range(8)])):
                out_ref[c, rows, :] = value
        for arrival in whole_arrivals:
            arrival.wait_recv()
        gw_out[...] = whole[...]
        for copy in started:
            copy.wait_send()


def place_kernel(rows_ref, weights_ref, out_ref, gw_out):
    for x in range(2):
        for ab in range(9):
            row = x * 18 + ab * 2
            out_ref[:, x, ab // 3, ab % 3, :, :] = rows_ref[:, row : row + 2, :]
    for i in range(8):
        value = weights_ref[i]
        for l in range(8):
            gw_out[pl.ds(i * 64 + l, 8, stride=8), :] = value[:, l * 8 : l * 8 + 8]


def resident(scale, yz_count, gauge_links, in_field, cotangent, bilinear_weights):
    f32 = jnp.float32
    vmem = pl.BlockSpec(memory_space=pltpu.VMEM)
    dma = pltpu.SemaphoreType.DMA
    placed = pl.BlockSpec(memory_space=pltpu.HBM)
    rows, weights = pl.pallas_call(
        functools.partial(whole_kernel, scale, yz_count),
        out_shape=(
            jax.ShapeDtypeStruct((8, 40, LANES), f32),
            jax.ShapeDtypeStruct((8, 8, LANES), f32),
        ),
        in_specs=[placed] * 4,
        out_specs=(vmem, vmem),
        scratch_shapes=[
            pltpu.VMEM((2, 3, 3, 2, LANES), f32),
            pltpu.VMEM((8, 2, 3, 3, 2, LANES), f32),
            pltpu.VMEM((8, 2, 3, 3, 2, LANES), f32),
            pltpu.VMEM((512, 8), f32),
            pltpu.VMEM((8, 80, LANES), f32),
            pltpu.VMEM((8, 80, LANES), f32),
            pltpu.VMEM((8, 80, LANES), f32),
            pltpu.VMEM((640, LANES), f32),
            pltpu.VMEM((18, 2, 8, LANES), f32),
            pltpu.VMEM((18, 2, 8, LANES), f32),
            pltpu.VMEM((18, 2, 8, LANES), f32),
            pltpu.VMEM((18, 2, 8, LANES), f32),
            pltpu.VMEM((18, 2, 8, LANES), f32),
            pltpu.VMEM((128, 256), f32),
            pltpu.VMEM((256, 18 * LANES), jnp.bfloat16),
            pltpu.VMEM((128, 18 * LANES), f32),
            pltpu.VMEM((384, 18 * LANES), jnp.bfloat16),
            pltpu.VMEM((128, 18 * LANES), f32),
            pltpu.VMEM((80, 18 * LANES), f32),
            pltpu.VMEM((18, 2, 8, LANES), f32),
            pltpu.VMEM((320, LANES), f32),
            pltpu.VMEM((8, 40, LANES), f32),
            pltpu.VMEM((8, 40, LANES), f32),
            pltpu.VMEM((8, 8, LANES), f32),
            pltpu.VMEM((8, 8, LANES), f32),
            pltpu.VMEM((8, LANES), f32),
            pltpu.VMEM((yz_count, 8, LANES), f32),
            pltpu.VMEM((8, 8, LANES), f32),
        ]
        + [dma((8,))] * 10
        + [dma((yz_count,)), dma((yz_count,)), dma((8,)), dma((8,)), dma((4,))],
        compiler_params=pltpu.CompilerParams(
            collective_id=0, has_side_effects=True, vmem_limit_bytes=VMEM_BYTES
        ),
        name="lattice_backward",
    )(
        pltpu.with_memory_space_constraint(gauge_links.transpose(0, 2, 3, 1, 4), pltpu.HBM),
        pltpu.with_memory_space_constraint(in_field.transpose(0, 1, 3, 4, 2, 5), pltpu.HBM),
        pltpu.with_memory_space_constraint(cotangent.transpose(0, 1, 3, 4, 2, 5), pltpu.HBM),
        pltpu.with_memory_space_constraint(bilinear_weights.reshape(512, 8), pltpu.HBM),
    )
    grad_field, grad_weights = pl.pallas_call(
        place_kernel,
        out_shape=(
            jax.ShapeDtypeStruct((8, 2, 3, 3, 2, LANES), f32),
            jax.ShapeDtypeStruct((512, 8), f32),
        ),
        in_specs=[vmem] * 2,
        out_specs=(vmem, vmem),
        compiler_params=pltpu.CompilerParams(vmem_limit_bytes=VMEM_BYTES),
        name="place_rows",
    )(rows, weights)
    return grad_field.transpose(0, 1, 4, 2, 3, 5), grad_weights.reshape(8, 8, 8, 8)


def mm(left, right, left_h=False, right_h=False):
    def pick(m, h, a, b):
        return (m[0][b][a], m[1][b][a]) if h else (m[0][a][b], m[1][a][b])

    real = [[None] * 3 for _ in range(3)]
    imag = [[None] * 3 for _ in range(3)]
    for a in range(3):
        for b in range(3):
            re = im = None
            for k in range(3):
                lr, li = pick(left, left_h, a, k)
                rr, ri = pick(right, right_h, k, b)
                rr_lr, ii = lr * rr, li * ri
                re = rr_lr if re is None else re + rr_lr
                re = re + ii if left_h != right_h else re - ii
                first, second = lr * ri, li * rr
                if right_h and left_h:
                    term = -(first + second)
                elif right_h:
                    term = second - first
                elif left_h:
                    term = first - second
                else:
                    term = first + second
                im = term if im is None else im + term
            real[a][b], imag[a][b] = re, im
    return [real, imag]


def map_matrix(f, *ms):
    return [[[f(*(m[r][a][b] for m in ms)) for b in range(3)] for a in range(3)] for r in range(2)]


def comp(r, a, b):
    return (a * 3 + b) * 2 + r


def read_matrix(f):
    return [[[f(comp(r, a, b)) for b in range(3)] for a in range(3)] for r in range(2)]


def each(m):
    for r in range(2):
        for a in range(3):
            for b in range(3):
                yield comp(r, a, b), m[r][a][b]


def conjugate_by(v, m):
    return mm(mm(v, m), v, right_h=True)


def conjugate_by_h(v, m):
    return mm(mm(v, m, left_h=True), v)


def split(value):
    high = value.astype(jnp.bfloat16)
    return high, (value - high.astype(jnp.float32)).astype(jnp.bfloat16)


def per_device(gauge_links, in_field, cotangent, bilinear_weights):
    gx = lax.axis_size("gx")
    yz = lax.axis_size("yz")
    fits = (
        gx == 8
        and in_field.shape == (8, 2, 2, 3, 3, LANES)
        and bilinear_weights.shape == (8, 8, 8, 8)
    )
    if not fits:
        return general(gauge_links, in_field, cotangent, bilinear_weights)
    total = gauge_links.shape[0] * gx * gauge_links.shape[-1] * yz
    scale = 1.0 / math.sqrt(100.0 * total)
    return resident(scale, yz, gauge_links, in_field, cotangent, bilinear_weights)


def solution(mesh):
    placed = (
        P("gx", None, None, None, "yz"),
        P(None, "gx", None, None, None, "yz"),
        P(None, "gx", None, None, None, "yz"),
        P(),
    )
    return jax.shard_map(
        per_device,
        mesh=mesh,
        in_specs=placed,
        out_specs=(P(None, "gx", None, None, None, "yz"), P()),
        check_vma=False,
    )
```

```python
import functools
import math

import jax
import jax.numpy as jnp
from jax import lax
from jax.experimental import pallas as pl
from jax.experimental.pallas import tpu as pltpu
from jax.sharding import PartitionSpec as P

MESH = pl.DeviceIdType.MESH
LANES = 128
VMEM_BYTES = 20 * 1024 * 1024


def from_behind(block, axis, distance):
    devices = range(lax.axis_size(axis))
    route = [((i - distance) % len(devices), i) for i in devices]
    return lax.ppermute(block, axis, route)


def matmul_three(left, right):
    return jnp.sum(left[..., :, :, None, :] * right[..., None, :, :, :], axis=-3)


def complex_mul(left, right):
    left_re = left[..., 0, :, :, :]
    left_im = left[..., 1, :, :, :]
    right_re = right[..., 0, :, :, :]
    right_im = right[..., 1, :, :, :]
    real_part = matmul_three(left_re, right_re) - matmul_three(left_im, right_im)
    imag_part = matmul_three(left_re, right_im) + matmul_three(left_im, right_re)
    return jnp.stack([real_part, imag_part], axis=-4)


def dagger(matrix):
    swapped = jnp.swapaxes(matrix, -3, -2)
    return jnp.stack([swapped[..., 0, :, :, :], -swapped[..., 1, :, :, :]], axis=-4)


def general(gauge_links, in_field, cotangent, bilinear_weights):
    part_x = gauge_links.shape[0]
    channels = in_field.shape[0]
    line_count = bilinear_weights.shape[2]
    site_count = gauge_links.shape[-1]
    reach_devs = (part_x - 1 + line_count) // part_x
    highest = lax.Precision.HIGHEST
    weight_rows = bilinear_weights.reshape(channels * channels, line_count * channels)

    def advance(carry, unused):
        arrived = from_behind(carry, "gx", -1)
        return (arrived, arrived)

    unused_last, stacked = lax.scan(advance, (gauge_links, in_field), None, length=reach_devs)
    window_links = jnp.concatenate(
        [gauge_links, stacked[0].reshape((-1, 2, 3, 3, site_count))], axis=0
    )
    later_field = jnp.moveaxis(stacked[1], 0, 1).reshape((channels, -1, 2, 3, 3, site_count))
    window_field = jnp.concatenate([in_field, later_field], axis=1)
    pair_grad = complex_mul(dagger(in_field)[None], cotangent[:, None]).reshape(
        channels * channels, -1
    )

    def forward_step(line, offset):
        shifted = lax.dynamic_slice_in_dim(window_field, offset, part_x, axis=1)
        transported = complex_mul(complex_mul(line[None], shifted), dagger(line)[None])
        next_links = lax.dynamic_slice_in_dim(window_links, offset, part_x, axis=0)
        return (complex_mul(line, next_links), (transported, line))

    offsets = jnp.arange(1, line_count + 1, dtype=jnp.int32)
    unused_line, (all_transported, all_lines) = lax.scan(forward_step, gauge_links, offsets)
    transported_flat = all_transported.reshape(line_count * channels, -1)
    partial_grad = lax.dot_general(
        pair_grad, transported_flat, (((1,), (1,)), ((), ())), precision=highest
    )
    mixed = jnp.dot(weight_rows, transported_flat, precision=highest)
    mixed_matrix = mixed.reshape((channels, channels) + in_field.shape[1:])
    direct = jnp.sum(complex_mul(cotangent[:, None], dagger(mixed_matrix)), axis=0)
    line_grad = jnp.dot(weight_rows.T, pair_grad, precision=highest)
    line_grad = line_grad.reshape((line_count,) + in_field.shape)
    accumulator = jnp.zeros((channels, (reach_devs + 1) * part_x, 2, 3, 3, site_count), jnp.float32)

    def backward_step(carry, inputs):
        offset, grad_piece, line = inputs
        contribution = complex_mul(complex_mul(dagger(line)[None], grad_piece), line[None])
        current = lax.dynamic_slice_in_dim(carry, offset, part_x, axis=1)
        return (
            lax.dynamic_update_slice_in_dim(carry, current + contribution, offset, axis=1),
            None,
        )

    accumulator, unused_out = lax.scan(backward_step, accumulator, (offsets, line_grad, all_lines))
    block_count = reach_devs + 1
    half_span = 1 << reach_devs.bit_length() - 1
    pending = accumulator
    while half_span >= 1:
        moving = pending[:, half_span * part_x : block_count * part_x]
        arrived = from_behind(moving, "gx", half_span)
        kept_count = block_count - half_span
        updated = pending[:, : kept_count * part_x] + arrived
        pending = jnp.concatenate(
            [updated, pending[:, kept_count * part_x : half_span * part_x]], axis=1
        )
        block_count = half_span
        half_span = half_span // 2
    grad_field = direct + pending
    total_x = part_x * lax.axis_size("gx")
    total_sites = site_count * lax.axis_size("yz")
    summed = lax.psum(partial_grad, ("gx", "yz"))
    grad_weights = summed.reshape(channels, channels, line_count, channels) / math.sqrt(
        100.0 * total_x * total_sites
    )
    return (grad_field, grad_weights)


def block_transpose(arrays):
    arrays = list(arrays)
    lane = lax.broadcasted_iota(jnp.int32, arrays[0].shape, 1)
    for bit in (1, 2, 4):
        upper = (lane & (16 * bit)) != 0
        for r in range(8):
            if r & bit:
                continue
            low, high = arrays[r], arrays[r | bit]
            arrays[r] = jnp.where(upper, pltpu.roll(high, 16 * bit, 1), low)
            arrays[r | bit] = jnp.where(upper, high, pltpu.roll(low, LANES - 16 * bit, 1))
    return arrays


def greet(axes):
    barrier = pltpu.get_barrier_semaphore()
    total = 0
    for axis, count in axes:
        me = lax.axis_index(axis)
        for k in range(1, count):
            peer = lax.rem(me + k, count)
            pl.semaphore_signal(barrier, inc=1, device_id={axis: peer}, device_id_type=MESH)
        total += count - 1
    return lambda: pl.semaphore_wait(barrier, total)


def spread(axis, count, source, target, send, recv):
    at = lax.axis_index(axis)
    outgoing, incoming = [], []
    for k in range(1, count):
        for found, slot, there in (
            (outgoing, at, lax.rem(at + k, count)),
            (incoming, lax.rem(at + count - k, count), lax.rem(at + count - k, count)),
        ):
            found.append(
                pltpu.make_async_remote_copy(
                    src_ref=source,
                    dst_ref=target.at[slot],
                    send_sem=send.at[k],
                    recv_sem=recv.at[k],
                    device_id={axis: there},
                    device_id_type=MESH,
                )
            )
    return outgoing, incoming


def other(me, mask):
    for bit in (1, 2, 4):
        if mask & bit:
            me = me + bit - 2 * bit * (me // bit % 2)
    return me


FAR_FIRST = (4, 5, 6, 7, 2, 3, 1)


def exchange(source, target, rows, send_sem, recv_sem):
    me = lax.axis_index("gx")
    outgoing, incoming = [], []
    for k in FAR_FIRST:
        peer = other(me, k)
        for found, slot in ((outgoing, me), (incoming, peer)):
            found.append(
                pltpu.make_async_remote_copy(
                    src_ref=source.at[peer, rows, :],
                    dst_ref=target.at[slot, rows, :],
                    send_sem=send_sem.at[k],
                    recv_sem=recv_sem.at[k],
                    device_id={"gx": peer},
                    device_id_type=MESH,
                )
            )
    return outgoing, incoming


def deal(source, target, send_sem, recv_sem):
    me = lax.axis_index("yz")
    outgoing, incoming = [], []
    for k in range(1, 4):
        peer = other(me, k)
        for found, slot in ((outgoing, me), (incoming, peer)):
            found.append(
                pltpu.make_async_remote_copy(
                    src_ref=source.at[peer],
                    dst_ref=target.at[slot],
                    send_sem=send_sem.at[k],
                    recv_sem=recv_sem.at[k],
                    device_id={"yz": peer},
                    device_id_type=MESH,
                )
            )
    return outgoing, incoming


def whole_kernel(
    scale,
    yz_count,
    u_hbm,
    w_hbm,
    g_hbm,
    weight_hbm,
    out_ref,
    gw_out,
    u_ref,
    w_ref,
    g_ref,
    weight_ref,
    packed,
    sending,
    landed,
    sites,
    field,
    cot,
    wrapped,
    v_all,
    v_wrap,
    rows_ref,
    z,
    pair,
    halves,
    mixed,
    line,
    total,
    final,
    back,
    returned,
    partial,
    shares,
    mine,
    across,
    whole,
    first_send,
    first_recv,
    second_send,
    second_recv,
    third_send,
    third_recv,
    back_send,
    back_recv,
    last_send,
    last_recv,
    share_send,
    share_recv,
    across_send,
    across_recv,
    whole_send,
    whole_recv,
    load_sem,
):
    me = lax.axis_index("gx")
    here = lax.axis_index("yz")
    loads = [
        pltpu.make_async_copy(source, target, load_sem.at[k])
        for k, (source, target) in enumerate(
            ((w_hbm, w_ref), (u_hbm, u_ref), (g_hbm, g_ref), (weight_hbm, weight_ref))
        )
    ]
    for load in loads:
        load.start()
    ready = greet((("gx", 8), ("yz", yz_count)))
    lane1 = lax.broadcasted_iota(jnp.int32, (1, LANES), 1)
    lane = lax.broadcasted_iota(jnp.int32, (8, LANES), 1)
    early, even, odd_part = slice(0, 48), slice(48, 64), slice(64, 80)

    with jax.named_scope("pack"):
        packed[:, 32:48, :] = jnp.zeros((8, 16, LANES), jnp.float32)
        packed[:, 72:80, :] = jnp.zeros((8, 8, LANES), jnp.float32)
        loads[0].wait()
        loads[1].wait()
        for x in range(2):
            for ab in range(9):
                row = x * 18 + ab * 2
                packed[:, row : row + 2, :] = w_ref[:, x, ab // 3, ab % 3, :, :]
                for part in range(2):
                    r, t = divmod(row + part, 5)
                    packed[r, 36 + t : 37 + t, :] = u_ref[x, ab // 3, ab % 3, part : part + 1, :]
        loads[2].wait()
        for x in range(2):
            for ab in range(9):
                row = x * 18 + ab * 2
                packed[:, 41 + row : 43 + row, :] = g_ref[:, x, ab // 3, ab % 3, :, :]
        started = []
        arrivals = []
        for rows, send, recv in (
            (early, first_send, first_recv),
            (even, second_send, second_recv),
            (odd_part, third_send, third_recv),
        ):
            for d, value in enumerate(block_transpose([packed[r, rows, :] for r in range(8)])):
                sending[d, rows, :] = value
            if not started:
                ready()
            copies, incoming = exchange(sending, landed, rows, send, recv)
            for copy in copies:
                copy.start()
            started += copies
            arrivals.append(incoming)
        landed[me] = sending[me]

    with jax.named_scope("weights"):
        loads[3].wait()
        rows_ref[...] = jnp.zeros((128, 256), jnp.float32)
        for i in range(8):
            pieces = [weight_ref[pl.ds(i * 64 + l, 8, stride=8), :] for l in range(8)]
            joined = jnp.concatenate(pieces, axis=1)
            rows_ref[i * 8 : i * 8 + 8, 0:64] = joined
            rows_ref[64 + i * 8 : 72 + i * 8, 8:72] = joined
        value = rows_ref[...]
        high = value.astype(jnp.bfloat16).astype(jnp.float32)
        low = value - high
        w3 = (high + pltpu.roll(high, 80, 1) + pltpu.roll(low, 160, 1)).astype(jnp.bfloat16)
        turned = value[:, 0:LANES].T[0:80]
        high = turned.astype(jnp.bfloat16).astype(jnp.float32)
        low = turned - high
        wt3 = []
        for p in range(2):
            part = slice(p * 64, p * 64 + 64)
            joined = jnp.concatenate([high[:, part], high[:, part], low[:, part]], axis=1)
            wt3.append(joined.astype(jnp.bfloat16))

    with jax.named_scope("links_and_field"):
        for arrival in arrivals[0]:
            arrival.wait_recv()
        for c, value in enumerate(block_transpose([landed[r, early, :] for r in range(8)])):
            sites[c * 80 : c * 80 + 48, :] = value

        def link(p, c):
            r, t = divmod(p * 18 + c, 5)
            return sites[r * 80 + 36 + t : r * 80 + 37 + t, :]

        u0 = read_matrix(lambda c: link(0, c))
        u1 = read_matrix(lambda c: link(1, c))
        one = [[[jnp.float32(1.0 if r == 0 and a == b else 0.0) for b in range(3)] for a in range(3)] for r in range(2)]
        prefix = mm(u0, u1)
        for step in (1, 2, 4):
            before = map_matrix(
                lambda m, i: jnp.where(lane1 >= 16 * step, pltpu.roll(m, 16 * step, 1), i), prefix, one
            )
            prefix = mm(before, prefix)
        start = map_matrix(lambda m, i: jnp.where(lane1 >= 16, pltpu.roll(m, 16, 1), i), prefix, one)

        def last_group(m):
            m = jnp.where(lane1 >= 112, m, 0.0)
            for step in (1, 2, 4):
                m = m + pltpu.roll(m, 16 * step, 1)
            return m

        loop = map_matrix(last_group, prefix)
        odd = mm(start, u0)
        for p, m in enumerate((start, odd)):
            for c, value in each(m):
                v_all[c, p] = jnp.broadcast_to(value, (8, LANES))
            for c, value in each(mm(loop, m)):
                v_wrap[c, p] = jnp.broadcast_to(value, (8, LANES))

        def read_sites(base):
            return read_matrix(
                lambda c: jnp.stack([sites[pl.ds(base + p * 18 + c, 8, stride=80), :] for p in range(2)])
            )

        v = read_matrix(lambda c: v_all[c])
        w = read_sites(0)
        for c, value in each(conjugate_by(v, w)):
            field[c] = value
        for c, value in each(conjugate_by(read_matrix(lambda c: v_wrap[c]), w)):
            wrapped[c] = value

    with jax.named_scope("window"):
        z[240:256, :] = jnp.zeros((16, 18 * LANES), jnp.bfloat16)
        for c in range(18):
            pieces = []
            for t in range(9):
                q, k = (t + 1) % 2, (t + 1) // 2
                if k == 0:
                    pieces.append(field[c, q])
                else:
                    joined = jnp.where(lane < 16 * k, wrapped[c, q], field[c, q])
                    pieces.append(pltpu.roll(joined, LANES - 16 * k, 1))
            pieces.append(jnp.zeros((8, LANES), jnp.float32))
            high, low = split(jnp.concatenate(pieces, axis=0))
            columns = slice(c * LANES, (c + 1) * LANES)
            z[0:80, columns] = high
            z[80:160, columns] = low
            z[160:240, columns] = high

    def direct(p):
        @pl.loop(0, 3)
        def _(a):
            sums = [[None, None] for _ in range(3)]
            for i in range(8):
                lines = slice(p * 64 + i * 8, p * 64 + i * 8 + 8)
                for k in range(3):
                    at = (a * 3 + k) * 2
                    gr = jnp.broadcast_to(cot[at, p, i : i + 1, :], (8, LANES))
                    gi = jnp.broadcast_to(cot[at + 1, p, i : i + 1, :], (8, LANES))
                    for b in range(3):
                        at = comp(0, b, k) * LANES
                        mr = mixed[lines, at : at + LANES]
                        at = comp(1, b, k) * LANES
                        mi = mixed[lines, at : at + LANES]
                        re = gr * mr + gi * mi
                        im = gi * mr - gr * mi
                        s = sums[b]
                        sums[b] = [re, im] if s[0] is None else [s[0] + re, s[1] + im]
            for b in range(3):
                total[(a * 3 + b) * 2, p] = sums[b][0]
                total[(a * 3 + b) * 2 + 1, p] = sums[b][1]

    with jax.named_scope("mixed"):
        for chunk in range(9):
            columns = slice(chunk * 256, (chunk + 1) * 256)
            mixed[:, columns] = jnp.dot(w3, z[:, columns], preferred_element_type=jnp.float32)

    sums = []
    for p, rows in ((0, even), (1, odd_part)):
        with jax.named_scope("pairs"):
            for arrival in arrivals[1 + p]:
                arrival.wait_recv()
            for c, value in enumerate(block_transpose([landed[r, rows, :] for r in range(8)])):
                sites[c * 80 + rows.start : c * 80 + rows.stop, :] = value
            v = read_matrix(lambda c: v_all[c, p])
            g = read_matrix(lambda c: sites[pl.ds(41 + p * 18 + c, 8, stride=80), :])
            for c, value in each(conjugate_by(v, g)):
                cot[c, p] = value

            @pl.loop(0, 8)
            def _(i):
                w = read_matrix(lambda c: field[c, p])
                g = read_matrix(lambda c: jnp.broadcast_to(cot[c, p, pl.ds(i, 1), :], (8, LANES)))
                row = pl.multiple_of(i * 8, 8)
                for c, value in each(mm(w, g, left_h=True)):
                    pair[pl.ds(row, 8), c * LANES : (c + 1) * LANES] = value

        with jax.named_scope("products"):
            for chunk in range(9):
                columns = slice(chunk * 256, (chunk + 1) * 256)
                high, low = split(pair[:, columns])
                halves[0:64, columns] = high
                halves[64:128, columns] = low
                halves[128:192, columns] = high
            weights = lax.dot_general(
                halves[0:128, :], z[0:160, :], (((1,), (1,)), ((), ())), preferred_element_type=jnp.float32
            )
            half = weights[0:64] + weights[64:128]
            half = half[:, 0:80] + half[:, 80:160]
            sums.append(half[:, 8 * p : 8 * p + 64])
            if p == 1:
                both = sums[0] + sums[1]
                both = jnp.concatenate([both[0:32], both[32:64]], axis=1)
                for d in range(4):
                    partial[d] = both[d * 8 : d * 8 + 8]
                share_copies, share_arrivals = deal(partial, shares, share_send, share_recv)
                for copy in share_copies:
                    copy.start()
                shares[here] = partial[here]
                started += share_copies
            for chunk in range(9):
                columns = slice(chunk * 256, (chunk + 1) * 256)
                value = jnp.dot(wt3[p], halves[:, columns], preferred_element_type=jnp.float32)
                line[:, columns] = value if p == 0 else line[:, columns] + value
        if p == 0:
            direct(0)

    for r in range(8):
        final[r * 40 + 32 : r * 40 + 40, :] = jnp.zeros((8, LANES), jnp.float32)
    back_arrivals = []
    for p, rows, send, recv in (
        (0, slice(0, 16), back_send, back_recv),
        (1, slice(16, 40), last_send, last_recv),
    ):
        if p == 1:
            direct(1)
        with jax.named_scope("from_frame"):
            near, far = {}, {}
            for c in range(18):
                inside, outside = total[c, p], None
                for t in range(9):
                    if (t + 1) % 2 != p:
                        continue
                    k = (t + 1) // 2
                    piece = line[t * 8 : t * 8 + 8, c * LANES : (c + 1) * LANES]
                    if k == 0:
                        inside = inside + piece
                        continue
                    piece = pltpu.roll(piece, 16 * k, 1)
                    inside = inside + jnp.where(lane >= 16 * k, piece, 0.0)
                    beyond = jnp.where(lane < 16 * k, piece, 0.0)
                    outside = beyond if outside is None else outside + beyond
                near[c], far[c] = inside, outside
            first = conjugate_by_h(read_matrix(lambda c: v_all[c, p]), read_matrix(lambda c: near[c]))
            second = conjugate_by_h(read_matrix(lambda c: v_wrap[c, p]), read_matrix(lambda c: far[c]))
            for c, value in each(map_matrix(lambda m, n: m + n, first, second)):
                final[pl.ds(p * 18 + c, 8, stride=40), :] = value
            ready_rows = [final[r * 40 + rows.start : r * 40 + rows.stop, :] for r in range(8)]
            for d, value in enumerate(block_transpose(ready_rows)):
                back[d, rows, :] = value
            copies, incoming = exchange(back, returned, rows, send, recv)
            for copy in copies:
                copy.start()
            started += copies
            back_arrivals.append((rows, incoming))
            returned[me, rows, :] = back[me, rows, :]

    with jax.named_scope("share_sum"):
        for arrival in share_arrivals:
            arrival.wait_recv()
        subtotal = shares[0]
        for s in range(1, yz_count):
            subtotal = subtotal + shares[s]
        mine[...] = subtotal
        across_copies, across_arrivals = spread("gx", 8, mine, across, across_send, across_recv)
        for copy in across_copies:
            copy.start()
        across[me] = subtotal
        started += across_copies

    with jax.named_scope("unpack"):
        for p, (rows, incoming) in enumerate(back_arrivals):
            for arrival in incoming:
                arrival.wait_recv()
            for c, value in enumerate(block_transpose([returned[r, rows, :] for r in range(8)])):
                out_ref[c, rows, :] = value
            if p == 0:
                for arrival in across_arrivals:
                    arrival.wait_recv()
                summed = across[0]
                for s in range(1, 8):
                    summed = summed + across[s]
                whole[here] = summed * scale
                whole_copies, whole_arrivals = spread(
                    "yz", yz_count, whole.at[here], whole, whole_send, whole_recv
                )
                for copy in whole_copies:
                    copy.start()
                started += whole_copies
        for arrival in whole_arrivals:
            arrival.wait_recv()
        gw_out[...] = whole[...]
        for copy in started:
            copy.wait_send()


def place_kernel(rows_ref, weights_ref, out_ref, gw_out):
    for x in range(2):
        for ab in range(9):
            row = x * 18 + ab * 2
            out_ref[:, x, ab // 3, ab % 3, :, :] = rows_ref[:, row : row + 2, :]
    for i in range(8):
        value = weights_ref[i % 4]
        for l in range(8):
            at = i // 4 * 64 + l * 8
            gw_out[pl.ds(i * 64 + l, 8, stride=8), :] = value[:, at : at + 8]


def resident(scale, yz_count, gauge_links, in_field, cotangent, bilinear_weights):
    f32 = jnp.float32
    vmem = pl.BlockSpec(memory_space=pltpu.VMEM)
    dma = pltpu.SemaphoreType.DMA
    placed = pl.BlockSpec(memory_space=pltpu.HBM)
    rows, weights = pl.pallas_call(
        functools.partial(whole_kernel, scale, yz_count),
        out_shape=(
            jax.ShapeDtypeStruct((8, 40, LANES), f32),
            jax.ShapeDtypeStruct((yz_count, 8, LANES), f32),
        ),
        in_specs=[placed] * 4,
        out_specs=(vmem, vmem),
        scratch_shapes=[
            pltpu.VMEM((2, 3, 3, 2, LANES), f32),
            pltpu.VMEM((8, 2, 3, 3, 2, LANES), f32),
            pltpu.VMEM((8, 2, 3, 3, 2, LANES), f32),
            pltpu.VMEM((512, 8), f32),
            pltpu.VMEM((8, 80, LANES), f32),
            pltpu.VMEM((8, 80, LANES), f32),
            pltpu.VMEM((8, 80, LANES), f32),
            pltpu.VMEM((640, LANES), f32),
            pltpu.VMEM((18, 2, 8, LANES), f32),
            pltpu.VMEM((18, 2, 8, LANES), f32),
            pltpu.VMEM((18, 2, 8, LANES), f32),
            pltpu.VMEM((18, 2, 8, LANES), f32),
            pltpu.VMEM((18, 2, 8, LANES), f32),
            pltpu.VMEM((128, 256), f32),
            pltpu.VMEM((256, 18 * LANES), jnp.bfloat16),
            pltpu.VMEM((64, 18 * LANES), f32),
            pltpu.VMEM((192, 18 * LANES), jnp.bfloat16),
            pltpu.VMEM((128, 18 * LANES), f32),
            pltpu.VMEM((80, 18 * LANES), f32),
            pltpu.VMEM((18, 2, 8, LANES), f32),
            pltpu.VMEM((320, LANES), f32),
            pltpu.VMEM((8, 40, LANES), f32),
            pltpu.VMEM((8, 40, LANES), f32),
            pltpu.VMEM((yz_count, 8, LANES), f32),
            pltpu.VMEM((yz_count, 8, LANES), f32),
            pltpu.VMEM((8, LANES), f32),
            pltpu.VMEM((8, 8, LANES), f32),
            pltpu.VMEM((yz_count, 8, LANES), f32),
        ]
        + [dma((8,))] * 10
        + [dma((yz_count,))] * 2
        + [dma((8,))] * 2
        + [dma((yz_count,))] * 2
        + [dma((4,))],
        compiler_params=pltpu.CompilerParams(
            collective_id=0, has_side_effects=True, vmem_limit_bytes=VMEM_BYTES
        ),
        name="lattice_backward",
    )(
        pltpu.with_memory_space_constraint(gauge_links.transpose(0, 2, 3, 1, 4), pltpu.HBM),
        pltpu.with_memory_space_constraint(in_field.transpose(0, 1, 3, 4, 2, 5), pltpu.HBM),
        pltpu.with_memory_space_constraint(cotangent.transpose(0, 1, 3, 4, 2, 5), pltpu.HBM),
        pltpu.with_memory_space_constraint(bilinear_weights.reshape(512, 8), pltpu.HBM),
    )
    grad_field, grad_weights = pl.pallas_call(
        place_kernel,
        out_shape=(
            jax.ShapeDtypeStruct((8, 2, 3, 3, 2, LANES), f32),
            jax.ShapeDtypeStruct((512, 8), f32),
        ),
        in_specs=[vmem] * 2,
        out_specs=(vmem, vmem),
        compiler_params=pltpu.CompilerParams(vmem_limit_bytes=VMEM_BYTES),
        name="place_rows",
    )(rows, weights)
    return grad_field.transpose(0, 1, 4, 2, 3, 5), grad_weights.reshape(8, 8, 8, 8)


def mm(left, right, left_h=False, right_h=False):
    def pick(m, h, a, b):
        return (m[0][b][a], m[1][b][a]) if h else (m[0][a][b], m[1][a][b])

    real = [[None] * 3 for _ in range(3)]
    imag = [[None] * 3 for _ in range(3)]
    for a in range(3):
        for b in range(3):
            re = im = None
            for k in range(3):
                lr, li = pick(left, left_h, a, k)
                rr, ri = pick(right, right_h, k, b)
                rr_lr, ii = lr * rr, li * ri
                re = rr_lr if re is None else re + rr_lr
                re = re + ii if left_h != right_h else re - ii
                first, second = lr * ri, li * rr
                if right_h and left_h:
                    term = -(first + second)
                elif right_h:
                    term = second - first
                elif left_h:
                    term = first - second
                else:
                    term = first + second
                im = term if im is None else im + term
            real[a][b], imag[a][b] = re, im
    return [real, imag]


def map_matrix(f, *ms):
    return [[[f(*(m[r][a][b] for m in ms)) for b in range(3)] for a in range(3)] for r in range(2)]


def comp(r, a, b):
    return (a * 3 + b) * 2 + r


def read_matrix(f):
    return [[[f(comp(r, a, b)) for b in range(3)] for a in range(3)] for r in range(2)]


def each(m):
    for r in range(2):
        for a in range(3):
            for b in range(3):
                yield comp(r, a, b), m[r][a][b]


def conjugate_by(v, m):
    return mm(mm(v, m), v, right_h=True)


def conjugate_by_h(v, m):
    return mm(mm(v, m, left_h=True), v)


def split(value):
    high = value.astype(jnp.bfloat16)
    return high, (value - high.astype(jnp.float32)).astype(jnp.bfloat16)


def per_device(gauge_links, in_field, cotangent, bilinear_weights):
    gx = lax.axis_size("gx")
    yz = lax.axis_size("yz")
    fits = (
        gx == 8
        and yz == 4
        and in_field.shape == (8, 2, 2, 3, 3, LANES)
        and bilinear_weights.shape == (8, 8, 8, 8)
    )
    if not fits:
        return general(gauge_links, in_field, cotangent, bilinear_weights)
    total = gauge_links.shape[0] * gx * gauge_links.shape[-1] * yz
    scale = 1.0 / math.sqrt(100.0 * total)
    return resident(scale, yz, gauge_links, in_field, cotangent, bilinear_weights)


def solution(mesh):
    placed = (
        P("gx", None, None, None, "yz"),
        P(None, "gx", None, None, None, "yz"),
        P(None, "gx", None, None, None, "yz"),
        P(),
    )
    return jax.shard_map(
        per_device,
        mesh=mesh,
        in_specs=placed,
        out_specs=(P(None, "gx", None, None, None, "yz"), P()),
        check_vma=False,
    )
```

```python
import functools
import math

import jax
import jax.numpy as jnp
from jax import lax
from jax.experimental import pallas as pl
from jax.experimental.pallas import tpu as pltpu
from jax.sharding import PartitionSpec as P

MESH = pl.DeviceIdType.MESH
LANES = 128
VMEM_BYTES = 20 * 1024 * 1024


def from_behind(block, axis, distance):
    devices = range(lax.axis_size(axis))
    route = [((i - distance) % len(devices), i) for i in devices]
    return lax.ppermute(block, axis, route)


def matmul_three(left, right):
    return jnp.sum(left[..., :, :, None, :] * right[..., None, :, :, :], axis=-3)


def complex_mul(left, right):
    left_re = left[..., 0, :, :, :]
    left_im = left[..., 1, :, :, :]
    right_re = right[..., 0, :, :, :]
    right_im = right[..., 1, :, :, :]
    real_part = matmul_three(left_re, right_re) - matmul_three(left_im, right_im)
    imag_part = matmul_three(left_re, right_im) + matmul_three(left_im, right_re)
    return jnp.stack([real_part, imag_part], axis=-4)


def dagger(matrix):
    swapped = jnp.swapaxes(matrix, -3, -2)
    return jnp.stack([swapped[..., 0, :, :, :], -swapped[..., 1, :, :, :]], axis=-4)


def general(gauge_links, in_field, cotangent, bilinear_weights):
    part_x = gauge_links.shape[0]
    channels = in_field.shape[0]
    line_count = bilinear_weights.shape[2]
    site_count = gauge_links.shape[-1]
    reach_devs = (part_x - 1 + line_count) // part_x
    highest = lax.Precision.HIGHEST
    weight_rows = bilinear_weights.reshape(channels * channels, line_count * channels)

    def advance(carry, unused):
        arrived = from_behind(carry, "gx", -1)
        return (arrived, arrived)

    unused_last, stacked = lax.scan(advance, (gauge_links, in_field), None, length=reach_devs)
    window_links = jnp.concatenate(
        [gauge_links, stacked[0].reshape((-1, 2, 3, 3, site_count))], axis=0
    )
    later_field = jnp.moveaxis(stacked[1], 0, 1).reshape((channels, -1, 2, 3, 3, site_count))
    window_field = jnp.concatenate([in_field, later_field], axis=1)
    pair_grad = complex_mul(dagger(in_field)[None], cotangent[:, None]).reshape(
        channels * channels, -1
    )

    def forward_step(line, offset):
        shifted = lax.dynamic_slice_in_dim(window_field, offset, part_x, axis=1)
        transported = complex_mul(complex_mul(line[None], shifted), dagger(line)[None])
        next_links = lax.dynamic_slice_in_dim(window_links, offset, part_x, axis=0)
        return (complex_mul(line, next_links), (transported, line))

    offsets = jnp.arange(1, line_count + 1, dtype=jnp.int32)
    unused_line, (all_transported, all_lines) = lax.scan(forward_step, gauge_links, offsets)
    transported_flat = all_transported.reshape(line_count * channels, -1)
    partial_grad = lax.dot_general(
        pair_grad, transported_flat, (((1,), (1,)), ((), ())), precision=highest
    )
    mixed = jnp.dot(weight_rows, transported_flat, precision=highest)
    mixed_matrix = mixed.reshape((channels, channels) + in_field.shape[1:])
    direct = jnp.sum(complex_mul(cotangent[:, None], dagger(mixed_matrix)), axis=0)
    line_grad = jnp.dot(weight_rows.T, pair_grad, precision=highest)
    line_grad = line_grad.reshape((line_count,) + in_field.shape)
    accumulator = jnp.zeros((channels, (reach_devs + 1) * part_x, 2, 3, 3, site_count), jnp.float32)

    def backward_step(carry, inputs):
        offset, grad_piece, line = inputs
        contribution = complex_mul(complex_mul(dagger(line)[None], grad_piece), line[None])
        current = lax.dynamic_slice_in_dim(carry, offset, part_x, axis=1)
        return (
            lax.dynamic_update_slice_in_dim(carry, current + contribution, offset, axis=1),
            None,
        )

    accumulator, unused_out = lax.scan(backward_step, accumulator, (offsets, line_grad, all_lines))
    block_count = reach_devs + 1
    half_span = 1 << reach_devs.bit_length() - 1
    pending = accumulator
    while half_span >= 1:
        moving = pending[:, half_span * part_x : block_count * part_x]
        arrived = from_behind(moving, "gx", half_span)
        kept_count = block_count - half_span
        updated = pending[:, : kept_count * part_x] + arrived
        pending = jnp.concatenate(
            [updated, pending[:, kept_count * part_x : half_span * part_x]], axis=1
        )
        block_count = half_span
        half_span = half_span // 2
    grad_field = direct + pending
    total_x = part_x * lax.axis_size("gx")
    total_sites = site_count * lax.axis_size("yz")
    summed = lax.psum(partial_grad, ("gx", "yz"))
    grad_weights = summed.reshape(channels, channels, line_count, channels) / math.sqrt(
        100.0 * total_x * total_sites
    )
    return (grad_field, grad_weights)


def block_transpose(arrays):
    arrays = list(arrays)
    lane = lax.broadcasted_iota(jnp.int32, arrays[0].shape, 1)
    for bit in (1, 2, 4):
        upper = (lane & (16 * bit)) != 0
        for r in range(8):
            if r & bit:
                continue
            low, high = arrays[r], arrays[r | bit]
            arrays[r] = jnp.where(upper, pltpu.roll(high, 16 * bit, 1), low)
            arrays[r | bit] = jnp.where(upper, high, pltpu.roll(low, LANES - 16 * bit, 1))
    return arrays


def greet(axes):
    barrier = pltpu.get_barrier_semaphore()
    total = 0
    for axis, count in axes:
        me = lax.axis_index(axis)
        for k in range(1, count):
            peer = lax.rem(me + k, count)
            pl.semaphore_signal(barrier, inc=1, device_id={axis: peer}, device_id_type=MESH)
        total += count - 1
    return lambda: pl.semaphore_wait(barrier, total)


def spread(axis, count, source, target, send, recv):
    at = lax.axis_index(axis)
    outgoing, incoming = [], []
    for k in range(1, count):
        for found, slot, there in (
            (outgoing, at, lax.rem(at + k, count)),
            (incoming, lax.rem(at + count - k, count), lax.rem(at + count - k, count)),
        ):
            found.append(
                pltpu.make_async_remote_copy(
                    src_ref=source,
                    dst_ref=target.at[slot],
                    send_sem=send.at[k],
                    recv_sem=recv.at[k],
                    device_id={axis: there},
                    device_id_type=MESH,
                )
            )
    return outgoing, incoming


def other(me, mask):
    for bit in (1, 2, 4):
        if mask & bit:
            me = me + bit - 2 * bit * (me // bit % 2)
    return me


FAR_FIRST = (4, 5, 6, 7, 2, 3, 1)


def exchange(source, target, rows, send_sem, recv_sem):
    me = lax.axis_index("gx")
    outgoing, incoming = [], []
    for k in FAR_FIRST:
        peer = other(me, k)
        for found, slot in ((outgoing, me), (incoming, peer)):
            found.append(
                pltpu.make_async_remote_copy(
                    src_ref=source.at[peer, rows, :],
                    dst_ref=target.at[slot, rows, :],
                    send_sem=send_sem.at[k],
                    recv_sem=recv_sem.at[k],
                    device_id={"gx": peer},
                    device_id_type=MESH,
                )
            )
    return outgoing, incoming


def whole_kernel(
    scale,
    yz_count,
    u_hbm,
    w_hbm,
    g_hbm,
    weight_hbm,
    out_ref,
    gw_out,
    u_ref,
    w_ref,
    g_ref,
    weight_ref,
    packed,
    sending,
    landed,
    sites,
    field,
    cot,
    wrapped,
    v_all,
    v_wrap,
    rows_ref,
    z,
    pair,
    halves,
    mixed,
    line,
    total,
    final,
    back,
    returned,
    partial,
    shares,
    mine,
    across,
    whole,
    first_send,
    first_recv,
    second_send,
    second_recv,
    third_send,
    third_recv,
    back_send,
    back_recv,
    last_send,
    last_recv,
    share_send,
    share_recv,
    across_send,
    across_recv,
    whole_send,
    whole_recv,
    load_sem,
):
    me = lax.axis_index("gx")
    here = lax.axis_index("yz")
    loads = [
        pltpu.make_async_copy(source, target, load_sem.at[k])
        for k, (source, target) in enumerate(
            ((w_hbm, w_ref), (u_hbm, u_ref), (g_hbm, g_ref), (weight_hbm, weight_ref))
        )
    ]
    for load in loads:
        load.start()
    ready = greet((("gx", 8), ("yz", yz_count)))
    lane1 = lax.broadcasted_iota(jnp.int32, (1, LANES), 1)
    lane = lax.broadcasted_iota(jnp.int32, (8, LANES), 1)
    early, even, odd_part = slice(0, 48), slice(48, 64), slice(64, 80)

    with jax.named_scope("pack"):
        packed[:, 32:48, :] = jnp.zeros((8, 16, LANES), jnp.float32)
        packed[:, 72:80, :] = jnp.zeros((8, 8, LANES), jnp.float32)
        loads[0].wait()
        loads[1].wait()
        for x in range(2):
            for ab in range(9):
                row = x * 18 + ab * 2
                packed[:, row : row + 2, :] = w_ref[:, x, ab // 3, ab % 3, :, :]
                for part in range(2):
                    r, t = divmod(row + part, 5)
                    packed[r, 36 + t : 37 + t, :] = u_ref[x, ab // 3, ab % 3, part : part + 1, :]
        loads[2].wait()
        for x in range(2):
            for ab in range(9):
                row = x * 18 + ab * 2
                packed[:, 41 + row : 43 + row, :] = g_ref[:, x, ab // 3, ab % 3, :, :]
        started = []
        arrivals = []
        for rows, send, recv in (
            (early, first_send, first_recv),
            (even, second_send, second_recv),
            (odd_part, third_send, third_recv),
        ):
            for d, value in enumerate(block_transpose([packed[r, rows, :] for r in range(8)])):
                sending[d, rows, :] = value
            if not started:
                ready()
            copies, incoming = exchange(sending, landed, rows, send, recv)
            for copy in copies:
                copy.start()
            started += copies
            arrivals.append(incoming)
        landed[me] = sending[me]

    with jax.named_scope("weights"):
        loads[3].wait()
        rows_ref[...] = jnp.zeros((128, 256), jnp.float32)
        for i in range(8):
            pieces = [weight_ref[pl.ds(i * 64 + l, 8, stride=8), :] for l in range(8)]
            joined = jnp.concatenate(pieces, axis=1)
            rows_ref[i * 8 : i * 8 + 8, 0:64] = joined
            rows_ref[64 + i * 8 : 72 + i * 8, 8:72] = joined
        value = rows_ref[...]
        high = value.astype(jnp.bfloat16).astype(jnp.float32)
        low = value - high
        w3 = (high + pltpu.roll(high, 80, 1) + pltpu.roll(low, 160, 1)).astype(jnp.bfloat16)
        turned = value[:, 0:LANES].T[0:80]
        high = turned.astype(jnp.bfloat16).astype(jnp.float32)
        low = turned - high
        wt3 = []
        for p in range(2):
            part = slice(p * 64, p * 64 + 64)
            joined = jnp.concatenate([high[:, part], high[:, part], low[:, part]], axis=1)
            wt3.append(joined.astype(jnp.bfloat16))

    with jax.named_scope("links_and_field"):
        for arrival in arrivals[0]:
            arrival.wait_recv()
        for c, value in enumerate(block_transpose([landed[r, early, :] for r in range(8)])):
            sites[c * 80 : c * 80 + 48, :] = value

        def link(p, c):
            r, t = divmod(p * 18 + c, 5)
            return sites[r * 80 + 36 + t : r * 80 + 37 + t, :]

        u0 = read_matrix(lambda c: link(0, c))
        u1 = read_matrix(lambda c: link(1, c))
        one = [[[jnp.float32(1.0 if r == 0 and a == b else 0.0) for b in range(3)] for a in range(3)] for r in range(2)]
        prefix = mm(u0, u1)
        for step in (1, 2, 4):
            before = map_matrix(
                lambda m, i: jnp.where(lane1 >= 16 * step, pltpu.roll(m, 16 * step, 1), i), prefix, one
            )
            prefix = mm(before, prefix)
        start = map_matrix(lambda m, i: jnp.where(lane1 >= 16, pltpu.roll(m, 16, 1), i), prefix, one)

        def last_group(m):
            m = jnp.where(lane1 >= 112, m, 0.0)
            for step in (1, 2, 4):
                m = m + pltpu.roll(m, 16 * step, 1)
            return m

        loop = map_matrix(last_group, prefix)
        odd = mm(start, u0)
        for p, m in enumerate((start, odd)):
            for c, value in each(m):
                v_all[c, p] = jnp.broadcast_to(value, (8, LANES))
            for c, value in each(mm(loop, m)):
                v_wrap[c, p] = jnp.broadcast_to(value, (8, LANES))

        def read_sites(base):
            return read_matrix(
                lambda c: jnp.stack([sites[pl.ds(base + p * 18 + c, 8, stride=80), :] for p in range(2)])
            )

        v = read_matrix(lambda c: v_all[c])
        w = read_sites(0)
        for c, value in each(conjugate_by(v, w)):
            field[c] = value
        for c, value in each(conjugate_by(read_matrix(lambda c: v_wrap[c]), w)):
            wrapped[c] = value

    with jax.named_scope("window"):
        z[240:256, :] = jnp.zeros((16, 18 * LANES), jnp.bfloat16)
        for c in range(18):
            pieces = []
            for t in range(9):
                q, k = (t + 1) % 2, (t + 1) // 2
                if k == 0:
                    pieces.append(field[c, q])
                else:
                    joined = jnp.where(lane < 16 * k, wrapped[c, q], field[c, q])
                    pieces.append(pltpu.roll(joined, LANES - 16 * k, 1))
            pieces.append(jnp.zeros((8, LANES), jnp.float32))
            high, low = split(jnp.concatenate(pieces, axis=0))
            columns = slice(c * LANES, (c + 1) * LANES)
            z[0:80, columns] = high
            z[80:160, columns] = low
            z[160:240, columns] = high

    def direct(p):
        @pl.loop(0, 3)
        def _(a):
            sums = [[None, None] for _ in range(3)]
            for i in range(8):
                lines = slice(p * 64 + i * 8, p * 64 + i * 8 + 8)
                for k in range(3):
                    at = (a * 3 + k) * 2
                    gr = jnp.broadcast_to(cot[at, p, i : i + 1, :], (8, LANES))
                    gi = jnp.broadcast_to(cot[at + 1, p, i : i + 1, :], (8, LANES))
                    for b in range(3):
                        at = comp(0, b, k) * LANES
                        mr = mixed[lines, at : at + LANES]
                        at = comp(1, b, k) * LANES
                        mi = mixed[lines, at : at + LANES]
                        re = gr * mr + gi * mi
                        im = gi * mr - gr * mi
                        s = sums[b]
                        sums[b] = [re, im] if s[0] is None else [s[0] + re, s[1] + im]
            for b in range(3):
                total[(a * 3 + b) * 2, p] = sums[b][0]
                total[(a * 3 + b) * 2 + 1, p] = sums[b][1]

    with jax.named_scope("mixed"):
        for chunk in range(9):
            columns = slice(chunk * 256, (chunk + 1) * 256)
            mixed[:, columns] = jnp.dot(w3, z[:, columns], preferred_element_type=jnp.float32)

    for p, rows in ((0, even), (1, odd_part)):
        with jax.named_scope("pairs"):
            for arrival in arrivals[1 + p]:
                arrival.wait_recv()
            for c, value in enumerate(block_transpose([landed[r, rows, :] for r in range(8)])):
                sites[c * 80 + rows.start : c * 80 + rows.stop, :] = value
            v = read_matrix(lambda c: v_all[c, p])
            g = read_matrix(lambda c: sites[pl.ds(41 + p * 18 + c, 8, stride=80), :])
            for c, value in each(conjugate_by(v, g)):
                cot[c, p] = value

            @pl.loop(0, 8)
            def _(i):
                w = read_matrix(lambda c: field[c, p])
                g = read_matrix(lambda c: jnp.broadcast_to(cot[c, p, pl.ds(i, 1), :], (8, LANES)))
                row = pl.multiple_of(i * 8, 8)
                for c, value in each(mm(w, g, left_h=True)):
                    pair[pl.ds(row, 8), c * LANES : (c + 1) * LANES] = value

        with jax.named_scope("products"):
            base = p * 192
            for chunk in range(9):
                columns = slice(chunk * 256, (chunk + 1) * 256)
                high, low = split(pair[:, columns])
                halves[base : base + 64, columns] = high
                halves[base + 64 : base + 128, columns] = low
                halves[base + 128 : base + 192, columns] = high
            if p == 1:
                weights = lax.dot_general(
                    jnp.concatenate([halves[0:128, :], halves[192:320, :]], axis=0),
                    z[0:160, :],
                    (((1,), (1,)), ((), ())),
                    preferred_element_type=jnp.float32,
                )
                half = weights[:, 0:80] + weights[:, 80:160]
                both = half[0:64, 0:64] + half[64:128, 0:64] + half[128:192, 8:72] + half[192:256, 8:72]
                both = jnp.concatenate([both, jnp.zeros((64, 64), jnp.float32)], axis=1)
                for d in range(8):
                    partial[d] = both[d * 8 : d * 8 + 8]
                share_copies, share_arrivals = exchange(
                    partial, shares, slice(0, 8), share_send, share_recv
                )
                for copy in share_copies:
                    copy.start()
                shares[me] = partial[me]
                started += share_copies
            for chunk in range(9):
                columns = slice(chunk * 256, (chunk + 1) * 256)
                value = jnp.dot(wt3[p], halves[base : base + 192, columns], preferred_element_type=jnp.float32)
                line[:, columns] = value if p == 0 else line[:, columns] + value
        if p == 0:
            direct(0)

    for r in range(8):
        final[r * 40 + 32 : r * 40 + 40, :] = jnp.zeros((8, LANES), jnp.float32)
    back_arrivals = []
    for p, rows, send, recv in (
        (0, slice(0, 16), back_send, back_recv),
        (1, slice(16, 40), last_send, last_recv),
    ):
        if p == 1:
            direct(1)
        with jax.named_scope("from_frame"):
            near, far = {}, {}
            for c in range(18):
                inside, outside = total[c, p], None
                for t in range(9):
                    if (t + 1) % 2 != p:
                        continue
                    k = (t + 1) // 2
                    piece = line[t * 8 : t * 8 + 8, c * LANES : (c + 1) * LANES]
                    if k == 0:
                        inside = inside + piece
                        continue
                    piece = pltpu.roll(piece, 16 * k, 1)
                    inside = inside + jnp.where(lane >= 16 * k, piece, 0.0)
                    beyond = jnp.where(lane < 16 * k, piece, 0.0)
                    outside = beyond if outside is None else outside + beyond
                near[c], far[c] = inside, outside
            first = conjugate_by_h(read_matrix(lambda c: v_all[c, p]), read_matrix(lambda c: near[c]))
            second = conjugate_by_h(read_matrix(lambda c: v_wrap[c, p]), read_matrix(lambda c: far[c]))
            for c, value in each(map_matrix(lambda m, n: m + n, first, second)):
                final[pl.ds(p * 18 + c, 8, stride=40), :] = value
            ready_rows = [final[r * 40 + rows.start : r * 40 + rows.stop, :] for r in range(8)]
            for d, value in enumerate(block_transpose(ready_rows)):
                back[d, rows, :] = value
            copies, incoming = exchange(back, returned, rows, send, recv)
            for copy in copies:
                copy.start()
            started += copies
            back_arrivals.append((rows, incoming))
            returned[me, rows, :] = back[me, rows, :]

        if p == 0:
            with jax.named_scope("share_sum"):
                for arrival in share_arrivals:
                    arrival.wait_recv()
                subtotal = shares[0]
                for s in range(1, 8):
                    subtotal = subtotal + shares[s]
                mine[...] = subtotal
                across_copies, across_arrivals = spread(
                    "yz", yz_count, mine, across, across_send, across_recv
                )
                for copy in across_copies:
                    copy.start()
                across[here] = subtotal
                started += across_copies

    with jax.named_scope("weight_sum"):
        for arrival in across_arrivals:
            arrival.wait_recv()
        summed = across[0]
        for s in range(1, yz_count):
            summed = summed + across[s]
        whole[me] = summed * scale
        whole_copies, whole_arrivals = spread("gx", 8, whole.at[me], whole, whole_send, whole_recv)
        for copy in whole_copies:
            copy.start()
        started += whole_copies

    with jax.named_scope("unpack"):
        for p, (rows, incoming) in enumerate(back_arrivals):
            for arrival in incoming:
                arrival.wait_recv()
            for c, value in enumerate(block_transpose([returned[r, rows, :] for r in range(8)])):
                out_ref[c, rows, :] = value
        for arrival in whole_arrivals:
            arrival.wait_recv()
        gw_out[...] = whole[...]
        for copy in started:
            copy.wait_send()


def place_kernel(rows_ref, weights_ref, out_ref, gw_out):
    for x in range(2):
        for ab in range(9):
            row = x * 18 + ab * 2
            out_ref[:, x, ab // 3, ab % 3, :, :] = rows_ref[:, row : row + 2, :]
    for i in range(8):
        value = weights_ref[i]
        for l in range(8):
            gw_out[pl.ds(i * 64 + l, 8, stride=8), :] = value[:, l * 8 : l * 8 + 8]


def resident(scale, yz_count, gauge_links, in_field, cotangent, bilinear_weights):
    f32 = jnp.float32
    vmem = pl.BlockSpec(memory_space=pltpu.VMEM)
    dma = pltpu.SemaphoreType.DMA
    placed = pl.BlockSpec(memory_space=pltpu.HBM)
    rows, weights = pl.pallas_call(
        functools.partial(whole_kernel, scale, yz_count),
        out_shape=(
            jax.ShapeDtypeStruct((8, 40, LANES), f32),
            jax.ShapeDtypeStruct((8, 8, LANES), f32),
        ),
        in_specs=[placed] * 4,
        out_specs=(vmem, vmem),
        scratch_shapes=[
            pltpu.VMEM((2, 3, 3, 2, LANES), f32),
            pltpu.VMEM((8, 2, 3, 3, 2, LANES), f32),
            pltpu.VMEM((8, 2, 3, 3, 2, LANES), f32),
            pltpu.VMEM((512, 8), f32),
            pltpu.VMEM((8, 80, LANES), f32),
            pltpu.VMEM((8, 80, LANES), f32),
            pltpu.VMEM((8, 80, LANES), f32),
            pltpu.VMEM((640, LANES), f32),
            pltpu.VMEM((18, 2, 8, LANES), f32),
            pltpu.VMEM((18, 2, 8, LANES), f32),
            pltpu.VMEM((18, 2, 8, LANES), f32),
            pltpu.VMEM((18, 2, 8, LANES), f32),
            pltpu.VMEM((18, 2, 8, LANES), f32),
            pltpu.VMEM((128, 256), f32),
            pltpu.VMEM((256, 18 * LANES), jnp.bfloat16),
            pltpu.VMEM((64, 18 * LANES), f32),
            pltpu.VMEM((384, 18 * LANES), jnp.bfloat16),
            pltpu.VMEM((128, 18 * LANES), f32),
            pltpu.VMEM((80, 18 * LANES), f32),
            pltpu.VMEM((18, 2, 8, LANES), f32),
            pltpu.VMEM((320, LANES), f32),
            pltpu.VMEM((8, 40, LANES), f32),
            pltpu.VMEM((8, 40, LANES), f32),
            pltpu.VMEM((8, 8, LANES), f32),
            pltpu.VMEM((8, 8, LANES), f32),
            pltpu.VMEM((8, LANES), f32),
            pltpu.VMEM((yz_count, 8, LANES), f32),
            pltpu.VMEM((8, 8, LANES), f32),
        ]
        + [dma((8,))] * 12
        + [dma((yz_count,))] * 2
        + [dma((8,))] * 2
        + [dma((4,))],
        compiler_params=pltpu.CompilerParams(
            collective_id=0, has_side_effects=True, vmem_limit_bytes=VMEM_BYTES
        ),
        name="lattice_backward",
    )(
        pltpu.with_memory_space_constraint(gauge_links.transpose(0, 2, 3, 1, 4), pltpu.HBM),
        pltpu.with_memory_space_constraint(in_field.transpose(0, 1, 3, 4, 2, 5), pltpu.HBM),
        pltpu.with_memory_space_constraint(cotangent.transpose(0, 1, 3, 4, 2, 5), pltpu.HBM),
        pltpu.with_memory_space_constraint(bilinear_weights.reshape(512, 8), pltpu.HBM),
    )
    grad_field, grad_weights = pl.pallas_call(
        place_kernel,
        out_shape=(
            jax.ShapeDtypeStruct((8, 2, 3, 3, 2, LANES), f32),
            jax.ShapeDtypeStruct((512, 8), f32),
        ),
        in_specs=[vmem] * 2,
        out_specs=(vmem, vmem),
        compiler_params=pltpu.CompilerParams(vmem_limit_bytes=VMEM_BYTES),
        name="place_rows",
    )(rows, weights)
    return grad_field.transpose(0, 1, 4, 2, 3, 5), grad_weights.reshape(8, 8, 8, 8)


def mm(left, right, left_h=False, right_h=False):
    def pick(m, h, a, b):
        return (m[0][b][a], m[1][b][a]) if h else (m[0][a][b], m[1][a][b])

    real = [[None] * 3 for _ in range(3)]
    imag = [[None] * 3 for _ in range(3)]
    for a in range(3):
        for b in range(3):
            re = im = None
            for k in range(3):
                lr, li = pick(left, left_h, a, k)
                rr, ri = pick(right, right_h, k, b)
                rr_lr, ii = lr * rr, li * ri
                re = rr_lr if re is None else re + rr_lr
                re = re + ii if left_h != right_h else re - ii
                first, second = lr * ri, li * rr
                if right_h and left_h:
                    term = -(first + second)
                elif right_h:
                    term = second - first
                elif left_h:
                    term = first - second
                else:
                    term = first + second
                im = term if im is None else im + term
            real[a][b], imag[a][b] = re, im
    return [real, imag]


def map_matrix(f, *ms):
    return [[[f(*(m[r][a][b] for m in ms)) for b in range(3)] for a in range(3)] for r in range(2)]


def comp(r, a, b):
    return (a * 3 + b) * 2 + r


def read_matrix(f):
    return [[[f(comp(r, a, b)) for b in range(3)] for a in range(3)] for r in range(2)]


def each(m):
    for r in range(2):
        for a in range(3):
            for b in range(3):
                yield comp(r, a, b), m[r][a][b]


def conjugate_by(v, m):
    return mm(mm(v, m), v, right_h=True)


def conjugate_by_h(v, m):
    return mm(mm(v, m, left_h=True), v)


def split(value):
    high = value.astype(jnp.bfloat16)
    return high, (value - high.astype(jnp.float32)).astype(jnp.bfloat16)


def per_device(gauge_links, in_field, cotangent, bilinear_weights):
    gx = lax.axis_size("gx")
    yz = lax.axis_size("yz")
    fits = (
        gx == 8
        and in_field.shape == (8, 2, 2, 3, 3, LANES)
        and bilinear_weights.shape == (8, 8, 8, 8)
    )
    if not fits:
        return general(gauge_links, in_field, cotangent, bilinear_weights)
    total = gauge_links.shape[0] * gx * gauge_links.shape[-1] * yz
    scale = 1.0 / math.sqrt(100.0 * total)
    return resident(scale, yz, gauge_links, in_field, cotangent, bilinear_weights)


def solution(mesh):
    placed = (
        P("gx", None, None, None, "yz"),
        P(None, "gx", None, None, None, "yz"),
        P(None, "gx", None, None, None, "yz"),
        P(),
    )
    return jax.shard_map(
        per_device,
        mesh=mesh,
        in_specs=placed,
        out_specs=(P(None, "gx", None, None, None, "yz"), P()),
        check_vma=False,
    )
```

```python
import functools
import math

import jax
import jax.numpy as jnp
from jax import lax
from jax.experimental import pallas as pl
from jax.experimental.pallas import tpu as pltpu
from jax.sharding import PartitionSpec as P

MESH = pl.DeviceIdType.MESH
LANES = 128
VMEM_BYTES = 20 * 1024 * 1024


def from_behind(block, axis, distance):
    devices = range(lax.axis_size(axis))
    route = [((i - distance) % len(devices), i) for i in devices]
    return lax.ppermute(block, axis, route)


def matmul_three(left, right):
    return jnp.sum(left[..., :, :, None, :] * right[..., None, :, :, :], axis=-3)


def complex_mul(left, right):
    left_re = left[..., 0, :, :, :]
    left_im = left[..., 1, :, :, :]
    right_re = right[..., 0, :, :, :]
    right_im = right[..., 1, :, :, :]
    real_part = matmul_three(left_re, right_re) - matmul_three(left_im, right_im)
    imag_part = matmul_three(left_re, right_im) + matmul_three(left_im, right_re)
    return jnp.stack([real_part, imag_part], axis=-4)


def dagger(matrix):
    swapped = jnp.swapaxes(matrix, -3, -2)
    return jnp.stack([swapped[..., 0, :, :, :], -swapped[..., 1, :, :, :]], axis=-4)


def general(gauge_links, in_field, cotangent, bilinear_weights):
    part_x = gauge_links.shape[0]
    channels = in_field.shape[0]
    line_count = bilinear_weights.shape[2]
    site_count = gauge_links.shape[-1]
    reach_devs = (part_x - 1 + line_count) // part_x
    highest = lax.Precision.HIGHEST
    weight_rows = bilinear_weights.reshape(channels * channels, line_count * channels)

    def advance(carry, unused):
        arrived = from_behind(carry, "gx", -1)
        return (arrived, arrived)

    unused_last, stacked = lax.scan(advance, (gauge_links, in_field), None, length=reach_devs)
    window_links = jnp.concatenate(
        [gauge_links, stacked[0].reshape((-1, 2, 3, 3, site_count))], axis=0
    )
    later_field = jnp.moveaxis(stacked[1], 0, 1).reshape((channels, -1, 2, 3, 3, site_count))
    window_field = jnp.concatenate([in_field, later_field], axis=1)
    pair_grad = complex_mul(dagger(in_field)[None], cotangent[:, None]).reshape(
        channels * channels, -1
    )

    def forward_step(line, offset):
        shifted = lax.dynamic_slice_in_dim(window_field, offset, part_x, axis=1)
        transported = complex_mul(complex_mul(line[None], shifted), dagger(line)[None])
        next_links = lax.dynamic_slice_in_dim(window_links, offset, part_x, axis=0)
        return (complex_mul(line, next_links), (transported, line))

    offsets = jnp.arange(1, line_count + 1, dtype=jnp.int32)
    unused_line, (all_transported, all_lines) = lax.scan(forward_step, gauge_links, offsets)
    transported_flat = all_transported.reshape(line_count * channels, -1)
    partial_grad = lax.dot_general(
        pair_grad, transported_flat, (((1,), (1,)), ((), ())), precision=highest
    )
    mixed = jnp.dot(weight_rows, transported_flat, precision=highest)
    mixed_matrix = mixed.reshape((channels, channels) + in_field.shape[1:])
    direct = jnp.sum(complex_mul(cotangent[:, None], dagger(mixed_matrix)), axis=0)
    line_grad = jnp.dot(weight_rows.T, pair_grad, precision=highest)
    line_grad = line_grad.reshape((line_count,) + in_field.shape)
    accumulator = jnp.zeros((channels, (reach_devs + 1) * part_x, 2, 3, 3, site_count), jnp.float32)

    def backward_step(carry, inputs):
        offset, grad_piece, line = inputs
        contribution = complex_mul(complex_mul(dagger(line)[None], grad_piece), line[None])
        current = lax.dynamic_slice_in_dim(carry, offset, part_x, axis=1)
        return (
            lax.dynamic_update_slice_in_dim(carry, current + contribution, offset, axis=1),
            None,
        )

    accumulator, unused_out = lax.scan(backward_step, accumulator, (offsets, line_grad, all_lines))
    block_count = reach_devs + 1
    half_span = 1 << reach_devs.bit_length() - 1
    pending = accumulator
    while half_span >= 1:
        moving = pending[:, half_span * part_x : block_count * part_x]
        arrived = from_behind(moving, "gx", half_span)
        kept_count = block_count - half_span
        updated = pending[:, : kept_count * part_x] + arrived
        pending = jnp.concatenate(
            [updated, pending[:, kept_count * part_x : half_span * part_x]], axis=1
        )
        block_count = half_span
        half_span = half_span // 2
    grad_field = direct + pending
    total_x = part_x * lax.axis_size("gx")
    total_sites = site_count * lax.axis_size("yz")
    summed = lax.psum(partial_grad, ("gx", "yz"))
    grad_weights = summed.reshape(channels, channels, line_count, channels) / math.sqrt(
        100.0 * total_x * total_sites
    )
    return (grad_field, grad_weights)


def block_transpose(arrays):
    arrays = list(arrays)
    lane = lax.broadcasted_iota(jnp.int32, arrays[0].shape, 1)
    for bit in (1, 2, 4):
        upper = (lane & (16 * bit)) != 0
        for r in range(8):
            if r & bit:
                continue
            low, high = arrays[r], arrays[r | bit]
            arrays[r] = jnp.where(upper, pltpu.roll(high, 16 * bit, 1), low)
            arrays[r | bit] = jnp.where(upper, high, pltpu.roll(low, LANES - 16 * bit, 1))
    return arrays


def other(me, mask):
    for bit in (1, 2, 4):
        if mask & bit:
            me = me + bit - 2 * bit * (me // bit % 2)
    return me


FAR_FIRST = (4, 5, 6, 7, 2, 3, 1)


def everyone():
    me, here = lax.axis_index("gx"), lax.axis_index("yz")
    return [
        (g * 4 + y, other(me, g), other(here, y))
        for g in FAR_FIRST + (0,)
        for y in (3, 1, 2, 0)
        if g or y
    ]


def greet():
    barrier = pltpu.get_barrier_semaphore()
    for _, gx, yz in everyone():
        pl.semaphore_signal(barrier, inc=1, device_id={"gx": gx, "yz": yz}, device_id_type=MESH)
    return lambda: pl.semaphore_wait(barrier, 31)


def spread(source, target, send, recv):
    mine = lax.axis_index("gx") * 4 + lax.axis_index("yz")
    outgoing, incoming = [], []
    for k, gx, yz in everyone():
        for found, slot in ((outgoing, mine), (incoming, gx * 4 + yz)):
            found.append(
                pltpu.make_async_remote_copy(
                    src_ref=source,
                    dst_ref=target.at[slot],
                    send_sem=send.at[k],
                    recv_sem=recv.at[k],
                    device_id={"gx": gx, "yz": yz},
                    device_id_type=MESH,
                )
            )
    return outgoing, incoming


def exchange(source, target, rows, send_sem, recv_sem):
    me = lax.axis_index("gx")
    outgoing, incoming = [], []
    for k in FAR_FIRST:
        peer = other(me, k)
        for found, slot in ((outgoing, me), (incoming, peer)):
            found.append(
                pltpu.make_async_remote_copy(
                    src_ref=source.at[peer, rows],
                    dst_ref=target.at[slot, rows],
                    send_sem=send_sem.at[k],
                    recv_sem=recv_sem.at[k],
                    device_id={"gx": peer},
                    device_id_type=MESH,
                )
            )
    return outgoing, incoming


def whole_kernel(
    scale,
    u_hbm,
    w_hbm,
    g_hbm,
    weight_hbm,
    out_ref,
    gw_out,
    u_ref,
    w_ref,
    g_ref,
    weight_ref,
    packed,
    sending,
    landed,
    sites,
    field,
    cot,
    wrapped,
    v_all,
    v_wrap,
    rows_ref,
    z,
    pair,
    halves,
    mixed,
    line,
    total,
    final,
    back,
    returned,
    partial,
    shares,
    mine,
    across,
    first_send,
    first_recv,
    second_send,
    second_recv,
    third_send,
    third_recv,
    back_send,
    back_recv,
    last_send,
    last_recv,
    share_send,
    share_recv,
    across_send,
    across_recv,
    load_sem,
):
    me = lax.axis_index("gx")
    here = lax.axis_index("yz")
    loads = [
        pltpu.make_async_copy(source, target, load_sem.at[k])
        for k, (source, target) in enumerate(
            ((w_hbm, w_ref), (u_hbm, u_ref), (g_hbm, g_ref), (weight_hbm, weight_ref))
        )
    ]
    for load in loads:
        load.start()
    ready = greet()
    lane1 = lax.broadcasted_iota(jnp.int32, (1, LANES), 1)
    lane = lax.broadcasted_iota(jnp.int32, (8, LANES), 1)
    early, even, odd_part = slice(0, 48), slice(48, 64), slice(64, 80)

    with jax.named_scope("pack"):
        packed[:, 32:48, :] = jnp.zeros((8, 16, LANES), jnp.float32)
        packed[:, 72:80, :] = jnp.zeros((8, 8, LANES), jnp.float32)
        loads[0].wait()
        loads[1].wait()
        for x in range(2):
            for ab in range(9):
                row = x * 18 + ab * 2
                packed[:, row : row + 2, :] = w_ref[:, x, ab // 3, ab % 3, :, :]
                for part in range(2):
                    r, t = divmod(row + part, 5)
                    packed[r, 36 + t : 37 + t, :] = u_ref[x, ab // 3, ab % 3, part : part + 1, :]
        loads[2].wait()
        for x in range(2):
            for ab in range(9):
                row = x * 18 + ab * 2
                packed[:, 41 + row : 43 + row, :] = g_ref[:, x, ab // 3, ab % 3, :, :]
        started = []
        arrivals = []
        for rows, send, recv in (
            (early, first_send, first_recv),
            (even, second_send, second_recv),
            (odd_part, third_send, third_recv),
        ):
            for d, value in enumerate(block_transpose([packed[r, rows, :] for r in range(8)])):
                sending[d, rows, :] = value
            if not started:
                ready()
            copies, incoming = exchange(sending, landed, rows, send, recv)
            for copy in copies:
                copy.start()
            started += copies
            arrivals.append(incoming)
        landed[me] = sending[me]

    with jax.named_scope("weights"):
        loads[3].wait()
        rows_ref[...] = jnp.zeros((128, 256), jnp.float32)
        for i in range(8):
            pieces = [weight_ref[pl.ds(i * 64 + l, 8, stride=8), :] for l in range(8)]
            joined = jnp.concatenate(pieces, axis=1)
            rows_ref[i * 8 : i * 8 + 8, 0:64] = joined
            rows_ref[64 + i * 8 : 72 + i * 8, 8:72] = joined
        value = rows_ref[...]
        high = value.astype(jnp.bfloat16).astype(jnp.float32)
        low = value - high
        w3 = (high + pltpu.roll(high, 80, 1) + pltpu.roll(low, 160, 1)).astype(jnp.bfloat16)
        turned = value[:, 0:LANES].T[0:80]
        high = turned.astype(jnp.bfloat16).astype(jnp.float32)
        low = turned - high
        wt3 = []
        for p in range(2):
            part = slice(p * 64, p * 64 + 64)
            joined = jnp.concatenate([high[:, part], high[:, part], low[:, part]], axis=1)
            wt3.append(joined.astype(jnp.bfloat16))

    with jax.named_scope("links_and_field"):
        for arrival in arrivals[0]:
            arrival.wait_recv()
        for c, value in enumerate(block_transpose([landed[r, early, :] for r in range(8)])):
            sites[c * 80 : c * 80 + 48, :] = value

        def link(p, c):
            r, t = divmod(p * 18 + c, 5)
            return sites[r * 80 + 36 + t : r * 80 + 37 + t, :]

        u0 = read_matrix(lambda c: link(0, c))
        u1 = read_matrix(lambda c: link(1, c))
        one = [[[jnp.float32(1.0 if r == 0 and a == b else 0.0) for b in range(3)] for a in range(3)] for r in range(2)]
        prefix = mm(u0, u1)
        for step in (1, 2, 4):
            before = map_matrix(
                lambda m, i: jnp.where(lane1 >= 16 * step, pltpu.roll(m, 16 * step, 1), i), prefix, one
            )
            prefix = mm(before, prefix)
        start = map_matrix(lambda m, i: jnp.where(lane1 >= 16, pltpu.roll(m, 16, 1), i), prefix, one)

        def last_group(m):
            m = jnp.where(lane1 >= 112, m, 0.0)
            for step in (1, 2, 4):
                m = m + pltpu.roll(m, 16 * step, 1)
            return m

        loop = map_matrix(last_group, prefix)
        odd = mm(start, u0)
        for p, m in enumerate((start, odd)):
            for c, value in each(m):
                v_all[c, p] = jnp.broadcast_to(value, (8, LANES))
            for c, value in each(mm(loop, m)):
                v_wrap[c, p] = jnp.broadcast_to(value, (8, LANES))

        def read_sites(base):
            return read_matrix(
                lambda c: jnp.stack([sites[pl.ds(base + p * 18 + c, 8, stride=80), :] for p in range(2)])
            )

        v = read_matrix(lambda c: v_all[c])
        w = read_sites(0)
        for c, value in each(conjugate_by(v, w)):
            field[c] = value
        for c, value in each(conjugate_by(read_matrix(lambda c: v_wrap[c]), w)):
            wrapped[c] = value

    with jax.named_scope("window"):
        z[240:256, :] = jnp.zeros((16, 18 * LANES), jnp.bfloat16)
        for c in range(18):
            pieces = []
            for t in range(9):
                q, k = (t + 1) % 2, (t + 1) // 2
                if k == 0:
                    pieces.append(field[c, q])
                else:
                    joined = jnp.where(lane < 16 * k, wrapped[c, q], field[c, q])
                    pieces.append(pltpu.roll(joined, LANES - 16 * k, 1))
            pieces.append(jnp.zeros((8, LANES), jnp.float32))
            high, low = split(jnp.concatenate(pieces, axis=0))
            columns = slice(c * LANES, (c + 1) * LANES)
            z[0:80, columns] = high
            z[80:160, columns] = low
            z[160:240, columns] = high

    def direct(p):
        @pl.loop(0, 3)
        def _(a):
            sums = [[None, None] for _ in range(3)]
            for i in range(8):
                lines = slice(p * 64 + i * 8, p * 64 + i * 8 + 8)
                for k in range(3):
                    at = (a * 3 + k) * 2
                    gr = jnp.broadcast_to(cot[at, p, i : i + 1, :], (8, LANES))
                    gi = jnp.broadcast_to(cot[at + 1, p, i : i + 1, :], (8, LANES))
                    for b in range(3):
                        at = comp(0, b, k) * LANES
                        mr = mixed[lines, at : at + LANES]
                        at = comp(1, b, k) * LANES
                        mi = mixed[lines, at : at + LANES]
                        re = gr * mr + gi * mi
                        im = gi * mr - gr * mi
                        s = sums[b]
                        sums[b] = [re, im] if s[0] is None else [s[0] + re, s[1] + im]
            for b in range(3):
                total[(a * 3 + b) * 2, p] = sums[b][0]
                total[(a * 3 + b) * 2 + 1, p] = sums[b][1]

    with jax.named_scope("mixed"):
        for chunk in range(9):
            columns = slice(chunk * 256, (chunk + 1) * 256)
            mixed[:, columns] = jnp.dot(w3, z[:, columns], preferred_element_type=jnp.float32)

    for p, rows in ((0, even), (1, odd_part)):
        with jax.named_scope("pairs"):
            for arrival in arrivals[1 + p]:
                arrival.wait_recv()
            for c, value in enumerate(block_transpose([landed[r, rows, :] for r in range(8)])):
                sites[c * 80 + rows.start : c * 80 + rows.stop, :] = value
            v = read_matrix(lambda c: v_all[c, p])
            g = read_matrix(lambda c: sites[pl.ds(41 + p * 18 + c, 8, stride=80), :])
            for c, value in each(conjugate_by(v, g)):
                cot[c, p] = value

            @pl.loop(0, 8)
            def _(i):
                w = read_matrix(lambda c: field[c, p])
                g = read_matrix(lambda c: jnp.broadcast_to(cot[c, p, pl.ds(i, 1), :], (8, LANES)))
                row = pl.multiple_of(i * 8, 8)
                for c, value in each(mm(w, g, left_h=True)):
                    pair[pl.ds(row, 8), c * LANES : (c + 1) * LANES] = value

        with jax.named_scope("products"):
            base = p * 192
            for chunk in range(9):
                columns = slice(chunk * 256, (chunk + 1) * 256)
                high, low = split(pair[:, columns])
                halves[base : base + 64, columns] = high
                halves[base + 64 : base + 128, columns] = low
                halves[base + 128 : base + 192, columns] = high
            if p == 1:
                weights = lax.dot_general(
                    jnp.concatenate([halves[0:128, :], halves[192:320, :]], axis=0),
                    z[0:160, :],
                    (((1,), (1,)), ((), ())),
                    preferred_element_type=jnp.float32,
                )
                half = weights[:, 0:80] + weights[:, 80:160]
                both = half[0:64, 0:64] + half[64:128, 0:64] + half[128:192, 8:72] + half[192:256, 8:72]
                for d in range(8):
                    partial[d] = jnp.concatenate(
                        [both[d * 8 : d * 8 + 4], both[d * 8 + 4 : d * 8 + 8]], axis=1
                    )
                share_copies, share_arrivals = exchange(
                    partial, shares, slice(0, 4), share_send, share_recv
                )
                for copy in share_copies:
                    copy.start()
                shares[me] = partial[me]
                started += share_copies
            for chunk in range(9):
                columns = slice(chunk * 256, (chunk + 1) * 256)
                value = jnp.dot(wt3[p], halves[base : base + 192, columns], preferred_element_type=jnp.float32)
                line[:, columns] = value if p == 0 else line[:, columns] + value
        if p == 0:
            direct(0)

    for r in range(8):
        final[r * 40 + 32 : r * 40 + 40, :] = jnp.zeros((8, LANES), jnp.float32)
    back_arrivals = []
    for p, rows, send, recv in (
        (0, slice(0, 16), back_send, back_recv),
        (1, slice(16, 40), last_send, last_recv),
    ):
        if p == 1:
            direct(1)
        with jax.named_scope("from_frame"):
            near, far = {}, {}
            for c in range(18):
                inside, outside = total[c, p], None
                for t in range(9):
                    if (t + 1) % 2 != p:
                        continue
                    k = (t + 1) // 2
                    piece = line[t * 8 : t * 8 + 8, c * LANES : (c + 1) * LANES]
                    if k == 0:
                        inside = inside + piece
                        continue
                    piece = pltpu.roll(piece, 16 * k, 1)
                    inside = inside + jnp.where(lane >= 16 * k, piece, 0.0)
                    beyond = jnp.where(lane < 16 * k, piece, 0.0)
                    outside = beyond if outside is None else outside + beyond
                near[c], far[c] = inside, outside
            first = conjugate_by_h(read_matrix(lambda c: v_all[c, p]), read_matrix(lambda c: near[c]))
            second = conjugate_by_h(read_matrix(lambda c: v_wrap[c, p]), read_matrix(lambda c: far[c]))
            for c, value in each(map_matrix(lambda m, n: m + n, first, second)):
                final[pl.ds(p * 18 + c, 8, stride=40), :] = value
            ready_rows = [final[r * 40 + rows.start : r * 40 + rows.stop, :] for r in range(8)]
            for d, value in enumerate(block_transpose(ready_rows)):
                back[d, rows, :] = value
            copies, incoming = exchange(back, returned, rows, send, recv)
            for copy in copies:
                copy.start()
            started += copies
            back_arrivals.append((rows, incoming))
            returned[me, rows, :] = back[me, rows, :]

        if p == 0:
            with jax.named_scope("share_sum"):
                for arrival in share_arrivals:
                    arrival.wait_recv()
                subtotal = shares[0]
                for s in range(1, 8):
                    subtotal = subtotal + shares[s]
                mine[...] = subtotal
                across_copies, across_arrivals = spread(mine, across, across_send, across_recv)
                for copy in across_copies:
                    copy.start()
                across[me * 4 + here] = subtotal
                started += across_copies

    with jax.named_scope("unpack"):
        for p, (rows, incoming) in enumerate(back_arrivals):
            for arrival in incoming:
                arrival.wait_recv()
            for c, value in enumerate(block_transpose([returned[r, rows, :] for r in range(8)])):
                out_ref[c, rows, :] = value
        for arrival in across_arrivals:
            arrival.wait_recv()
        for d in range(8):
            summed = across[d * 4]
            for y in range(1, 4):
                summed = summed + across[d * 4 + y]
            gw_out[d] = summed * scale
        for copy in started:
            copy.wait_send()


def place_kernel(rows_ref, weights_ref, out_ref, gw_out):
    for x in range(2):
        for ab in range(9):
            row = x * 18 + ab * 2
            out_ref[:, x, ab // 3, ab % 3, :, :] = rows_ref[:, row : row + 2, :]
    for i in range(8):
        value = weights_ref[i]
        value = jnp.concatenate([value[:, 0:64], value[:, 64:LANES]], axis=0)
        for l in range(8):
            gw_out[pl.ds(i * 64 + l, 8, stride=8), :] = value[:, l * 8 : l * 8 + 8]


def resident(scale, gauge_links, in_field, cotangent, bilinear_weights):
    f32 = jnp.float32
    vmem = pl.BlockSpec(memory_space=pltpu.VMEM)
    dma = pltpu.SemaphoreType.DMA
    placed = pl.BlockSpec(memory_space=pltpu.HBM)
    rows, weights = pl.pallas_call(
        functools.partial(whole_kernel, scale),
        out_shape=(
            jax.ShapeDtypeStruct((8, 40, LANES), f32),
            jax.ShapeDtypeStruct((8, 4, LANES), f32),
        ),
        in_specs=[placed] * 4,
        out_specs=(vmem, vmem),
        scratch_shapes=[
            pltpu.VMEM((2, 3, 3, 2, LANES), f32),
            pltpu.VMEM((8, 2, 3, 3, 2, LANES), f32),
            pltpu.VMEM((8, 2, 3, 3, 2, LANES), f32),
            pltpu.VMEM((512, 8), f32),
            pltpu.VMEM((8, 80, LANES), f32),
            pltpu.VMEM((8, 80, LANES), f32),
            pltpu.VMEM((8, 80, LANES), f32),
            pltpu.VMEM((640, LANES), f32),
            pltpu.VMEM((18, 2, 8, LANES), f32),
            pltpu.VMEM((18, 2, 8, LANES), f32),
            pltpu.VMEM((18, 2, 8, LANES), f32),
            pltpu.VMEM((18, 2, 8, LANES), f32),
            pltpu.VMEM((18, 2, 8, LANES), f32),
            pltpu.VMEM((128, 256), f32),
            pltpu.VMEM((256, 18 * LANES), jnp.bfloat16),
            pltpu.VMEM((64, 18 * LANES), f32),
            pltpu.VMEM((384, 18 * LANES), jnp.bfloat16),
            pltpu.VMEM((128, 18 * LANES), f32),
            pltpu.VMEM((80, 18 * LANES), f32),
            pltpu.VMEM((18, 2, 8, LANES), f32),
            pltpu.VMEM((320, LANES), f32),
            pltpu.VMEM((8, 40, LANES), f32),
            pltpu.VMEM((8, 40, LANES), f32),
            pltpu.VMEM((8, 4, LANES), f32),
            pltpu.VMEM((8, 4, LANES), f32),
            pltpu.VMEM((4, LANES), f32),
            pltpu.VMEM((32, 4, LANES), f32),
        ]
        + [dma((8,))] * 12
        + [dma((32,))] * 2
        + [dma((4,))],
        compiler_params=pltpu.CompilerParams(
            collective_id=0, has_side_effects=True, vmem_limit_bytes=VMEM_BYTES
        ),
        name="lattice_backward",
    )(
        pltpu.with_memory_space_constraint(gauge_links.transpose(0, 2, 3, 1, 4), pltpu.HBM),
        pltpu.with_memory_space_constraint(in_field.transpose(0, 1, 3, 4, 2, 5), pltpu.HBM),
        pltpu.with_memory_space_constraint(cotangent.transpose(0, 1, 3, 4, 2, 5), pltpu.HBM),
        pltpu.with_memory_space_constraint(bilinear_weights.reshape(512, 8), pltpu.HBM),
    )
    grad_field, grad_weights = pl.pallas_call(
        place_kernel,
        out_shape=(
            jax.ShapeDtypeStruct((8, 2, 3, 3, 2, LANES), f32),
            jax.ShapeDtypeStruct((512, 8), f32),
        ),
        in_specs=[vmem] * 2,
        out_specs=(vmem, vmem),
        compiler_params=pltpu.CompilerParams(vmem_limit_bytes=VMEM_BYTES),
        name="place_rows",
    )(rows, weights)
    return grad_field.transpose(0, 1, 4, 2, 3, 5), grad_weights.reshape(8, 8, 8, 8)


def mm(left, right, left_h=False, right_h=False):
    def pick(m, h, a, b):
        return (m[0][b][a], m[1][b][a]) if h else (m[0][a][b], m[1][a][b])

    real = [[None] * 3 for _ in range(3)]
    imag = [[None] * 3 for _ in range(3)]
    for a in range(3):
        for b in range(3):
            re = im = None
            for k in range(3):
                lr, li = pick(left, left_h, a, k)
                rr, ri = pick(right, right_h, k, b)
                rr_lr, ii = lr * rr, li * ri
                re = rr_lr if re is None else re + rr_lr
                re = re + ii if left_h != right_h else re - ii
                first, second = lr * ri, li * rr
                if right_h and left_h:
                    term = -(first + second)
                elif right_h:
                    term = second - first
                elif left_h:
                    term = first - second
                else:
                    term = first + second
                im = term if im is None else im + term
            real[a][b], imag[a][b] = re, im
    return [real, imag]


def map_matrix(f, *ms):
    return [[[f(*(m[r][a][b] for m in ms)) for b in range(3)] for a in range(3)] for r in range(2)]


def comp(r, a, b):
    return (a * 3 + b) * 2 + r


def read_matrix(f):
    return [[[f(comp(r, a, b)) for b in range(3)] for a in range(3)] for r in range(2)]


def each(m):
    for r in range(2):
        for a in range(3):
            for b in range(3):
                yield comp(r, a, b), m[r][a][b]


def conjugate_by(v, m):
    return mm(mm(v, m), v, right_h=True)


def conjugate_by_h(v, m):
    return mm(mm(v, m, left_h=True), v)


def split(value):
    high = value.astype(jnp.bfloat16)
    return high, (value - high.astype(jnp.float32)).astype(jnp.bfloat16)


def per_device(gauge_links, in_field, cotangent, bilinear_weights):
    gx = lax.axis_size("gx")
    yz = lax.axis_size("yz")
    fits = (
        gx == 8
        and yz == 4
        and in_field.shape == (8, 2, 2, 3, 3, LANES)
        and bilinear_weights.shape == (8, 8, 8, 8)
    )
    if not fits:
        return general(gauge_links, in_field, cotangent, bilinear_weights)
    total = gauge_links.shape[0] * gx * gauge_links.shape[-1] * yz
    scale = 1.0 / math.sqrt(100.0 * total)
    return resident(scale, gauge_links, in_field, cotangent, bilinear_weights)


def solution(mesh):
    placed = (
        P("gx", None, None, None, "yz"),
        P(None, "gx", None, None, None, "yz"),
        P(None, "gx", None, None, None, "yz"),
        P(),
    )
    return jax.shard_map(
        per_device,
        mesh=mesh,
        in_specs=placed,
        out_specs=(P(None, "gx", None, None, None, "yz"), P()),
        check_vma=False,
    )
```

```python
import functools
import math

import jax
import jax.numpy as jnp
from jax import lax
from jax.experimental import pallas as pl
from jax.experimental.pallas import tpu as pltpu
from jax.sharding import PartitionSpec as P

MESH = pl.DeviceIdType.MESH
LANES = 128
VMEM_BYTES = 20 * 1024 * 1024


def from_behind(block, axis, distance):
    devices = range(lax.axis_size(axis))
    route = [((i - distance) % len(devices), i) for i in devices]
    return lax.ppermute(block, axis, route)


def matmul_three(left, right):
    return jnp.sum(left[..., :, :, None, :] * right[..., None, :, :, :], axis=-3)


def complex_mul(left, right):
    left_re = left[..., 0, :, :, :]
    left_im = left[..., 1, :, :, :]
    right_re = right[..., 0, :, :, :]
    right_im = right[..., 1, :, :, :]
    real_part = matmul_three(left_re, right_re) - matmul_three(left_im, right_im)
    imag_part = matmul_three(left_re, right_im) + matmul_three(left_im, right_re)
    return jnp.stack([real_part, imag_part], axis=-4)


def dagger(matrix):
    swapped = jnp.swapaxes(matrix, -3, -2)
    return jnp.stack([swapped[..., 0, :, :, :], -swapped[..., 1, :, :, :]], axis=-4)


def general(gauge_links, in_field, cotangent, bilinear_weights):
    part_x = gauge_links.shape[0]
    channels = in_field.shape[0]
    line_count = bilinear_weights.shape[2]
    site_count = gauge_links.shape[-1]
    reach_devs = (part_x - 1 + line_count) // part_x
    highest = lax.Precision.HIGHEST
    weight_rows = bilinear_weights.reshape(channels * channels, line_count * channels)

    def advance(carry, unused):
        arrived = from_behind(carry, "gx", -1)
        return (arrived, arrived)

    unused_last, stacked = lax.scan(advance, (gauge_links, in_field), None, length=reach_devs)
    window_links = jnp.concatenate(
        [gauge_links, stacked[0].reshape((-1, 2, 3, 3, site_count))], axis=0
    )
    later_field = jnp.moveaxis(stacked[1], 0, 1).reshape((channels, -1, 2, 3, 3, site_count))
    window_field = jnp.concatenate([in_field, later_field], axis=1)
    pair_grad = complex_mul(dagger(in_field)[None], cotangent[:, None]).reshape(
        channels * channels, -1
    )

    def forward_step(line, offset):
        shifted = lax.dynamic_slice_in_dim(window_field, offset, part_x, axis=1)
        transported = complex_mul(complex_mul(line[None], shifted), dagger(line)[None])
        next_links = lax.dynamic_slice_in_dim(window_links, offset, part_x, axis=0)
        return (complex_mul(line, next_links), (transported, line))

    offsets = jnp.arange(1, line_count + 1, dtype=jnp.int32)
    unused_line, (all_transported, all_lines) = lax.scan(forward_step, gauge_links, offsets)
    transported_flat = all_transported.reshape(line_count * channels, -1)
    partial_grad = lax.dot_general(
        pair_grad, transported_flat, (((1,), (1,)), ((), ())), precision=highest
    )
    mixed = jnp.dot(weight_rows, transported_flat, precision=highest)
    mixed_matrix = mixed.reshape((channels, channels) + in_field.shape[1:])
    direct = jnp.sum(complex_mul(cotangent[:, None], dagger(mixed_matrix)), axis=0)
    line_grad = jnp.dot(weight_rows.T, pair_grad, precision=highest)
    line_grad = line_grad.reshape((line_count,) + in_field.shape)
    accumulator = jnp.zeros((channels, (reach_devs + 1) * part_x, 2, 3, 3, site_count), jnp.float32)

    def backward_step(carry, inputs):
        offset, grad_piece, line = inputs
        contribution = complex_mul(complex_mul(dagger(line)[None], grad_piece), line[None])
        current = lax.dynamic_slice_in_dim(carry, offset, part_x, axis=1)
        return (
            lax.dynamic_update_slice_in_dim(carry, current + contribution, offset, axis=1),
            None,
        )

    accumulator, unused_out = lax.scan(backward_step, accumulator, (offsets, line_grad, all_lines))
    block_count = reach_devs + 1
    half_span = 1 << reach_devs.bit_length() - 1
    pending = accumulator
    while half_span >= 1:
        moving = pending[:, half_span * part_x : block_count * part_x]
        arrived = from_behind(moving, "gx", half_span)
        kept_count = block_count - half_span
        updated = pending[:, : kept_count * part_x] + arrived
        pending = jnp.concatenate(
            [updated, pending[:, kept_count * part_x : half_span * part_x]], axis=1
        )
        block_count = half_span
        half_span = half_span // 2
    grad_field = direct + pending
    total_x = part_x * lax.axis_size("gx")
    total_sites = site_count * lax.axis_size("yz")
    summed = lax.psum(partial_grad, ("gx", "yz"))
    grad_weights = summed.reshape(channels, channels, line_count, channels) / math.sqrt(
        100.0 * total_x * total_sites
    )
    return (grad_field, grad_weights)


def block_transpose(arrays):
    arrays = list(arrays)
    lane = lax.broadcasted_iota(jnp.int32, arrays[0].shape, 1)
    for bit in (1, 2, 4):
        upper = (lane & (16 * bit)) != 0
        for r in range(8):
            if r & bit:
                continue
            low, high = arrays[r], arrays[r | bit]
            arrays[r] = jnp.where(upper, pltpu.roll(high, 16 * bit, 1), low)
            arrays[r | bit] = jnp.where(upper, high, pltpu.roll(low, LANES - 16 * bit, 1))
    return arrays


def greet(axes):
    barrier = pltpu.get_barrier_semaphore()
    total = 0
    for axis, count in axes:
        me = lax.axis_index(axis)
        for k in range(1, count):
            peer = lax.rem(me + k, count)
            pl.semaphore_signal(barrier, inc=1, device_id={axis: peer}, device_id_type=MESH)
        total += count - 1
    return lambda: pl.semaphore_wait(barrier, total)


def spread(axis, count, source, target, send, recv):
    at = lax.axis_index(axis)
    outgoing, incoming = [], []
    for k in range(1, count):
        for found, slot, there in (
            (outgoing, at, lax.rem(at + k, count)),
            (incoming, lax.rem(at + count - k, count), lax.rem(at + count - k, count)),
        ):
            found.append(
                pltpu.make_async_remote_copy(
                    src_ref=source,
                    dst_ref=target.at[slot],
                    send_sem=send.at[k],
                    recv_sem=recv.at[k],
                    device_id={axis: there},
                    device_id_type=MESH,
                )
            )
    return outgoing, incoming


def other(me, mask):
    for bit in (1, 2, 4):
        if mask & bit:
            me = me + bit - 2 * bit * (me // bit % 2)
    return me


FAR_FIRST = (4, 5, 6, 7, 2, 3, 1)


def exchange(source, target, rows, send_sem, recv_sem):
    me = lax.axis_index("gx")
    outgoing, incoming = [], []
    for k in FAR_FIRST:
        peer = other(me, k)
        for found, slot in ((outgoing, me), (incoming, peer)):
            found.append(
                pltpu.make_async_remote_copy(
                    src_ref=source.at[peer, rows, :],
                    dst_ref=target.at[slot, rows, :],
                    send_sem=send_sem.at[k],
                    recv_sem=recv_sem.at[k],
                    device_id={"gx": peer},
                    device_id_type=MESH,
                )
            )
    return outgoing, incoming


def whole_kernel(
    scale,
    yz_count,
    u_hbm,
    w_hbm,
    g_hbm,
    weight_hbm,
    out_ref,
    gw_out,
    u_ref,
    w_ref,
    g_ref,
    weight_ref,
    packed,
    sending,
    landed,
    sites,
    field,
    cot,
    wrapped,
    v_all,
    v_wrap,
    rows_ref,
    z,
    pair,
    halves,
    mixed,
    line,
    total,
    final,
    back,
    returned,
    partial,
    shares,
    mine,
    across,
    whole,
    first_send,
    first_recv,
    second_send,
    second_recv,
    third_send,
    third_recv,
    back_send,
    back_recv,
    last_send,
    last_recv,
    share_send,
    share_recv,
    across_send,
    across_recv,
    whole_send,
    whole_recv,
    load_sem,
):
    me = lax.axis_index("gx")
    here = lax.axis_index("yz")
    loads = [
        pltpu.make_async_copy(source, target, load_sem.at[k])
        for k, (source, target) in enumerate(
            ((w_hbm, w_ref), (u_hbm, u_ref), (g_hbm, g_ref), (weight_hbm, weight_ref))
        )
    ]
    for load in loads:
        load.start()
    ready = greet((("gx", 8), ("yz", yz_count)))
    lane1 = lax.broadcasted_iota(jnp.int32, (1, LANES), 1)
    lane = lax.broadcasted_iota(jnp.int32, (8, LANES), 1)
    early, even, odd_part = slice(0, 40), slice(40, 64), slice(64, 80)

    with jax.named_scope("pack"):
        loads[0].wait()
        loads[1].wait()
        for x in range(2):
            for ab in range(9):
                row = x * 18 + ab * 2
                packed[:, row : row + 2, :] = w_ref[:, x, ab // 3, ab % 3, :, :]
                if ab == 8:
                    continue
                for part in range(2):
                    r, t = divmod(x * 16 + ab * 2 + part, 4)
                    packed[r, 36 + t : 37 + t, :] = u_ref[x, ab // 3, ab % 3, part : part + 1, :]
        started = []
        arrivals = []
        for rows, send, recv in (
            (early, first_send, first_recv),
            (even, second_send, second_recv),
            (odd_part, third_send, third_recv),
        ):
            if rows is even:
                loads[2].wait()
                packed[:, 72:80, :] = jnp.zeros((8, 8, LANES), jnp.float32)
                for x in range(2):
                    for ab in range(9):
                        row = 40 + x * 18 + ab * 2
                        packed[:, row : row + 2, :] = g_ref[:, x, ab // 3, ab % 3, :, :]
            for d, value in enumerate(block_transpose([packed[r, rows, :] for r in range(8)])):
                sending[d, rows, :] = value
            if not started:
                ready()
            copies, incoming = exchange(sending, landed, rows, send, recv)
            for copy in copies:
                copy.start()
            started += copies
            arrivals.append(incoming)
        landed[me] = sending[me]

    with jax.named_scope("weights"):
        loads[3].wait()
        rows_ref[...] = jnp.zeros((128, 256), jnp.float32)
        for i in range(8):
            pieces = [weight_ref[pl.ds(i * 64 + l, 8, stride=8), :] for l in range(8)]
            joined = jnp.concatenate(pieces, axis=1)
            rows_ref[i * 8 : i * 8 + 8, 0:64] = joined
            rows_ref[64 + i * 8 : 72 + i * 8, 8:72] = joined
        value = rows_ref[...]
        high = value.astype(jnp.bfloat16).astype(jnp.float32)
        low = value - high
        w3 = (high + pltpu.roll(high, 80, 1) + pltpu.roll(low, 160, 1)).astype(jnp.bfloat16)
        turned = value[:, 0:LANES].T[0:80]
        high = turned.astype(jnp.bfloat16).astype(jnp.float32)
        low = turned - high
        wt3 = []
        for p in range(2):
            part = slice(p * 64, p * 64 + 64)
            joined = jnp.concatenate([high[:, part], high[:, part], low[:, part]], axis=1)
            wt3.append(joined.astype(jnp.bfloat16))

    with jax.named_scope("links_and_field"):
        for arrival in arrivals[0]:
            arrival.wait_recv()
        for c, value in enumerate(block_transpose([landed[r, early, :] for r in range(8)])):
            sites[c * 80 : c * 80 + 40, :] = value

        def link(p):
            def read(c):
                if c >= 16:
                    return None
                r, t = divmod(p * 16 + c, 4)
                return sites[r * 80 + 36 + t : r * 80 + 37 + t, :]

            m = read_matrix(read)
            re, im = m
            re[2][2] = re[0][0] * re[1][1] - im[0][0] * im[1][1] - re[0][1] * re[1][0] + im[0][1] * im[1][0]
            im[2][2] = re[0][1] * im[1][0] + im[0][1] * re[1][0] - re[0][0] * im[1][1] - im[0][0] * re[1][1]
            return m

        u0 = link(0)
        u1 = link(1)
        one = [[[jnp.float32(1.0 if r == 0 and a == b else 0.0) for b in range(3)] for a in range(3)] for r in range(2)]
        prefix = mm(u0, u1)
        for step in (1, 2, 4):
            before = map_matrix(
                lambda m, i: jnp.where(lane1 >= 16 * step, pltpu.roll(m, 16 * step, 1), i), prefix, one
            )
            prefix = mm(before, prefix)
        start = map_matrix(lambda m, i: jnp.where(lane1 >= 16, pltpu.roll(m, 16, 1), i), prefix, one)

        def last_group(m):
            m = jnp.where(lane1 >= 112, m, 0.0)
            for step in (1, 2, 4):
                m = m + pltpu.roll(m, 16 * step, 1)
            return m

        loop = map_matrix(last_group, prefix)
        odd = mm(start, u0)
        for p, m in enumerate((start, odd)):
            for c, value in each(m):
                v_all[c, p] = jnp.broadcast_to(value, (8, LANES))
            for c, value in each(mm(loop, m)):
                v_wrap[c, p] = jnp.broadcast_to(value, (8, LANES))

        def read_sites(base):
            return read_matrix(
                lambda c: jnp.stack([sites[pl.ds(base + p * 18 + c, 8, stride=80), :] for p in range(2)])
            )

        v = read_matrix(lambda c: v_all[c])
        w = read_sites(0)
        for c, value in each(conjugate_by(v, w)):
            field[c] = value
        for c, value in each(conjugate_by(read_matrix(lambda c: v_wrap[c]), w)):
            wrapped[c] = value

    with jax.named_scope("window"):
        z[240:256, :] = jnp.zeros((16, 18 * LANES), jnp.bfloat16)
        for c in range(18):
            pieces = []
            for t in range(9):
                q, k = (t + 1) % 2, (t + 1) // 2
                if k == 0:
                    pieces.append(field[c, q])
                else:
                    joined = jnp.where(lane < 16 * k, wrapped[c, q], field[c, q])
                    pieces.append(pltpu.roll(joined, LANES - 16 * k, 1))
            pieces.append(jnp.zeros((8, LANES), jnp.float32))
            high, low = split(jnp.concatenate(pieces, axis=0))
            columns = slice(c * LANES, (c + 1) * LANES)
            z[0:80, columns] = high
            z[80:160, columns] = low
            z[160:240, columns] = high

    def direct(p):
        @pl.loop(0, 3)
        def _(a):
            sums = [[None, None] for _ in range(3)]
            for i in range(8):
                lines = slice(p * 64 + i * 8, p * 64 + i * 8 + 8)
                for k in range(3):
                    at = (a * 3 + k) * 2
                    gr = jnp.broadcast_to(cot[at, p, i : i + 1, :], (8, LANES))
                    gi = jnp.broadcast_to(cot[at + 1, p, i : i + 1, :], (8, LANES))
                    for b in range(3):
                        at = comp(0, b, k) * LANES
                        mr = mixed[lines, at : at + LANES]
                        at = comp(1, b, k) * LANES
                        mi = mixed[lines, at : at + LANES]
                        re = gr * mr + gi * mi
                        im = gi * mr - gr * mi
                        s = sums[b]
                        sums[b] = [re, im] if s[0] is None else [s[0] + re, s[1] + im]
            for b in range(3):
                total[(a * 3 + b) * 2, p] = sums[b][0]
                total[(a * 3 + b) * 2 + 1, p] = sums[b][1]

    with jax.named_scope("mixed"):
        for chunk in range(9):
            columns = slice(chunk * 256, (chunk + 1) * 256)
            mixed[:, columns] = jnp.dot(w3, z[:, columns], preferred_element_type=jnp.float32)

    for p, rows in ((0, even), (1, odd_part)):
        with jax.named_scope("pairs"):
            for arrival in arrivals[1 + p]:
                arrival.wait_recv()
            for c, value in enumerate(block_transpose([landed[r, rows, :] for r in range(8)])):
                sites[c * 80 + rows.start : c * 80 + rows.stop, :] = value
            v = read_matrix(lambda c: v_all[c, p])
            g = read_matrix(lambda c: sites[pl.ds(40 + p * 18 + c, 8, stride=80), :])
            for c, value in each(conjugate_by(v, g)):
                cot[c, p] = value

            @pl.loop(0, 8)
            def _(i):
                w = read_matrix(lambda c: field[c, p])
                g = read_matrix(lambda c: jnp.broadcast_to(cot[c, p, pl.ds(i, 1), :], (8, LANES)))
                row = pl.multiple_of(i * 8, 8)
                for c, value in each(mm(w, g, left_h=True)):
                    pair[pl.ds(row, 8), c * LANES : (c + 1) * LANES] = value

        with jax.named_scope("products"):
            base = p * 192
            for chunk in range(9):
                columns = slice(chunk * 256, (chunk + 1) * 256)
                high, low = split(pair[:, columns])
                halves[base : base + 64, columns] = high
                halves[base + 64 : base + 128, columns] = low
                halves[base + 128 : base + 192, columns] = high
            if p == 1:
                weights = lax.dot_general(
                    jnp.concatenate([halves[0:128, :], halves[192:320, :]], axis=0),
                    z[0:160, :],
                    (((1,), (1,)), ((), ())),
                    preferred_element_type=jnp.float32,
                )
                half = weights[:, 0:80] + weights[:, 80:160]
                both = half[0:64, 0:64] + half[64:128, 0:64] + half[128:192, 8:72] + half[192:256, 8:72]
                both = jnp.concatenate([both, jnp.zeros((64, 64), jnp.float32)], axis=1)
                for d in range(8):
                    partial[d] = both[d * 8 : d * 8 + 8]
                share_copies, share_arrivals = exchange(
                    partial, shares, slice(0, 8), share_send, share_recv
                )
                for copy in share_copies:
                    copy.start()
                shares[me] = partial[me]
                started += share_copies
            for chunk in range(9):
                columns = slice(chunk * 256, (chunk + 1) * 256)
                value = jnp.dot(wt3[p], halves[base : base + 192, columns], preferred_element_type=jnp.float32)
                line[:, columns] = value if p == 0 else line[:, columns] + value
        if p == 0:
            direct(0)

    for r in range(8):
        final[r * 40 + 32 : r * 40 + 40, :] = jnp.zeros((8, LANES), jnp.float32)
    back_arrivals = []
    for p, rows, send, recv in (
        (0, slice(0, 16), back_send, back_recv),
        (1, slice(16, 40), last_send, last_recv),
    ):
        if p == 1:
            direct(1)
        with jax.named_scope("from_frame"):
            near, far = {}, {}
            for c in range(18):
                inside, outside = total[c, p], None
                for t in range(9):
                    if (t + 1) % 2 != p:
                        continue
                    k = (t + 1) // 2
                    piece = line[t * 8 : t * 8 + 8, c * LANES : (c + 1) * LANES]
                    if k == 0:
                        inside = inside + piece
                        continue
                    piece = pltpu.roll(piece, 16 * k, 1)
                    inside = inside + jnp.where(lane >= 16 * k, piece, 0.0)
                    beyond = jnp.where(lane < 16 * k, piece, 0.0)
                    outside = beyond if outside is None else outside + beyond
                near[c], far[c] = inside, outside
            first = conjugate_by_h(read_matrix(lambda c: v_all[c, p]), read_matrix(lambda c: near[c]))
            second = conjugate_by_h(read_matrix(lambda c: v_wrap[c, p]), read_matrix(lambda c: far[c]))
            for c, value in each(map_matrix(lambda m, n: m + n, first, second)):
                final[pl.ds(p * 18 + c, 8, stride=40), :] = value
            ready_rows = [final[r * 40 + rows.start : r * 40 + rows.stop, :] for r in range(8)]
            for d, value in enumerate(block_transpose(ready_rows)):
                back[d, rows, :] = value
            copies, incoming = exchange(back, returned, rows, send, recv)
            for copy in copies:
                copy.start()
            started += copies
            back_arrivals.append((rows, incoming))
            returned[me, rows, :] = back[me, rows, :]

        if p == 0:
            with jax.named_scope("share_sum"):
                for arrival in share_arrivals:
                    arrival.wait_recv()
                subtotal = shares[0]
                for s in range(1, 8):
                    subtotal = subtotal + shares[s]
                mine[...] = subtotal
                across_copies, across_arrivals = spread(
                    "yz", yz_count, mine, across, across_send, across_recv
                )
                for copy in across_copies:
                    copy.start()
                across[here] = subtotal
                started += across_copies

    with jax.named_scope("weight_sum"):
        for arrival in across_arrivals:
            arrival.wait_recv()
        summed = across[0]
        for s in range(1, yz_count):
            summed = summed + across[s]
        whole[me] = summed * scale
        whole_copies, whole_arrivals = spread("gx", 8, whole.at[me], whole, whole_send, whole_recv)
        for copy in whole_copies:
            copy.start()
        started += whole_copies

    with jax.named_scope("unpack"):
        for p, (rows, incoming) in enumerate(back_arrivals):
            for arrival in incoming:
                arrival.wait_recv()
            for c, value in enumerate(block_transpose([returned[r, rows, :] for r in range(8)])):
                out_ref[c, rows, :] = value
        for arrival in whole_arrivals:
            arrival.wait_recv()
        gw_out[...] = whole[...]
        for copy in started:
            copy.wait_send()


def place_kernel(rows_ref, weights_ref, out_ref, gw_out):
    for x in range(2):
        for ab in range(9):
            row = x * 18 + ab * 2
            out_ref[:, x, ab // 3, ab % 3, :, :] = rows_ref[:, row : row + 2, :]
    for i in range(8):
        value = weights_ref[i]
        for l in range(8):
            gw_out[pl.ds(i * 64 + l, 8, stride=8), :] = value[:, l * 8 : l * 8 + 8]


def resident(scale, yz_count, gauge_links, in_field, cotangent, bilinear_weights):
    f32 = jnp.float32
    vmem = pl.BlockSpec(memory_space=pltpu.VMEM)
    dma = pltpu.SemaphoreType.DMA
    placed = pl.BlockSpec(memory_space=pltpu.HBM)
    rows, weights = pl.pallas_call(
        functools.partial(whole_kernel, scale, yz_count),
        out_shape=(
            jax.ShapeDtypeStruct((8, 40, LANES), f32),
            jax.ShapeDtypeStruct((8, 8, LANES), f32),
        ),
        in_specs=[placed] * 4,
        out_specs=(vmem, vmem),
        scratch_shapes=[
            pltpu.VMEM((2, 3, 3, 2, LANES), f32),
            pltpu.VMEM((8, 2, 3, 3, 2, LANES), f32),
            pltpu.VMEM((8, 2, 3, 3, 2, LANES), f32),
            pltpu.VMEM((512, 8), f32),
            pltpu.VMEM((8, 80, LANES), f32),
            pltpu.VMEM((8, 80, LANES), f32),
            pltpu.VMEM((8, 80, LANES), f32),
            pltpu.VMEM((640, LANES), f32),
            pltpu.VMEM((18, 2, 8, LANES), f32),
            pltpu.VMEM((18, 2, 8, LANES), f32),
            pltpu.VMEM((18, 2, 8, LANES), f32),
            pltpu.VMEM((18, 2, 8, LANES), f32),
            pltpu.VMEM((18, 2, 8, LANES), f32),
            pltpu.VMEM((128, 256), f32),
            pltpu.VMEM((256, 18 * LANES), jnp.bfloat16),
            pltpu.VMEM((64, 18 * LANES), f32),
            pltpu.VMEM((384, 18 * LANES), jnp.bfloat16),
            pltpu.VMEM((128, 18 * LANES), f32),
            pltpu.VMEM((80, 18 * LANES), f32),
            pltpu.VMEM((18, 2, 8, LANES), f32),
            pltpu.VMEM((320, LANES), f32),
            pltpu.VMEM((8, 40, LANES), f32),
            pltpu.VMEM((8, 40, LANES), f32),
            pltpu.VMEM((8, 8, LANES), f32),
            pltpu.VMEM((8, 8, LANES), f32),
            pltpu.VMEM((8, LANES), f32),
            pltpu.VMEM((yz_count, 8, LANES), f32),
            pltpu.VMEM((8, 8, LANES), f32),
        ]
        + [dma((8,))] * 12
        + [dma((yz_count,))] * 2
        + [dma((8,))] * 2
        + [dma((4,))],
        compiler_params=pltpu.CompilerParams(
            collective_id=0, has_side_effects=True, vmem_limit_bytes=VMEM_BYTES
        ),
        name="lattice_backward",
    )(
        pltpu.with_memory_space_constraint(gauge_links.transpose(0, 2, 3, 1, 4), pltpu.HBM),
        pltpu.with_memory_space_constraint(in_field.transpose(0, 1, 3, 4, 2, 5), pltpu.HBM),
        pltpu.with_memory_space_constraint(cotangent.transpose(0, 1, 3, 4, 2, 5), pltpu.HBM),
        pltpu.with_memory_space_constraint(bilinear_weights.reshape(512, 8), pltpu.HBM),
    )
    grad_field, grad_weights = pl.pallas_call(
        place_kernel,
        out_shape=(
            jax.ShapeDtypeStruct((8, 2, 3, 3, 2, LANES), f32),
            jax.ShapeDtypeStruct((512, 8), f32),
        ),
        in_specs=[vmem] * 2,
        out_specs=(vmem, vmem),
        compiler_params=pltpu.CompilerParams(vmem_limit_bytes=VMEM_BYTES),
        name="place_rows",
    )(rows, weights)
    return grad_field.transpose(0, 1, 4, 2, 3, 5), grad_weights.reshape(8, 8, 8, 8)


def mm(left, right, left_h=False, right_h=False):
    def pick(m, h, a, b):
        return (m[0][b][a], m[1][b][a]) if h else (m[0][a][b], m[1][a][b])

    real = [[None] * 3 for _ in range(3)]
    imag = [[None] * 3 for _ in range(3)]
    for a in range(3):
        for b in range(3):
            re = im = None
            for k in range(3):
                lr, li = pick(left, left_h, a, k)
                rr, ri = pick(right, right_h, k, b)
                rr_lr, ii = lr * rr, li * ri
                re = rr_lr if re is None else re + rr_lr
                re = re + ii if left_h != right_h else re - ii
                first, second = lr * ri, li * rr
                if right_h and left_h:
                    term = -(first + second)
                elif right_h:
                    term = second - first
                elif left_h:
                    term = first - second
                else:
                    term = first + second
                im = term if im is None else im + term
            real[a][b], imag[a][b] = re, im
    return [real, imag]


def map_matrix(f, *ms):
    return [[[f(*(m[r][a][b] for m in ms)) for b in range(3)] for a in range(3)] for r in range(2)]


def comp(r, a, b):
    return (a * 3 + b) * 2 + r


def read_matrix(f):
    return [[[f(comp(r, a, b)) for b in range(3)] for a in range(3)] for r in range(2)]


def each(m):
    for r in range(2):
        for a in range(3):
            for b in range(3):
                yield comp(r, a, b), m[r][a][b]


def conjugate_by(v, m):
    return mm(mm(v, m), v, right_h=True)


def conjugate_by_h(v, m):
    return mm(mm(v, m, left_h=True), v)


def split(value):
    high = value.astype(jnp.bfloat16)
    return high, (value - high.astype(jnp.float32)).astype(jnp.bfloat16)


def per_device(gauge_links, in_field, cotangent, bilinear_weights):
    gx = lax.axis_size("gx")
    yz = lax.axis_size("yz")
    fits = (
        gx == 8
        and in_field.shape == (8, 2, 2, 3, 3, LANES)
        and bilinear_weights.shape == (8, 8, 8, 8)
    )
    if not fits:
        return general(gauge_links, in_field, cotangent, bilinear_weights)
    total = gauge_links.shape[0] * gx * gauge_links.shape[-1] * yz
    scale = 1.0 / math.sqrt(100.0 * total)
    return resident(scale, yz, gauge_links, in_field, cotangent, bilinear_weights)


def solution(mesh):
    placed = (
        P("gx", None, None, None, "yz"),
        P(None, "gx", None, None, None, "yz"),
        P(None, "gx", None, None, None, "yz"),
        P(),
    )
    return jax.shard_map(
        per_device,
        mesh=mesh,
        in_specs=placed,
        out_specs=(P(None, "gx", None, None, None, "yz"), P()),
        check_vma=False,
    )
```

```python
import functools
import math

import jax
import jax.numpy as jnp
from jax import lax
from jax.experimental import pallas as pl
from jax.experimental.pallas import tpu as pltpu
from jax.sharding import PartitionSpec as P

MESH = pl.DeviceIdType.MESH
LANES = 128
VMEM_BYTES = 20 * 1024 * 1024


def from_behind(block, axis, distance):
    devices = range(lax.axis_size(axis))
    route = [((i - distance) % len(devices), i) for i in devices]
    return lax.ppermute(block, axis, route)


def matmul_three(left, right):
    return jnp.sum(left[..., :, :, None, :] * right[..., None, :, :, :], axis=-3)


def complex_mul(left, right):
    left_re = left[..., 0, :, :, :]
    left_im = left[..., 1, :, :, :]
    right_re = right[..., 0, :, :, :]
    right_im = right[..., 1, :, :, :]
    real_part = matmul_three(left_re, right_re) - matmul_three(left_im, right_im)
    imag_part = matmul_three(left_re, right_im) + matmul_three(left_im, right_re)
    return jnp.stack([real_part, imag_part], axis=-4)


def dagger(matrix):
    swapped = jnp.swapaxes(matrix, -3, -2)
    return jnp.stack([swapped[..., 0, :, :, :], -swapped[..., 1, :, :, :]], axis=-4)


def general(gauge_links, in_field, cotangent, bilinear_weights):
    part_x = gauge_links.shape[0]
    channels = in_field.shape[0]
    line_count = bilinear_weights.shape[2]
    site_count = gauge_links.shape[-1]
    reach_devs = (part_x - 1 + line_count) // part_x
    highest = lax.Precision.HIGHEST
    weight_rows = bilinear_weights.reshape(channels * channels, line_count * channels)

    def advance(carry, unused):
        arrived = from_behind(carry, "gx", -1)
        return (arrived, arrived)

    unused_last, stacked = lax.scan(advance, (gauge_links, in_field), None, length=reach_devs)
    window_links = jnp.concatenate(
        [gauge_links, stacked[0].reshape((-1, 2, 3, 3, site_count))], axis=0
    )
    later_field = jnp.moveaxis(stacked[1], 0, 1).reshape((channels, -1, 2, 3, 3, site_count))
    window_field = jnp.concatenate([in_field, later_field], axis=1)
    pair_grad = complex_mul(dagger(in_field)[None], cotangent[:, None]).reshape(
        channels * channels, -1
    )

    def forward_step(line, offset):
        shifted = lax.dynamic_slice_in_dim(window_field, offset, part_x, axis=1)
        transported = complex_mul(complex_mul(line[None], shifted), dagger(line)[None])
        next_links = lax.dynamic_slice_in_dim(window_links, offset, part_x, axis=0)
        return (complex_mul(line, next_links), (transported, line))

    offsets = jnp.arange(1, line_count + 1, dtype=jnp.int32)
    unused_line, (all_transported, all_lines) = lax.scan(forward_step, gauge_links, offsets)
    transported_flat = all_transported.reshape(line_count * channels, -1)
    partial_grad = lax.dot_general(
        pair_grad, transported_flat, (((1,), (1,)), ((), ())), precision=highest
    )
    mixed = jnp.dot(weight_rows, transported_flat, precision=highest)
    mixed_matrix = mixed.reshape((channels, channels) + in_field.shape[1:])
    direct = jnp.sum(complex_mul(cotangent[:, None], dagger(mixed_matrix)), axis=0)
    line_grad = jnp.dot(weight_rows.T, pair_grad, precision=highest)
    line_grad = line_grad.reshape((line_count,) + in_field.shape)
    accumulator = jnp.zeros((channels, (reach_devs + 1) * part_x, 2, 3, 3, site_count), jnp.float32)

    def backward_step(carry, inputs):
        offset, grad_piece, line = inputs
        contribution = complex_mul(complex_mul(dagger(line)[None], grad_piece), line[None])
        current = lax.dynamic_slice_in_dim(carry, offset, part_x, axis=1)
        return (
            lax.dynamic_update_slice_in_dim(carry, current + contribution, offset, axis=1),
            None,
        )

    accumulator, unused_out = lax.scan(backward_step, accumulator, (offsets, line_grad, all_lines))
    block_count = reach_devs + 1
    half_span = 1 << reach_devs.bit_length() - 1
    pending = accumulator
    while half_span >= 1:
        moving = pending[:, half_span * part_x : block_count * part_x]
        arrived = from_behind(moving, "gx", half_span)
        kept_count = block_count - half_span
        updated = pending[:, : kept_count * part_x] + arrived
        pending = jnp.concatenate(
            [updated, pending[:, kept_count * part_x : half_span * part_x]], axis=1
        )
        block_count = half_span
        half_span = half_span // 2
    grad_field = direct + pending
    total_x = part_x * lax.axis_size("gx")
    total_sites = site_count * lax.axis_size("yz")
    summed = lax.psum(partial_grad, ("gx", "yz"))
    grad_weights = summed.reshape(channels, channels, line_count, channels) / math.sqrt(
        100.0 * total_x * total_sites
    )
    return (grad_field, grad_weights)


def block_transpose(arrays):
    arrays = list(arrays)
    lane = lax.broadcasted_iota(jnp.int32, arrays[0].shape, 1)
    for bit in (1, 2, 4):
        upper = (lane & (16 * bit)) != 0
        for r in range(8):
            if r & bit:
                continue
            low, high = arrays[r], arrays[r | bit]
            arrays[r] = jnp.where(upper, pltpu.roll(high, 16 * bit, 1), low)
            arrays[r | bit] = jnp.where(upper, high, pltpu.roll(low, LANES - 16 * bit, 1))
    return arrays


def greet(axes):
    barrier = pltpu.get_barrier_semaphore()
    total = 0
    for axis, count in axes:
        me = lax.axis_index(axis)
        for k in range(1, count):
            peer = lax.rem(me + k, count)
            pl.semaphore_signal(barrier, inc=1, device_id={axis: peer}, device_id_type=MESH)
        total += count - 1
    return lambda: pl.semaphore_wait(barrier, total)


def spread(axis, count, source, target, send, recv):
    at = lax.axis_index(axis)
    outgoing, incoming = [], []
    for k in range(1, count):
        for found, slot, there in (
            (outgoing, at, lax.rem(at + k, count)),
            (incoming, lax.rem(at + count - k, count), lax.rem(at + count - k, count)),
        ):
            found.append(
                pltpu.make_async_remote_copy(
                    src_ref=source,
                    dst_ref=target.at[slot],
                    send_sem=send.at[k],
                    recv_sem=recv.at[k],
                    device_id={axis: there},
                    device_id_type=MESH,
                )
            )
    return outgoing, incoming


def other(me, mask):
    for bit in (1, 2, 4):
        if mask & bit:
            me = me + bit - 2 * bit * (me // bit % 2)
    return me


FAR_FIRST = (4, 5, 6, 7, 2, 3, 1)


def exchange(source, target, rows, send_sem, recv_sem):
    me = lax.axis_index("gx")
    outgoing, incoming = [], []
    for k in FAR_FIRST:
        peer = other(me, k)
        for found, slot in ((outgoing, me), (incoming, peer)):
            found.append(
                pltpu.make_async_remote_copy(
                    src_ref=source.at[peer, rows, :],
                    dst_ref=target.at[slot, rows, :],
                    send_sem=send_sem.at[k],
                    recv_sem=recv_sem.at[k],
                    device_id={"gx": peer},
                    device_id_type=MESH,
                )
            )
    return outgoing, incoming


def whole_kernel(
    scale,
    yz_count,
    u_hbm,
    w_hbm,
    g_hbm,
    weight_hbm,
    out_ref,
    gw_out,
    u_ref,
    w_ref,
    g_ref,
    weight_ref,
    packed,
    sending,
    landed,
    sites,
    field,
    cot,
    wrapped,
    v_all,
    v_wrap,
    rows_ref,
    z,
    pair,
    halves,
    mixed,
    line,
    total,
    final,
    back,
    returned,
    partial,
    shares,
    mine,
    across,
    whole,
    first_send,
    first_recv,
    second_send,
    second_recv,
    third_send,
    third_recv,
    back_send,
    back_recv,
    last_send,
    last_recv,
    share_send,
    share_recv,
    across_send,
    across_recv,
    whole_send,
    whole_recv,
    load_sem,
):
    me = lax.axis_index("gx")
    here = lax.axis_index("yz")
    loads = [
        pltpu.make_async_copy(source, target, load_sem.at[k])
        for k, (source, target) in enumerate(
            ((w_hbm, w_ref), (u_hbm, u_ref), (g_hbm, g_ref), (weight_hbm, weight_ref))
        )
    ]
    for load in loads:
        load.start()
    ready = greet((("gx", 8), ("yz", yz_count)))
    lane1 = lax.broadcasted_iota(jnp.int32, (1, LANES), 1)
    lane = lax.broadcasted_iota(jnp.int32, (8, LANES), 1)
    early, even, odd_part = slice(0, 40), slice(40, 64), slice(64, 76)

    with jax.named_scope("pack"):
        loads[0].wait()
        loads[1].wait()
        for x in range(2):
            for ab in range(9):
                row = x * 18 + ab * 2
                packed[:, row : row + 2, :] = w_ref[:, x, ab // 3, ab % 3, :, :]
                if ab == 8:
                    continue
                for part in range(2):
                    r, t = divmod(x * 16 + ab * 2 + part, 4)
                    packed[r, 36 + t : 37 + t, :] = u_ref[x, ab // 3, ab % 3, part : part + 1, :]
        started = []
        arrivals = []
        for rows, send, recv in (
            (early, first_send, first_recv),
            (even, second_send, second_recv),
            (odd_part, third_send, third_recv),
        ):
            if rows is even:
                loads[2].wait()
                for x in range(2):
                    for ab in range(9):
                        row = 40 + x * 18 + ab * 2
                        packed[:, row : row + 2, :] = g_ref[:, x, ab // 3, ab % 3, :, :]
            for d, value in enumerate(block_transpose([packed[r, rows, :] for r in range(8)])):
                sending[d, rows, :] = value
            if not started:
                ready()
            copies, incoming = exchange(sending, landed, rows, send, recv)
            for copy in copies:
                copy.start()
            started += copies
            arrivals.append(incoming)
        landed[me] = sending[me]

    with jax.named_scope("weights"):
        loads[3].wait()
        rows_ref[...] = jnp.zeros((128, 256), jnp.float32)
        for i in range(8):
            pieces = [weight_ref[pl.ds(i * 64 + l, 8, stride=8), :] for l in range(8)]
            joined = jnp.concatenate(pieces, axis=1)
            rows_ref[i * 8 : i * 8 + 8, 0:64] = joined
            rows_ref[64 + i * 8 : 72 + i * 8, 8:72] = joined
        value = rows_ref[...]
        high = value.astype(jnp.bfloat16).astype(jnp.float32)
        low = value - high
        w3 = (high + pltpu.roll(high, 80, 1) + pltpu.roll(low, 160, 1)).astype(jnp.bfloat16)
        turned = value[:, 0:LANES].T[0:80]
        high = turned.astype(jnp.bfloat16).astype(jnp.float32)
        low = turned - high
        wt3 = []
        for p in range(2):
            part = slice(p * 64, p * 64 + 64)
            joined = jnp.concatenate([high[:, part], high[:, part], low[:, part]], axis=1)
            wt3.append(joined.astype(jnp.bfloat16))

    with jax.named_scope("links_and_field"):
        for arrival in arrivals[0]:
            arrival.wait_recv()
        for c, value in enumerate(block_transpose([landed[r, early, :] for r in range(8)])):
            sites[c * 80 : c * 80 + 40, :] = value

        def link(p):
            def read(c):
                if c >= 16:
                    return None
                r, t = divmod(p * 16 + c, 4)
                return sites[r * 80 + 36 + t : r * 80 + 37 + t, :]

            m = read_matrix(read)
            re, im = m
            re[2][2] = re[0][0] * re[1][1] - im[0][0] * im[1][1] - re[0][1] * re[1][0] + im[0][1] * im[1][0]
            im[2][2] = re[0][1] * im[1][0] + im[0][1] * re[1][0] - re[0][0] * im[1][1] - im[0][0] * re[1][1]
            return m

        u0 = link(0)
        u1 = link(1)
        one = [[[jnp.float32(1.0 if r == 0 and a == b else 0.0) for b in range(3)] for a in range(3)] for r in range(2)]
        prefix = mm(u0, u1)
        for step in (1, 2, 4):
            before = map_matrix(
                lambda m, i: jnp.where(lane1 >= 16 * step, pltpu.roll(m, 16 * step, 1), i), prefix, one
            )
            prefix = mm(before, prefix)
        start = map_matrix(lambda m, i: jnp.where(lane1 >= 16, pltpu.roll(m, 16, 1), i), prefix, one)

        def last_group(m):
            m = jnp.where(lane1 >= 112, m, 0.0)
            for step in (1, 2, 4):
                m = m + pltpu.roll(m, 16 * step, 1)
            return m

        loop = map_matrix(last_group, prefix)
        odd = mm(start, u0)
        for p, m in enumerate((start, odd)):
            for c, value in each(m):
                v_all[c, p] = jnp.broadcast_to(value, (8, LANES))
            for c, value in each(mm(loop, m)):
                v_wrap[c, p] = jnp.broadcast_to(value, (8, LANES))

        def read_sites(base):
            return read_matrix(
                lambda c: jnp.stack([sites[pl.ds(base + p * 18 + c, 8, stride=80), :] for p in range(2)])
            )

        v = read_matrix(lambda c: v_all[c])
        w = read_sites(0)
        for c, value in each(conjugate_by(v, w)):
            field[c] = value
        for c, value in each(conjugate_by(read_matrix(lambda c: v_wrap[c]), w)):
            wrapped[c] = value

    with jax.named_scope("window"):
        z[240:256, :] = jnp.zeros((16, 18 * LANES), jnp.bfloat16)
        for c in range(18):
            pieces = []
            for t in range(9):
                q, k = (t + 1) % 2, (t + 1) // 2
                if k == 0:
                    pieces.append(field[c, q])
                else:
                    joined = jnp.where(lane < 16 * k, wrapped[c, q], field[c, q])
                    pieces.append(pltpu.roll(joined, LANES - 16 * k, 1))
            pieces.append(jnp.zeros((8, LANES), jnp.float32))
            high, low = split(jnp.concatenate(pieces, axis=0))
            columns = slice(c * LANES, (c + 1) * LANES)
            z[0:80, columns] = high
            z[80:160, columns] = low
            z[160:240, columns] = high

    def direct(p):
        @pl.loop(0, 3)
        def _(a):
            sums = [[None, None] for _ in range(3)]
            for i in range(8):
                lines = slice(p * 64 + i * 8, p * 64 + i * 8 + 8)
                for k in range(3):
                    at = (a * 3 + k) * 2
                    gr = jnp.broadcast_to(cot[at, p, i : i + 1, :], (8, LANES))
                    gi = jnp.broadcast_to(cot[at + 1, p, i : i + 1, :], (8, LANES))
                    for b in range(3):
                        at = comp(0, b, k) * LANES
                        mr = mixed[lines, at : at + LANES]
                        at = comp(1, b, k) * LANES
                        mi = mixed[lines, at : at + LANES]
                        re = gr * mr + gi * mi
                        im = gi * mr - gr * mi
                        s = sums[b]
                        sums[b] = [re, im] if s[0] is None else [s[0] + re, s[1] + im]
            for b in range(3):
                total[(a * 3 + b) * 2, p] = sums[b][0]
                total[(a * 3 + b) * 2 + 1, p] = sums[b][1]

    with jax.named_scope("mixed"):
        for chunk in range(9):
            columns = slice(chunk * 256, (chunk + 1) * 256)
            mixed[:, columns] = jnp.dot(w3, z[:, columns], preferred_element_type=jnp.float32)

    for p, rows in ((0, even), (1, odd_part)):
        with jax.named_scope("pairs"):
            for arrival in arrivals[1 + p]:
                arrival.wait_recv()
            for c, value in enumerate(block_transpose([landed[r, rows, :] for r in range(8)])):
                sites[c * 80 + rows.start : c * 80 + rows.stop, :] = value
            v = read_matrix(lambda c: v_all[c, p])
            g = read_matrix(lambda c: sites[pl.ds(40 + p * 18 + c, 8, stride=80), :])
            for c, value in each(conjugate_by(v, g)):
                cot[c, p] = value

            @pl.loop(0, 8)
            def _(i):
                w = read_matrix(lambda c: field[c, p])
                g = read_matrix(lambda c: jnp.broadcast_to(cot[c, p, pl.ds(i, 1), :], (8, LANES)))
                row = pl.multiple_of(i * 8, 8)
                for c, value in each(mm(w, g, left_h=True)):
                    pair[pl.ds(row, 8), c * LANES : (c + 1) * LANES] = value

        with jax.named_scope("products"):
            base = p * 192
            for chunk in range(9):
                columns = slice(chunk * 256, (chunk + 1) * 256)
                high, low = split(pair[:, columns])
                halves[base : base + 64, columns] = high
                halves[base + 64 : base + 128, columns] = low
                halves[base + 128 : base + 192, columns] = high
            if p == 1:
                weights = lax.dot_general(
                    jnp.concatenate([halves[0:128, :], halves[192:320, :]], axis=0),
                    z[0:160, :],
                    (((1,), (1,)), ((), ())),
                    preferred_element_type=jnp.float32,
                )
                half = weights[:, 0:80] + weights[:, 80:160]
                both = half[0:64, 0:64] + half[64:128, 0:64] + half[128:192, 8:72] + half[192:256, 8:72]
                both = jnp.concatenate([both, jnp.zeros((64, 64), jnp.float32)], axis=1)
                for d in range(8):
                    partial[d] = both[d * 8 : d * 8 + 8]
                share_copies, share_arrivals = exchange(
                    partial, shares, slice(0, 8), share_send, share_recv
                )
                for copy in share_copies:
                    copy.start()
                shares[me] = partial[me]
                started += share_copies
            for chunk in range(9):
                columns = slice(chunk * 256, (chunk + 1) * 256)
                value = jnp.dot(wt3[p], halves[base : base + 192, columns], preferred_element_type=jnp.float32)
                line[:, columns] = value if p == 0 else line[:, columns] + value
        if p == 0:
            direct(0)

    back_arrivals = []
    for p, rows, send, recv in (
        (0, slice(0, 16), back_send, back_recv),
        (1, slice(16, 36), last_send, last_recv),
    ):
        if p == 1:
            direct(1)
        with jax.named_scope("from_frame"):
            near, far = {}, {}
            for c in range(18):
                inside, outside = total[c, p], None
                for t in range(9):
                    if (t + 1) % 2 != p:
                        continue
                    k = (t + 1) // 2
                    piece = line[t * 8 : t * 8 + 8, c * LANES : (c + 1) * LANES]
                    if k == 0:
                        inside = inside + piece
                        continue
                    piece = pltpu.roll(piece, 16 * k, 1)
                    inside = inside + jnp.where(lane >= 16 * k, piece, 0.0)
                    beyond = jnp.where(lane < 16 * k, piece, 0.0)
                    outside = beyond if outside is None else outside + beyond
                near[c], far[c] = inside, outside
            first = conjugate_by_h(read_matrix(lambda c: v_all[c, p]), read_matrix(lambda c: near[c]))
            second = conjugate_by_h(read_matrix(lambda c: v_wrap[c, p]), read_matrix(lambda c: far[c]))
            for c, value in each(map_matrix(lambda m, n: m + n, first, second)):
                final[pl.ds(p * 18 + c, 8, stride=40), :] = value
            ready_rows = [final[r * 40 + rows.start : r * 40 + rows.stop, :] for r in range(8)]
            for d, value in enumerate(block_transpose(ready_rows)):
                back[d, rows, :] = value
            copies, incoming = exchange(back, returned, rows, send, recv)
            for copy in copies:
                copy.start()
            started += copies
            back_arrivals.append((rows, incoming))
            returned[me, rows, :] = back[me, rows, :]

        if p == 0:
            with jax.named_scope("share_sum"):
                for arrival in share_arrivals:
                    arrival.wait_recv()
                subtotal = shares[0]
                for s in range(1, 8):
                    subtotal = subtotal + shares[s]
                mine[...] = subtotal
                across_copies, across_arrivals = spread(
                    "yz", yz_count, mine, across, across_send, across_recv
                )
                for copy in across_copies:
                    copy.start()
                across[here] = subtotal
                started += across_copies

    with jax.named_scope("weight_sum"):
        for arrival in across_arrivals:
            arrival.wait_recv()
        summed = across[0]
        for s in range(1, yz_count):
            summed = summed + across[s]
        whole[me] = summed * scale
        whole_copies, whole_arrivals = spread("gx", 8, whole.at[me], whole, whole_send, whole_recv)
        for copy in whole_copies:
            copy.start()
        started += whole_copies

    with jax.named_scope("unpack"):
        for p, (rows, incoming) in enumerate(back_arrivals):
            for arrival in incoming:
                arrival.wait_recv()
            for c, value in enumerate(block_transpose([returned[r, rows, :] for r in range(8)])):
                out_ref[c, rows, :] = value
        for arrival in whole_arrivals:
            arrival.wait_recv()
        gw_out[...] = whole[...]
        for copy in started:
            copy.wait_send()


def place_kernel(rows_ref, weights_ref, out_ref, gw_out):
    for x in range(2):
        for ab in range(9):
            row = x * 18 + ab * 2
            out_ref[:, x, ab // 3, ab % 3, :, :] = rows_ref[:, row : row + 2, :]
    for i in range(8):
        value = weights_ref[i]
        for l in range(8):
            gw_out[pl.ds(i * 64 + l, 8, stride=8), :] = value[:, l * 8 : l * 8 + 8]


def resident(scale, yz_count, gauge_links, in_field, cotangent, bilinear_weights):
    f32 = jnp.float32
    vmem = pl.BlockSpec(memory_space=pltpu.VMEM)
    dma = pltpu.SemaphoreType.DMA
    placed = pl.BlockSpec(memory_space=pltpu.HBM)
    rows, weights = pl.pallas_call(
        functools.partial(whole_kernel, scale, yz_count),
        out_shape=(
            jax.ShapeDtypeStruct((8, 36, LANES), f32),
            jax.ShapeDtypeStruct((8, 8, LANES), f32),
        ),
        in_specs=[placed] * 4,
        out_specs=(vmem, vmem),
        scratch_shapes=[
            pltpu.VMEM((2, 3, 3, 2, LANES), f32),
            pltpu.VMEM((8, 2, 3, 3, 2, LANES), f32),
            pltpu.VMEM((8, 2, 3, 3, 2, LANES), f32),
            pltpu.VMEM((512, 8), f32),
            pltpu.VMEM((8, 80, LANES), f32),
            pltpu.VMEM((8, 76, LANES), f32),
            pltpu.VMEM((8, 76, LANES), f32),
            pltpu.VMEM((640, LANES), f32),
            pltpu.VMEM((18, 2, 8, LANES), f32),
            pltpu.VMEM((18, 2, 8, LANES), f32),
            pltpu.VMEM((18, 2, 8, LANES), f32),
            pltpu.VMEM((18, 2, 8, LANES), f32),
            pltpu.VMEM((18, 2, 8, LANES), f32),
            pltpu.VMEM((128, 256), f32),
            pltpu.VMEM((256, 18 * LANES), jnp.bfloat16),
            pltpu.VMEM((64, 18 * LANES), f32),
            pltpu.VMEM((384, 18 * LANES), jnp.bfloat16),
            pltpu.VMEM((128, 18 * LANES), f32),
            pltpu.VMEM((80, 18 * LANES), f32),
            pltpu.VMEM((18, 2, 8, LANES), f32),
            pltpu.VMEM((320, LANES), f32),
            pltpu.VMEM((8, 36, LANES), f32),
            pltpu.VMEM((8, 36, LANES), f32),
            pltpu.VMEM((8, 8, LANES), f32),
            pltpu.VMEM((8, 8, LANES), f32),
            pltpu.VMEM((8, LANES), f32),
            pltpu.VMEM((yz_count, 8, LANES), f32),
            pltpu.VMEM((8, 8, LANES), f32),
        ]
        + [dma((8,))] * 12
        + [dma((yz_count,))] * 2
        + [dma((8,))] * 2
        + [dma((4,))],
        compiler_params=pltpu.CompilerParams(
            collective_id=0, has_side_effects=True, vmem_limit_bytes=VMEM_BYTES
        ),
        name="lattice_backward",
    )(
        pltpu.with_memory_space_constraint(gauge_links.transpose(0, 2, 3, 1, 4), pltpu.HBM),
        pltpu.with_memory_space_constraint(in_field.transpose(0, 1, 3, 4, 2, 5), pltpu.HBM),
        pltpu.with_memory_space_constraint(cotangent.transpose(0, 1, 3, 4, 2, 5), pltpu.HBM),
        pltpu.with_memory_space_constraint(bilinear_weights.reshape(512, 8), pltpu.HBM),
    )
    grad_field, grad_weights = pl.pallas_call(
        place_kernel,
        out_shape=(
            jax.ShapeDtypeStruct((8, 2, 3, 3, 2, LANES), f32),
            jax.ShapeDtypeStruct((512, 8), f32),
        ),
        in_specs=[vmem] * 2,
        out_specs=(vmem, vmem),
        compiler_params=pltpu.CompilerParams(vmem_limit_bytes=VMEM_BYTES),
        name="place_rows",
    )(rows, weights)
    return grad_field.transpose(0, 1, 4, 2, 3, 5), grad_weights.reshape(8, 8, 8, 8)


def mm(left, right, left_h=False, right_h=False):
    def pick(m, h, a, b):
        return (m[0][b][a], m[1][b][a]) if h else (m[0][a][b], m[1][a][b])

    real = [[None] * 3 for _ in range(3)]
    imag = [[None] * 3 for _ in range(3)]
    for a in range(3):
        for b in range(3):
            re = im = None
            for k in range(3):
                lr, li = pick(left, left_h, a, k)
                rr, ri = pick(right, right_h, k, b)
                rr_lr, ii = lr * rr, li * ri
                re = rr_lr if re is None else re + rr_lr
                re = re + ii if left_h != right_h else re - ii
                first, second = lr * ri, li * rr
                if right_h and left_h:
                    term = -(first + second)
                elif right_h:
                    term = second - first
                elif left_h:
                    term = first - second
                else:
                    term = first + second
                im = term if im is None else im + term
            real[a][b], imag[a][b] = re, im
    return [real, imag]


def map_matrix(f, *ms):
    return [[[f(*(m[r][a][b] for m in ms)) for b in range(3)] for a in range(3)] for r in range(2)]


def comp(r, a, b):
    return (a * 3 + b) * 2 + r


def read_matrix(f):
    return [[[f(comp(r, a, b)) for b in range(3)] for a in range(3)] for r in range(2)]


def each(m):
    for r in range(2):
        for a in range(3):
            for b in range(3):
                yield comp(r, a, b), m[r][a][b]


def conjugate_by(v, m):
    return mm(mm(v, m), v, right_h=True)


def conjugate_by_h(v, m):
    return mm(mm(v, m, left_h=True), v)


def split(value):
    high = value.astype(jnp.bfloat16)
    return high, (value - high.astype(jnp.float32)).astype(jnp.bfloat16)


def per_device(gauge_links, in_field, cotangent, bilinear_weights):
    gx = lax.axis_size("gx")
    yz = lax.axis_size("yz")
    fits = (
        gx == 8
        and in_field.shape == (8, 2, 2, 3, 3, LANES)
        and bilinear_weights.shape == (8, 8, 8, 8)
    )
    if not fits:
        return general(gauge_links, in_field, cotangent, bilinear_weights)
    total = gauge_links.shape[0] * gx * gauge_links.shape[-1] * yz
    scale = 1.0 / math.sqrt(100.0 * total)
    return resident(scale, yz, gauge_links, in_field, cotangent, bilinear_weights)


def solution(mesh):
    placed = (
        P("gx", None, None, None, "yz"),
        P(None, "gx", None, None, None, "yz"),
        P(None, "gx", None, None, None, "yz"),
        P(),
    )
    return jax.shard_map(
        per_device,
        mesh=mesh,
        in_specs=placed,
        out_specs=(P(None, "gx", None, None, None, "yz"), P()),
        check_vma=False,
    )
```
